128 devices in a mesh: dp: 8 (over y_lo, z), expert: 16 (over x, y_hi, core).
Axes of the slice: x: 4, y: 4 (y_hi: 2, y_lo: 2; y = y_hi * 2 + y_lo), z: 4, core: 2. Of those that a mesh axis runs over, the one named last changes fastest.
Arguments:
- tokens: bfloat16 [16384, 4096], P(('dp', 'expert')), may hold values from -6 to 6
- up_grad: bfloat16 [16384, 8, 1536], P(('dp', 'expert')), may hold values from -6 to 6
- gate_weights: float32 [16384, 8], P(('dp', 'expert')), may hold values from 0.02 to 0.3
- expert_ids: int32 [16384, 8], P(('dp', 'expert')), may hold values from 0 to 127, all different within a row; in each aligned block of 128 rows (0 to 127, 128 to 255, ...) at most 10 rows name the same one
- new_home: int32 [128], replicated, may hold values from 0 to 127, as said below
- adapter_a: float32 [128, 32, 4096], P('expert'), may hold values from -0.09375 to 0.09375
- adapter_b: float32 [128, 32, 1536], P('expert'), may hold values from -0.15625 to 0.15625
- first_moment: float32 [128, 180224], P('expert', 'dp'), may hold values from -4 to 4
- second_moment: float32 [128, 180224], P('expert', 'dp'), may hold values from 0.01 to 1
Outputs:
- new_a: float32 [128, 32, 4096], P('expert')
- new_b: float32 [128, 32, 1536], P('expert')
- new_first: float32 [128, 180224], P('expert', 'dp')
- new_second: float32 [128, 180224], P('expert', 'dp')
The draws below stay inside these ranges and needn't reach their ends.
Inputs may be any that keep to these rules, and one draw needn't show every extreme that they name: `expert_ids`: each row names 8 different experts. Among the 128 rows of one device no expert is named by more than 10 rows, a bound that some block reaches. `new_home`: a permutation. Slot s lies on device s // 8 of the expert axis; expert e starts in slot e and ends in slot new_home[e]. Between two different devices at most one expert moves, and some pair has exactly one; every device sends as many experts to other devices as it receives, and all devices the same number.
All inputs are finite; a program needn't handle non-finite values.
Results may differ from the reference program's by a relative error of at most 0.0048.
Values may be sent and summed in bfloat16 or wider, within the bound.
A program may use at most 192 MiB of HBM per device.

```python
import math
import jax
import jax.numpy as jnp
import numpy as np
from jax import lax

D = 4096
FF = 1536
TOP = 8
R = 32
EXP_DEV = 8
TOK_DEV = 128
EXPERTS = 128
TOKENS = 16384
CAP = 10
PARAMS = 180224
N_DP = 8
N_EXPERT = 16


def draw_new_home(key, part):
    key = jax.random.fold_in(key, 7)
    first_key, second_key, third_key = jax.random.split(key, 3)
    devices = EXPERTS // EXP_DEV
    relabel = jax.random.permutation(first_key, devices).astype(jnp.int32)
    inverse = jnp.zeros((devices,), jnp.int32).at[relabel].set(jnp.arange(devices, dtype=jnp.int32))
    shifts = jax.random.permutation(second_key, devices)[:EXP_DEV].astype(jnp.int32)
    places = jax.random.permutation(third_key, EXP_DEV).astype(jnp.int32)
    device_ids = jnp.arange(devices, dtype=jnp.int32)[:, None]
    target = relabel[(inverse[device_ids] + shifts[None, :]) % devices]
    return (target * EXP_DEV + places[None, :]).reshape(EXPERTS).astype(jnp.int32)


def shard_levels(key, extent, shards, least, largest):
    def one(dim, blocks):
        heights = jax.random.uniform(jax.random.fold_in(jax.random.fold_in(key, 6), dim), (blocks,), jnp.float32, least / len(shards), largest / len(shards))
        return jnp.repeat(jnp.exp(heights), extent[dim] // blocks).reshape((-1,) + (1,) * (len(extent) - dim - 1))

    gain = one(*shards[0])
    for cut in shards[1:]:
        gain = gain * one(*cut)
    return gain


def deal_out(own_key, own, number, rows, count, top, bound, slope):
    ranking = jax.random.permutation(own_key, count)
    heavy_load, ordinary = portions_of(count, rows * top, bound, slope, True), portions_of(count, rows * top, bound, slope, False)
    places = jnp.arange(count)

    def named(sizes, offset_by):
        used = int((sizes > 0).sum())
        fixed = max(1, used // 4)
        moved = fixed + (places - fixed + offset_by * (used - fixed)) % max(1, count - fixed)
        return jnp.zeros((count,), jnp.int32).at[ranking[jnp.where(places < fixed, places, moved)]].set(jnp.asarray(sizes, jnp.int32))

    sizes = jnp.where(number % 4 == 0, named(heavy_load, number // 4), named(ordinary, number - number // 4 - 1))
    mixed = jax.random.permutation(jax.random.fold_in(own, 3), count)
    source_of, taker = mixed[0:count // 2 * 2:2], mixed[1:count // 2 * 2:2]
    slack = jnp.minimum(sizes[source_of] - 1, bound - sizes[taker]) // 2
    slack = jnp.where((source_of == ranking[0]) | (taker == ranking[0]) | (sizes[taker] == 0), 0, jnp.maximum(slack, 0))
    moved = jax.random.randint(jax.random.fold_in(own, 4), (count // 2,), 0, 1 << 20) % (slack + 1)
    sizes = sizes.at[source_of].add(-moved).at[taker].add(moved)
    members = jnp.searchsorted(jnp.cumsum(sizes), jnp.arange(rows * top), side="right").astype(jnp.int32)
    grid = members.reshape(top, rows).T
    grid = grid[jax.random.permutation(jax.random.fold_in(own, 1), rows)]
    offset_by = jax.random.randint(jax.random.fold_in(own, 2), (rows, 1), 0, top)
    return jnp.take_along_axis(grid, (jnp.arange(top)[None, :] + offset_by) % top, axis=1)


def portions_of(amount, total, most, slope, full):
    loads = [(1 << 20) // math.isqrt(standing ** slope) + 1 for standing in range(1, amount + 1)]
    largest = most if full else min(most, max(-(-total // amount), total * loads[0] // sum(loads)))
    least = 1 if total - largest >= amount - 1 else 0
    holding, surplus = [largest] + [least] * (amount - 1), total - largest - least * (amount - 1)
    while surplus > 0:
        free = [i for i in range(1, amount) if holding[i] < largest] or [i for i in range(1, amount) if holding[i] < most]
        mass, left = sum([loads[i] for i in free]), surplus
        for i in free:
            extra = min(most - holding[i], max(1, left * loads[i] // mass), surplus)
            holding[i] = holding[i] + extra
            surplus = surplus - extra
    return np.array(holding)


def normal_values(stream_key, shape, deviation, reach, pieces=(), kind=jnp.bfloat16):
    gain = shard_levels(stream_key, shape, pieces, -0.22, 0.18) if pieces else 1.0
    result = jax.random.normal(stream_key, shape, jnp.float32) * deviation * gain
    return jnp.minimum(jnp.maximum(result, -reach), reach).astype(kind)


def setup_inputs(seed: int = 0) -> dict:
    arg_keys = jax.random.split(jax.random.key(seed), 10)
    tokens = normal_values(arg_keys[0], (TOKENS, D), 1.0, 6.0, ((0, 128),))
    up_grad = normal_values(arg_keys[1], (TOKENS, TOP, FF), 1.0, 6.0, ((0, 128),))
    gate_weights = jnp.clip(0.02 + 0.28 * jax.random.uniform(arg_keys[2], (TOKENS, TOP), jnp.float32) ** shard_levels(arg_keys[2], (TOKENS, TOP), ((0, 128),), -0.2, 0.2), 0.02, 0.3)
    expert_ids_keys = jax.random.split(jax.random.fold_in(arg_keys[3], 1), TOKENS // TOK_DEV)
    expert_ids_turns = jax.random.permutation(jax.random.fold_in(arg_keys[3], 3), TOKENS // TOK_DEV)
    expert_ids = jax.vmap(lambda own, number: deal_out(jax.random.fold_in(arg_keys[3], 2), own, number, TOK_DEV, EXPERTS, TOP, CAP, 1))(expert_ids_keys, expert_ids_turns).reshape((TOKENS, TOP))
    new_home = draw_new_home(jax.random.fold_in(arg_keys[9], 71), 0)
    adapter_a = normal_values(arg_keys[5], (EXPERTS, R, D), D ** -0.5, 0.09375, ((0, 16),), jnp.float32)
    adapter_b = normal_values(arg_keys[6], (EXPERTS, R, FF), FF ** -0.5, 0.15625, ((0, 16),), jnp.float32)
    first_moment = normal_values(arg_keys[7], (EXPERTS, PARAMS), 0.3, 4.0, ((0, 16), (1, 8)), jnp.float32)
    second_moment = jnp.clip(jnp.exp(math.log(1.0) - 4.6051702 * jax.random.uniform(arg_keys[8], (EXPERTS, PARAMS), jnp.float32) ** shard_levels(arg_keys[8], (EXPERTS, PARAMS), ((0, 16), (1, 8)), -0.2, 0.2)), 0.01, 1.0)
    return {"tokens": tokens, "up_grad": up_grad, "gate_weights": gate_weights, "expert_ids": expert_ids, "new_home": new_home, "adapter_a": adapter_a, "adapter_b": adapter_b, "first_moment": first_moment, "second_moment": second_moment}


beta_one = 0.9
beta_two = 0.999
learn_rate = 0.001
decay_rate = 0.01
adam_eps = 1e-08
adapter_scale_factor = 2.0
adam_step = 10.0

def expert_grads(expert, tokens, flat_ids, cotangents, adapter_a, adapter_b):
    most = CAP * N_DP * N_EXPERT
    match = flat_ids == expert
    chosen = jnp.nonzero(match, size=most, fill_value=0)[0].astype(jnp.int32)
    count = jnp.sum(match.astype(jnp.int32))
    live = jnp.arange(most, dtype=jnp.int32) < count
    token_rows = tokens[chosen // TOP]
    output_gradients = jnp.where(live[:, None], cotangents[chosen], jnp.zeros((), jnp.bfloat16))
    a16 = adapter_a[expert].astype(jnp.bfloat16)
    b16 = adapter_b[expert].astype(jnp.bfloat16)
    low_rank_hidden = jnp.dot(token_rows, a16.T, preferred_element_type=jnp.float32).astype(jnp.bfloat16)
    backward_rows = jnp.dot(output_gradients, b16.T, preferred_element_type=jnp.float32).astype(jnp.bfloat16)
    down_adapter_gradient = adapter_scale_factor * jnp.dot(backward_rows.T, token_rows, preferred_element_type=jnp.float32)
    up_adapter_gradient = adapter_scale_factor * jnp.dot(low_rank_hidden.T, output_gradients, preferred_element_type=jnp.float32)
    return jnp.concatenate([down_adapter_gradient.reshape(-1), up_adapter_gradient.reshape(-1)])

def reference(tokens, up_grad, gate_weights, expert_ids, new_home, adapter_a, adapter_b, first_moment, second_moment):
    flat_ids = expert_ids.reshape(-1).astype(jnp.int32)
    cotangents = (gate_weights[:, :, None] * up_grad.astype(jnp.float32)).astype(jnp.bfloat16).reshape(TOKENS * TOP, FF)
    grads = lax.map(lambda expert: expert_grads(expert, tokens, flat_ids, cotangents, adapter_a, adapter_b), jnp.arange(EXPERTS, dtype=jnp.int32))
    param = jnp.concatenate([adapter_a.reshape(EXPERTS, -1), adapter_b.reshape(EXPERTS, -1)], axis=1)
    first = beta_one * first_moment + (1.0 - beta_one) * grads
    second = beta_two * second_moment + (1.0 - beta_two) * grads * grads
    fix_one = 1.0 - beta_one ** adam_step
    fix_two = 1.0 - beta_two ** adam_step
    updated = param - learn_rate * (first / fix_one / (jnp.sqrt(second / fix_two) + adam_eps) + decay_rate * param)
    owner = jnp.zeros((EXPERTS,), jnp.int32).at[new_home].set(jnp.arange(EXPERTS, dtype=jnp.int32))
    updated = updated[owner]
    new_a = updated[:, :R * D].reshape(EXPERTS, R, D)
    new_b = updated[:, R * D:].reshape(EXPERTS, R, FF)
    return (new_a, new_b, first[owner], second[owner])
```

```python
import functools

import jax
import jax.numpy as jnp
from jax import lax
from jax.experimental import pallas as pl
from jax.experimental.pallas import tpu as pltpu
from jax.sharding import PartitionSpec as P

beta_one = 0.9
beta_two = 0.999
learn_rate = 0.001
decay_rate = 0.01
adam_eps = 1e-08
adapter_scale_factor = 2.0
adam_step = 10.0

D = 4096
FF = 1536
TOP = 8
R = 32
J = 8
TOK = 128
COPIES = TOK * TOP
CAP = 10
NE = 16
ND = 8
ROWS = J * CAP
RJ = R * J
UNIT = 512
SHARE = 22528
HALF = SHARE // 2
UNITS = HALF // UNIT
PIECE = HALF // 8
HC = D // 2

MESH = pl.DeviceIdType.MESH
BF = jnp.bfloat16
F32 = jnp.float32
I32 = jnp.int32


def iota(shape, dim):
    return lax.broadcasted_iota(I32, shape, dim)


def unit_place(number):
    share, inside = divmod(number, 2 * UNITS)
    half, column = divmod(inside, UNITS)
    return share, half, column


def unit_source(number):
    if number < D // UNIT * R:
        return True, number // (D // UNIT), number % (D // UNIT)
    number = number - D // UNIT * R
    return False, number // (FF // UNIT), number % (FF // UNIT)


def dispatch_kernel(
    tok, up, gate, ids_flat, ids_t, a, b, out,
    gathered, cots, send, got, ids_all, a16, b16, pick, onehot, low, weights, lows, back, grad_a, grad_b, row,
    own_sem, ids_send, ids_recv, cot_send, cot_recv, tok_send, tok_recv, sib_recv,
):
    dp = lax.axis_index("dp")
    me = lax.axis_index("expert")
    x = me // 4
    yh = (me // 2) % 2
    core = me % 2
    dp_across = (dp + 4) % 8

    def place(dy, dx, dc):
        return ((x + dx) % 4) * 4 + ((yh + dy) % 2) * 2 + (core + dc) % 2

    def device(dy, dx, dc):
        return (dp_across if dy else dp, place(dy, dx, dc))

    peers = [(dy, dx, dc) for dx in (2, 1, 3, 0) for dy in (1, 0) for dc in (0, 1) if (dy, dx, dc) != (0, 0, 0)]

    own = pltpu.make_async_copy(tok, gathered.at[pl.ds(pl.multiple_of(me * TOK, TOK), TOK)], own_sem)
    own.start()
    barrier = pltpu.get_barrier_semaphore()
    for peer in peers:
        pl.semaphore_signal(barrier, inc=1, device_id=device(*peer), device_id_type=MESH)
    pl.semaphore_wait(barrier, len(peers))
    own.wait()

    sent = []

    def block(dy, dx, dc, half, part):
        rows = place(dy, dx, dc) * TOK
        size = TOK
        if part is not None:
            rows = rows + part * (TOK // 2)
            size = TOK // 2
        return gathered.at[pl.ds(pl.multiple_of(rows, TOK // 2), size), pl.ds(half * HC, HC)]

    def push(src, half, part, to, sem):
        ref = block(*src, half, part)
        copy = pltpu.make_async_remote_copy(
            src_ref=ref, dst_ref=ref, send_sem=tok_send.at[len(sent)], recv_sem=sem, device_id=device(*to), device_id_type=MESH
        )
        copy.start()
        sent.append(copy)

    def slot(half, dy, dx, part):
        return tok_recv.at[((half * 2 + dy) * 4 + dx) * 2 + part]

    def sib_slot(half, dy, dx):
        return sib_recv.at[(half * 2 + dy) * 4 + dx]

    def arrive(half, dy, dx, part=None):
        ref = block(dy, dx, 0, half, part)
        pltpu.make_async_remote_copy(
            src_ref=ref, dst_ref=ref, send_sem=tok_send.at[0], recv_sem=slot(half, dy, dx, part or 0), device_id=device(0, 1, 0), device_id_type=MESH
        ).wait_recv()

    def to_sibling(half, dy, dx):
        push((dy, dx, 0), half, None, (0, 0, 1), sib_slot(half, dy, dx))

    def to_across(half, dx):
        push((0, dx, 0), half, None, (1, 0, 0), slot(half, 1, dx, 0))

    def to_right(half, dy, dx, part=None):
        push((dy, dx, 0), half, part, (0, 1, 0), slot(half, dy, (dx + 3) % 4, part or 0))

    def to_left(half, dy, dx, part=None):
        push((dy, dx, 0), half, part, (0, 3, 0), slot(half, dy, (dx + 1) % 4, part or 0))

    to_across(1, 0)
    to_right(0, 0, 0)
    to_left(0, 0, 0)
    to_across(0, 0)
    to_right(1, 0, 0)
    to_left(1, 0, 0)
    to_sibling(0, 0, 0)
    to_sibling(1, 0, 0)

    small = []
    mine = ids_all.at[pl.ds(pl.multiple_of(me * TOP, TOP), TOP)]
    ids_all[pl.ds(pl.multiple_of(me * TOP, TOP), TOP), :] = ids_t[...]
    for number, peer in enumerate(peers):
        copy = pltpu.make_async_remote_copy(
            src_ref=mine, dst_ref=mine, send_sem=ids_send.at[number], recv_sem=ids_recv.at[me], device_id=device(*peer), device_id_type=MESH
        )
        copy.start()
        small.append(copy)

    before = (iota((TOK, TOK), 0) < iota((TOK, TOK), 1)).astype(BF)
    experts = iota((TOK, TOK), 0)
    total = jnp.zeros((TOK, 1), F32)
    for part in range(TOP):
        hit = ids_flat[:, part * TOK:(part + 1) * TOK] == experts
        value = hit.astype(F32)
        count = jnp.dot(value.astype(BF), before, preferred_element_type=F32) + total
        total = total + jnp.sum(value, axis=1, keepdims=True)
        row[:, part * TOK:(part + 1) * TOK] = jnp.sum(
            jnp.where(hit, count + (CAP * experts).astype(F32), 0.0), axis=0, keepdims=True
        ).astype(I32)

    @pl.loop(0, TOP)
    def _(part):
        rows = pl.ds(pl.multiple_of(part * TOK, TOK), TOK)
        cots[rows, :] = (gate[rows, :] * up[rows, :].astype(F32)).astype(BF)

    def pack(dx):
        base = pl.multiple_of(((x + dx) % 4) * (4 * ROWS), 4 * ROWS)
        pick[...] = jnp.where(iota((4 * ROWS, COPIES), 0) + base == row[...], 1.0, 0.0).astype(BF)

        @pl.loop(0, FF // UNIT)
        def _(part):
            cols = pl.ds(pl.multiple_of(part * UNIT, UNIT), UNIT)
            send[pl.ds(base, 4 * ROWS), cols] = jnp.dot(pick[...], cots[:, cols], preferred_element_type=F32).astype(BF)

    cot_sent = []
    for dx in (2, 1, 3, 0):
        pack(dx)
        for peer in [p for p in peers if p[1] == dx]:
            copy = pltpu.make_async_remote_copy(
                src_ref=send.at[pl.ds(pl.multiple_of(place(*peer) * ROWS, ROWS), ROWS)],
                dst_ref=got.at[pl.ds(pl.multiple_of(me * ROWS, ROWS), ROWS)],
                send_sem=cot_send.at[len(cot_sent)], recv_sem=cot_recv.at[me],
                device_id=device(*peer), device_id_type=MESH,
            )
            copy.start()
            cot_sent.append(copy)
    my_rows = pl.ds(pl.multiple_of(me * ROWS, ROWS), ROWS)
    got[my_rows, :] = send[my_rows, :]

    arrive(1, 1, 0)
    to_right(1, 1, 0)
    to_left(1, 1, 0)
    to_sibling(1, 1, 0)
    arrive(0, 0, 3)
    to_right(0, 0, 3, 0)
    to_across(0, 3)
    to_sibling(0, 0, 3)
    arrive(0, 0, 1)
    to_left(0, 0, 1, 1)
    to_across(0, 1)
    to_sibling(0, 0, 1)
    arrive(0, 1, 0)
    to_sibling(0, 1, 0)
    arrive(1, 0, 3)
    to_right(1, 0, 3, 0)
    to_sibling(1, 0, 3)
    arrive(1, 0, 1)
    to_left(1, 0, 1, 1)
    to_sibling(1, 0, 1)
    arrive(0, 0, 2, 0)
    arrive(0, 0, 2, 1)
    to_across(0, 2)
    to_sibling(0, 0, 2)
    arrive(1, 1, 3)
    to_right(1, 1, 3, 0)
    to_sibling(1, 1, 3)
    arrive(1, 1, 1)
    to_left(1, 1, 1, 1)
    to_sibling(1, 1, 1)
    arrive(0, 1, 3)
    to_sibling(0, 1, 3)
    arrive(0, 1, 1)
    to_sibling(0, 1, 1)

    turn = (iota((RJ, RJ), 1) == (iota((RJ, RJ), 0) % J) * R + iota((RJ, RJ), 0) // J).astype(F32).astype(BF)

    @pl.loop(0, D // UNIT)
    def _(part):
        cols = pl.ds(pl.multiple_of(part * UNIT, UNIT), UNIT)
        a16[:, cols] = jnp.dot(turn, a[:, cols].astype(BF), preferred_element_type=F32).astype(BF)

    @pl.loop(0, FF // UNIT)
    def _(part):
        cols = pl.ds(pl.multiple_of(part * UNIT, UNIT), UNIT)
        b16[:, cols] = jnp.dot(turn, b[:, cols].astype(BF), preferred_element_type=F32).astype(BF)

    for peer in peers:
        ref = ids_all.at[pl.ds(pl.multiple_of(place(*peer) * TOP, TOP), TOP)]
        pltpu.make_async_remote_copy(
            src_ref=ref, dst_ref=ref, send_sem=ids_send.at[0], recv_sem=ids_recv.at[place(*peer)], device_id=device(*peer), device_id_type=MESH
        ).wait_recv()
    repeat = (iota((ROWS, J), 0) // CAP == iota((ROWS, J), 1)).astype(F32).astype(BF)
    turn_in = (iota((ROWS, TOK), 0) % CAP).astype(F32)

    @pl.loop(0, NE)
    def _(source):
        ids = ids_all[pl.ds(pl.multiple_of(source * TOP, TOP), TOP), :]
        hit = jnp.zeros((J, TOK), F32)
        for k in range(TOP):
            hit = hit + jnp.where(ids[k:k + 1, :] == iota((J, TOK), 0) + me * J, 1.0, 0.0)
        count = jnp.dot(hit.astype(BF), before, preferred_element_type=F32)
        value = jnp.where(hit > 0.5, count, -1.0)
        spread = jnp.dot(repeat, value.astype(BF), preferred_element_type=F32)
        onehot[pl.ds(pl.multiple_of(source * ROWS, ROWS), ROWS), :] = jnp.where(spread == turn_in, 1.0, 0.0).astype(BF)

    for peer in peers:
        ref = got.at[pl.ds(pl.multiple_of(place(*peer) * ROWS, ROWS), ROWS)]
        pltpu.make_async_remote_copy(
            src_ref=ref, dst_ref=ref, send_sem=cot_send.at[0], recv_sem=cot_recv.at[place(*peer)], device_id=device(*peer), device_id_type=MESH
        ).wait_recv()

    own_column = (iota((4 * ROWS, RJ), 0) % ROWS) // CAP == iota((4 * ROWS, RJ), 1) % J

    @pl.loop(0, 4)
    def _(part):
        rows = pl.ds(pl.multiple_of(part * (4 * ROWS), 4 * ROWS), 4 * ROWS)
        value = lax.dot_general(got[rows, :], b16[...], (((1,), (1,)), ((), ())), preferred_element_type=F32)
        back[rows, :] = jnp.where(own_column, value, 0.0).astype(BF)

    @pl.loop(0, NE)
    def _(source):
        rows = pl.ds(pl.multiple_of(source * ROWS, ROWS), ROWS)
        cols = pl.ds(pl.multiple_of(source * TOK, TOK), TOK)
        weights[:, cols] = lax.dot_general(
            back[rows, :], onehot[rows, :], (((0,), (0,)), ((), ())), preferred_element_type=F32
        ).astype(BF)

    arrive(1, 0, 2, 0)
    arrive(1, 0, 2, 1)
    to_sibling(1, 0, 2)
    arrive(1, 1, 2, 0)
    arrive(1, 1, 2, 1)
    to_sibling(1, 1, 2)
    arrive(0, 1, 2)
    to_sibling(0, 1, 2)
    for half in range(2):
        for dy in range(2):
            for dx in range(4):
                ref = block(dy, dx, 1, half, None)
                pltpu.make_async_remote_copy(
                    src_ref=ref, dst_ref=ref, send_sem=tok_send.at[0], recv_sem=sib_slot(half, dy, dx), device_id=device(0, 0, 1), device_id_type=MESH
                ).wait_recv()

    @pl.loop(0, 4)
    def _(part):
        rows = pl.ds(pl.multiple_of(part * UNIT, UNIT), UNIT)
        low[rows, :] = lax.dot_general(
            gathered[rows, :], a16[...], (((1,), (1,)), ((), ())), preferred_element_type=F32
        ).astype(BF)

    @pl.loop(0, NE)
    def _(source):
        rows = pl.ds(pl.multiple_of(source * ROWS, ROWS), ROWS)
        value = jnp.dot(onehot[rows, :], low[pl.ds(pl.multiple_of(source * TOK, TOK), TOK), :], preferred_element_type=F32)
        lows[rows, :] = jnp.where(own_column[:ROWS], value, 0.0).astype(BF)

    @pl.loop(0, D // UNIT)
    def _(part):
        cols = pl.ds(pl.multiple_of(part * UNIT, UNIT), UNIT)
        grad_a[:, cols] = jnp.dot(weights[...], gathered[:, cols], preferred_element_type=F32)

    @pl.loop(0, FF // UNIT)
    def _(part):
        cols = pl.ds(pl.multiple_of(part * UNIT, UNIT), UNIT)
        grad_b[:, cols] = lax.dot_general(lows[...], got[:, cols], (((0,), (0,)), ((), ())), preferred_element_type=F32)

    def grad_unit(number):
        from_a, r, column = unit_source(number)
        ref = grad_a if from_a else grad_b
        return ref[r * J:(r + 1) * J, column * UNIT:(column + 1) * UNIT]

    for share in range(ND):
        for column in range(UNITS):
            first = share * 2 * UNITS + column
            both = jnp.concatenate([grad_unit(first), grad_unit(first + UNITS)], axis=0)
            out[share * 16:(share + 1) * 16, column * UNIT:(column + 1) * UNIT] = both.astype(BF)

    for copy in sent + small + cot_sent:
        copy.wait_send()


def update_kernel(
    grads, a, b, first, second, meta, whole, first_out, second_out,
    got, shared, rows_a, rows_b, param, moving, packed, landed,
    grad_send, grad_recv, move_send, move_recv, all_send, all_recv, own_sem,
):
    dp = lax.axis_index("dp")
    me = lax.axis_index("expert")
    barrier = pltpu.get_barrier_semaphore()
    groups = [((dp + step) % ND, me) for step in range(1, ND)]
    homes = [(dp, (me + step) % NE) for step in range(1, NE)]
    for peer in groups + homes:
        pl.semaphore_signal(barrier, inc=1, device_id=peer, device_id_type=MESH)
    pl.semaphore_wait(barrier, len(groups) + len(homes))

    def rows16(index):
        return pl.ds(pl.multiple_of(index * 16, 16), 16)

    grad_sent = []
    for step in (4, 1, 7, 3, 5, 2, 6):
        to = groups[step - 1]
        copy = pltpu.make_async_remote_copy(
            src_ref=grads.at[rows16(to[0])], dst_ref=got.at[rows16(dp)], send_sem=grad_send.at[step], recv_sem=grad_recv.at[dp],
            device_id=to, device_id_type=MESH,
        )
        copy.start()
        grad_sent.append(copy)
    got[rows16(dp), :] = grads[rows16(dp), :]

    exact = lax.Precision.HIGHEST
    start = 2 * UNITS * dp
    a_first = jnp.minimum(start // (D // UNIT), R - 8)
    b_first = jnp.clip((start - D // UNIT * R) // (FF // UNIT), 0, R - 16)

    def chooser(count, base):
        index = iota((count * J, RJ), 0)
        return (iota((count * J, RJ), 1) == (index % J) * R + index // J + base).astype(F32)

    @pl.loop(0, D // UNIT)
    def _(part):
        cols = pl.ds(pl.multiple_of(part * UNIT, UNIT), UNIT)
        rows_a[:, cols] = jnp.dot(chooser(8, a_first), a[:, cols], preferred_element_type=F32, precision=exact)

    @pl.loop(0, FF // UNIT)
    def _(part):
        cols = pl.ds(pl.multiple_of(part * UNIT, UNIT), UNIT)
        rows_b[:, cols] = jnp.dot(chooser(16, b_first), b[:, cols], preferred_element_type=F32, precision=exact)

    @pl.loop(0, UNITS)
    def _(column):
        for half in range(2):
            number = start + half * UNITS + column
            in_a = jnp.clip(number // (D // UNIT) - a_first, 0, 7)
            col_a = number % (D // UNIT)
            number_b = jnp.maximum(number - D // UNIT * R, 0)
            in_b = jnp.clip(number_b // (FF // UNIT) - b_first, 0, 15)
            col_b = number_b % (FF // UNIT)
            value_a = rows_a[pl.ds(pl.multiple_of(in_a * J, J), J), pl.ds(pl.multiple_of(col_a * UNIT, UNIT), UNIT)]
            value_b = rows_b[pl.ds(pl.multiple_of(in_b * J, J), J), pl.ds(pl.multiple_of(col_b * UNIT, UNIT), UNIT)]
            param[half * J:(half + 1) * J, pl.ds(pl.multiple_of(column * UNIT, UNIT), UNIT)] = jnp.where(
                number < D // UNIT * R, value_a, value_b
            )

    index = iota((256, 128), 0)
    lane = iota((256, 128), 1)
    same = (index % 8 == lane // 16) & ((index // 8) % 2 == (lane // 8) % 2)
    leave = (same & (index // 16 == meta[0:1, :]) & (index // 16 != me)).astype(F32).astype(BF)
    enter = (same & (index // 16 == meta[1:2, :]) & (index // 16 != me)).astype(F32).astype(BF)
    index = iota((128, 128), 0)
    lane = iota((128, 128), 1)
    stay = ((index // 8 == lane // 8) & (index % 8 == meta[2:3, :]) & (meta[1:2, :] == me)).astype(F32).astype(BF)

    for step in range(1, ND):
        ref = got.at[rows16((dp + step) % ND)]
        pltpu.make_async_remote_copy(
            src_ref=ref, dst_ref=ref, send_sem=grad_send.at[0], recv_sem=grad_recv.at[(dp + step) % ND],
            device_id=groups[step - 1], device_id_type=MESH,
        ).wait_recv()

    fix_one = 1.0 - beta_one**adam_step
    fix_two = 1.0 - beta_two**adam_step

    @pl.loop(0, 8)
    def _(piece):
        cols = pl.ds(pl.multiple_of(piece * PIECE, 128), PIECE)
        late = pl.ds(pl.multiple_of(HALF + piece * PIECE, 128), PIECE)
        grad = got[0:16, cols].astype(F32)
        for source in range(1, ND):
            grad = grad + got[source * 16:(source + 1) * 16, cols].astype(F32)
        grad = adapter_scale_factor * grad
        one = beta_one * jnp.concatenate([first[:, cols], first[:, late]], axis=0) + (1.0 - beta_one) * grad
        two = beta_two * jnp.concatenate([second[:, cols], second[:, late]], axis=0) + (1.0 - beta_two) * grad * grad
        old = param[:, cols]
        new = old - learn_rate * (one / fix_one / (jnp.sqrt(two / fix_two) + adam_eps) + decay_rate * old)
        place = rows16(piece)
        moving[0, place, :] = new.astype(BF)
        moving[1, place, :] = one.astype(BF)
        moving[2, place, :] = two.astype(BF)

    move_sent = []
    for kind in range(3):
        packed[kind] = jnp.dot(leave, moving[kind], preferred_element_type=F32).astype(BF)
        landed[kind, rows16(me), :] = jnp.zeros((16, PIECE), BF)
        for step in (8, 9, 10, 11, 7, 6, 5, 4, 12, 13, 14, 15, 3, 2, 1):
            to = homes[step - 1]
            copy = pltpu.make_async_remote_copy(
                src_ref=packed.at[kind, rows16(to[1])], dst_ref=landed.at[kind, rows16(me)],
                send_sem=move_send.at[kind * NE + step], recv_sem=move_recv.at[kind * NE + me],
                device_id=to, device_id_type=MESH,
            )
            copy.start()
            move_sent.append(copy)

    def arrived(kind):
        for step in range(1, NE):
            source = (me + step) % NE
            ref = landed.at[kind, rows16(source)]
            pltpu.make_async_remote_copy(
                src_ref=ref, dst_ref=ref, send_sem=move_send.at[0], recv_sem=move_recv.at[kind * NE + source],
                device_id=homes[step - 1], device_id_type=MESH,
            ).wait_recv()
        took = (((0,), (0,)), ((), ()))
        return lax.dot_general(enter, landed[kind], took, preferred_element_type=F32) + lax.dot_general(
            stay, moving[kind], took, preferred_element_type=F32
        )

    new = arrived(0).astype(BF)
    for piece in range(8):
        shared[:, piece * PIECE:(piece + 1) * PIECE] = new[piece * 16:(piece + 1) * 16, :]
    all_sent = []
    for step in (4, 1, 7, 3, 5, 2, 6):
        copy = pltpu.make_async_remote_copy(
            src_ref=shared, dst_ref=whole.at[rows16(dp)], send_sem=all_send.at[step], recv_sem=all_recv.at[dp],
            device_id=groups[step - 1], device_id_type=MESH,
        )
        copy.start()
        all_sent.append(copy)
    keep = pltpu.make_async_copy(shared, whole.at[rows16(dp)], own_sem)
    keep.start()
    first_out[...] = arrived(1).astype(BF)
    second_out[...] = arrived(2).astype(BF)
    for step in range(1, ND):
        ref = whole.at[rows16((dp + step) % ND)]
        pltpu.make_async_remote_copy(
            src_ref=ref, dst_ref=ref, send_sem=all_send.at[0], recv_sem=all_recv.at[(dp + step) % ND],
            device_id=groups[step - 1], device_id_type=MESH,
        ).wait_recv()
    keep.wait()
    for copy in grad_sent + move_sent + all_sent:
        copy.wait_send()


def finish_kernel(whole, first, second, new_a, new_b, new_first, new_second):
    turn = (iota((RJ, RJ), 1) == (iota((RJ, RJ), 0) % R) * J + iota((RJ, RJ), 0) // R).astype(F32).astype(BF)

    def unit(number):
        share, half, column = unit_place(number)
        value = whole[share * 16:(share + 1) * 16, column * UNIT:(column + 1) * UNIT].astype(F32)
        return value[half * J:(half + 1) * J]

    for out, columns, base in ((new_a, D // UNIT, 0), (new_b, FF // UNIT, D // UNIT * R)):
        for column in range(columns):
            stack = jnp.concatenate([unit(base + r * columns + column) for r in range(R)], axis=0).astype(BF)
            out[:, column * UNIT:(column + 1) * UNIT] = jnp.dot(turn, stack, preferred_element_type=F32)
    for out, value in ((new_first, first), (new_second, second)):
        for piece in range(8):
            both = value[piece * 16:(piece + 1) * 16, :].astype(F32)
            out[:, piece * PIECE:(piece + 1) * PIECE] = both[:J]
            out[:, HALF + piece * PIECE:HALF + (piece + 1) * PIECE] = both[J:]


def vmem(count):
    return [pl.BlockSpec(memory_space=pltpu.VMEM)] * count


def shards(tokens, up_grad, gate_weights, expert_ids, new_home, adapter_a, adapter_b, first_moment, second_moment):
    me = lax.axis_index("expert")
    places = jnp.arange(J, dtype=I32)
    dest = lax.dynamic_slice_in_dim(new_home, me * J, J, 0) // J
    named = new_home[None, :] == (me * J + places)[:, None]
    owner = jnp.sum(jnp.where(named, jnp.arange(NE * J, dtype=I32)[None, :], 0), axis=1)
    meta = jnp.tile(jnp.stack([dest, owner // J, owner % J] + [places] * 5), (1, 16))
    a = adapter_a.reshape(RJ, D)
    b = adapter_b.reshape(RJ, FF)
    dma = pltpu.SemaphoreType.DMA
    grads = pl.pallas_call(
        dispatch_kernel,
        out_shape=jax.ShapeDtypeStruct((ND * 16, HALF), BF),
        in_specs=[pl.BlockSpec(memory_space=pl.ANY)] + vmem(6),
        out_specs=pl.BlockSpec(memory_space=pltpu.VMEM),
        scratch_shapes=[
            pltpu.VMEM((NE * TOK, D), BF),
            pltpu.VMEM((COPIES, FF), BF),
            pltpu.VMEM((NE * ROWS, FF), BF),
            pltpu.VMEM((NE * ROWS, FF), BF),
            pltpu.VMEM((NE * TOP, TOK), I32),
            pltpu.VMEM((RJ, D), BF),
            pltpu.VMEM((RJ, FF), BF),
            pltpu.VMEM((4 * ROWS, COPIES), BF),
            pltpu.VMEM((NE * ROWS, TOK), BF),
            pltpu.VMEM((NE * TOK, RJ), BF),
            pltpu.VMEM((RJ, NE * TOK), BF),
            pltpu.VMEM((NE * ROWS, RJ), BF),
            pltpu.VMEM((NE * ROWS, RJ), BF),
            pltpu.VMEM((RJ, D), F32),
            pltpu.VMEM((RJ, FF), F32),
            pltpu.VMEM((1, COPIES), I32),
            dma,
            dma((NE,)),
            dma((NE,)),
            dma((NE,)),
            dma((NE,)),
            dma((64,)),
            dma((32,)),
            dma((16,)),
        ],
        compiler_params=pltpu.CompilerParams(collective_id=0, has_side_effects=True, vmem_limit_bytes=60 * 2**20),
        name="dispatch",
    )(
        tokens, up_grad.reshape(COPIES, FF), gate_weights.reshape(COPIES, 1), expert_ids.reshape(1, COPIES), expert_ids.T, a, b,
    )
    whole, first, second = pl.pallas_call(
        update_kernel,
        out_shape=[
            jax.ShapeDtypeStruct((ND * 16, HALF), BF),
            jax.ShapeDtypeStruct((128, PIECE), BF),
            jax.ShapeDtypeStruct((128, PIECE), BF),
        ],
        in_specs=vmem(6),
        out_specs=vmem(3),
        scratch_shapes=[
            pltpu.VMEM((ND * 16, HALF), BF),
            pltpu.VMEM((16, HALF), BF),
            pltpu.VMEM((8 * J, D), F32),
            pltpu.VMEM((16 * J, FF), F32),
            pltpu.VMEM((16, HALF), F32),
            pltpu.VMEM((3, 128, PIECE), BF),
            pltpu.VMEM((3, 256, PIECE), BF),
            pltpu.VMEM((3, 256, PIECE), BF),
            dma((ND,)),
            dma((ND,)),
            dma((3 * NE,)),
            dma((3 * NE,)),
            dma((ND,)),
            dma((ND,)),
            dma,
        ],
        compiler_params=pltpu.CompilerParams(collective_id=1, has_side_effects=True, vmem_limit_bytes=60 * 2**20),
        name="update",
    )(grads, a, b, first_moment, second_moment, meta)
    new_a, new_b, new_first, new_second = pl.pallas_call(
        finish_kernel,
        out_shape=[
            jax.ShapeDtypeStruct((RJ, D), F32),
            jax.ShapeDtypeStruct((RJ, FF), F32),
            jax.ShapeDtypeStruct((J, SHARE), F32),
            jax.ShapeDtypeStruct((J, SHARE), F32),
        ],
        in_specs=vmem(3),
        out_specs=vmem(4),
        compiler_params=pltpu.CompilerParams(vmem_limit_bytes=60 * 2**20),
        name="finish",
    )(whole, first, second)
    return new_a.reshape(J, R, D), new_b.reshape(J, R, FF), new_first, new_second


def solution(mesh):
    placed = (
        P(("dp", "expert"), None),
        P(("dp", "expert"), None, None),
        P(("dp", "expert"), None),
        P(("dp", "expert"), None),
        P(),
        P("expert", None, None),
        P("expert", None, None),
        P("expert", "dp"),
        P("expert", "dp"),
    )
    return jax.shard_map(
        shards,
        mesh=mesh,
        in_specs=placed,
        out_specs=(P("expert", None, None), P("expert", None, None), P("expert", "dp"), P("expert", "dp")),
        check_vma=False,
    )
```

```python
import jax
import jax.numpy as jnp
from jax import lax
from jax.experimental import pallas as pl
from jax.experimental.pallas import tpu as pltpu
from jax.sharding import PartitionSpec as P

beta_one = 0.9
beta_two = 0.999
learn_rate = 0.001
decay_rate = 0.01
adam_eps = 1e-08
adapter_scale_factor = 2.0
adam_step = 10.0

D = 4096
FF = 1536
TOP = 8
R = 32
J = 8
TOK = 128
COPIES = TOK * TOP
CAP = 10
NE = 16
ND = 8
ROWS = J * CAP
EARLY = 48
LATE = ROWS - EARLY
RJ = R * J
CH = 4
RC = R * CH
UNIT = 512
SHARE = 22528
PIECE = SHARE // 16
QUARTER = SHARE // 4
UNITS = QUARTER // UNIT
A_UNITS = D // UNIT
B_UNITS = FF // UNIT
SPLIT = 1536
Y_FIRST = 48

MESH = pl.DeviceIdType.MESH
BF = jnp.bfloat16
F32 = jnp.float32
I32 = jnp.int32


def iota(shape, dim):
    return lax.broadcasted_iota(I32, shape, dim)


def ones(mask):
    return mask.astype(F32).astype(BF)


def contract(lhs, rhs, i, k, precision=None):
    return lax.dot_general(lhs, rhs, (((i,), (k,)), ((), ())), preferred_element_type=F32, precision=precision)


def at(start, size, unit=None):
    return pl.ds(pl.multiple_of(start, unit or size), size)


def main_kernel(
    tok, up_hbm, gate_t, ids_t, homes_row, a_hbm, b_hbm, first_hbm, second_hbm, whole, first_out, second_out,
    gathered, cots, send, got_early, got_late, ids_all, a, b, a16, b16, pick, hot_early, hot_late, low, weights,
    low_early, low_late, back_early, back_late, grad_a, grad_b, row, wire, wire_got,
    first, second, rows_a, rows_b, param, moving, packed, landed,
    local, ids_send, ids_recv, cot_send, cot_recv, tok_send, tok_recv, sib_recv,
    grad_send, grad_recv, move_send, move_recv, all_send, all_recv,
):
    dp = lax.axis_index("dp")
    me = lax.axis_index("expert")
    x = me // 4
    yh = (me // 2) % 2
    core = me % 2
    dp_across = (dp + 4) % 8
    yl = dp // 4
    z = dp % 4

    def place(dy, dx, dc):
        return ((x + dx) % 4) * 4 + ((yh + dy) % 2) * 2 + (core + dc) % 2

    def device(dy, dx, dc):
        return (dp_across if dy else dp, place(dy, dx, dc))

    def copy_to(src, dst, send_sem, recv_sem, to):
        return pltpu.make_async_remote_copy(
            src_ref=src, dst_ref=dst, send_sem=send_sem, recv_sem=recv_sem, device_id=to, device_id_type=MESH
        )

    peers = [
        (1, 0, 0), (0, 2, 0), (0, 1, 0), (0, 3, 0), (1, 2, 0), (1, 0, 1), (0, 2, 1), (1, 1, 0),
        (0, 3, 1), (1, 2, 1), (1, 3, 0), (0, 1, 1), (1, 1, 1), (1, 3, 1), (0, 0, 1),
    ]
    groups = [((dp + step) % ND, me) for step in range(1, ND)]
    homes = [(dp, (me + step) % NE) for step in range(1, NE)]

    loads = [
        pltpu.make_async_copy(src, dst, local.at[number])
        for number, (src, dst) in enumerate([
            (tok, gathered.at[at(me * TOK, TOK)]), (up_hbm, cots), (a_hbm, a), (b_hbm, b), (first_hbm, first), (second_hbm, second),
        ])
    ]
    for load in loads:
        load.start()
    barrier = pltpu.get_barrier_semaphore()
    met = groups + homes + [device(*peer) for peer in peers if peer[0]]
    for peer in met:
        pl.semaphore_signal(barrier, inc=1, device_id=peer, device_id_type=MESH)
    pl.semaphore_wait(barrier, len(met))
    loads[0].wait()

    sent = []

    def block(dy, dx, dc, half, part):
        rows = place(dy, dx, dc) * TOK
        size = TOK
        if part is not None:
            rows = rows + part * (TOK // 2)
            size = TOK // 2
        cols = pl.ds(SPLIT, D - SPLIT) if half else pl.ds(0, SPLIT)
        return gathered.at[at(rows, size), cols]

    def push(src, half, part, to, sem):
        ref = block(*src, half, part)
        copy = copy_to(ref, ref, tok_send.at[len(sent)], sem, device(*to))
        copy.start()
        sent.append(copy)

    def slot(half, dy, dx, part):
        return tok_recv.at[((half * 2 + dy) * 4 + dx) * 2 + part]

    def sib_slot(half, dy, dx):
        return sib_recv.at[(half * 2 + dy) * 4 + dx]

    def arrive(half, dy, dx, part=None):
        ref = block(dy, dx, 0, half, part)
        copy_to(ref, ref, tok_send.at[0], slot(half, dy, dx, part or 0), device(0, 1, 0)).wait_recv()

    def to_sibling(half, dy, dx):
        push((dy, dx, 0), half, None, (0, 0, 1), sib_slot(half, dy, dx))

    def to_across(half, dx):
        push((0, dx, 0), half, None, (1, 0, 0), slot(half, 1, dx, 0))

    def to_right(half, dy, dx, part=None):
        push((dy, dx, 0), half, part, (0, 1, 0), slot(half, dy, (dx + 3) % 4, part or 0))

    def to_left(half, dy, dx, part=None):
        push((dy, dx, 0), half, part, (0, 3, 0), slot(half, dy, (dx + 1) % 4, part or 0))

    to_across(1, 0)
    to_right(0, 0, 0)
    to_left(0, 0, 0)
    to_across(0, 0)
    to_right(1, 0, 0)
    to_left(1, 0, 0)
    to_sibling(0, 0, 0)
    to_sibling(1, 0, 0)

    small = []
    mine = at(me * TOP, TOP)
    ids_all[mine, :] = ids_t[...]
    for number, peer in enumerate(peers):
        copy = copy_to(ids_all.at[mine], ids_all.at[mine], ids_send.at[number], ids_recv.at[me], device(*peer))
        copy.start()
        small.append(copy)

    owner_of = iota((TOK, COPIES), 1) // TOP == iota((TOK, COPIES), 0)
    which = iota((TOP, COPIES), 1) % TOP == iota((TOP, COPIES), 0)
    spread = jnp.dot(ids_t[...].astype(F32).astype(BF), ones(owner_of), preferred_element_type=F32)
    ids_flat = jnp.sum(jnp.where(which, spread, 0.0), axis=0, keepdims=True).astype(I32)
    before = ones(iota((TOK, TOK), 0) < iota((TOK, TOK), 1))
    experts = iota((TOK, TOK), 0)
    total = jnp.zeros((TOK, 1), F32)
    for part in range(TOP):
        hit = ids_flat[:, part * TOK:(part + 1) * TOK] == experts
        value = hit.astype(F32)
        count = jnp.dot(value.astype(BF), before, preferred_element_type=F32) + total
        total = total + jnp.sum(value, axis=1, keepdims=True)
        row[:, part * TOK:(part + 1) * TOK] = jnp.sum(
            jnp.where(hit, count + (CAP * experts).astype(F32), 0.0), axis=0, keepdims=True
        ).astype(I32)

    loads[1].wait()

    @pl.loop(0, TOP)
    def _(part):
        rows = at(part * TOK, TOK)
        mine_of = (iota((TOK, TOK), 0) + part * TOK) // TOP == iota((TOK, TOK), 1)
        scale = contract(mine_of.astype(F32), gate_t[...], 1, 1, lax.Precision.HIGHEST)
        scale = jnp.sum(jnp.where(iota((TOK, TOP), 0) % TOP == iota((TOK, TOP), 1), scale, 0.0), axis=1, keepdims=True)
        cots[rows, :] = (scale * cots[rows, :].astype(F32)).astype(BF)

    for dx in (2, 1, 3, 0):
        base = ((x + dx) % 4) * (4 * ROWS)
        pick[...] = ones(iota((4 * ROWS, COPIES), 0) + base == row[...])

        @pl.loop(0, FF // UNIT)
        def _(part):
            cols = at(part * UNIT, UNIT)
            send[at(base, 4 * ROWS), cols] = jnp.dot(pick[...], cots[:, cols], preferred_element_type=F32).astype(BF)

    cot_sent = []

    def send_cots(low_row, high_row, got, index):
        size = high_row - low_row
        for part in range(size // 16):
            for peer in peers:
                copy = copy_to(
                    send.at[at(place(*peer) * ROWS + low_row + part * 16, 16)], got.at[at(me * size + part * 16, 16)],
                    cot_send.at[len(cot_sent)], cot_recv.at[index * NE + me], device(*peer),
                )
                copy.start()
                cot_sent.append(copy)
        got[at(me * size, size, 16), :] = send[at(me * ROWS + low_row, size, 16), :]

    def wait_cots(size, got, index):
        for peer in peers:
            ref = got.at[at(place(*peer) * size, size, 16)]
            copy_to(ref, ref, cot_send.at[0], cot_recv.at[index * NE + place(*peer)], device(*peer)).wait_recv()

    send_cots(0, EARLY, got_early, 0)

    arrive(1, 1, 0)
    to_right(1, 1, 0)
    to_left(1, 1, 0)
    to_sibling(1, 1, 0)
    arrive(0, 0, 3)
    to_right(0, 0, 3, 0)
    to_across(0, 3)
    to_sibling(0, 0, 3)
    arrive(0, 0, 1)
    to_left(0, 0, 1, 1)
    to_across(0, 1)
    to_sibling(0, 0, 1)

    index = iota((RJ, RJ), 0)
    turn = ones(iota((RJ, RJ), 1) == (index // RC * CH + index % CH) * R + (index % RC) // CH)
    loads[2].wait()
    loads[3].wait()

    @pl.loop(0, A_UNITS)
    def _(part):
        cols = at(part * UNIT, UNIT)
        a16[:, cols] = jnp.dot(turn, a[:, cols].astype(BF), preferred_element_type=F32).astype(BF)

    @pl.loop(0, B_UNITS)
    def _(part):
        cols = at(part * UNIT, UNIT)
        b16[:, cols] = jnp.dot(turn, b[:, cols].astype(BF), preferred_element_type=F32).astype(BF)

    arrive(0, 1, 0)
    to_sibling(0, 1, 0)
    arrive(1, 0, 3)
    to_right(1, 0, 3, 0)
    to_sibling(1, 0, 3)
    arrive(1, 0, 1)
    to_left(1, 0, 1, 1)
    to_sibling(1, 0, 1)

    for peer in peers:
        ref = ids_all.at[at(place(*peer) * TOP, TOP)]
        copy_to(ref, ref, ids_send.at[0], ids_recv.at[place(*peer)], device(*peer)).wait_recv()
    repeat = ones(iota((ROWS, J), 0) // CAP == iota((ROWS, J), 1))
    turn_in = (iota((ROWS, TOK), 0) % CAP).astype(F32)

    @pl.loop(0, NE)
    def _(source):
        ids = ids_all[at(source * TOP, TOP), :]
        hit = jnp.zeros((J, TOK), F32)
        for k in range(TOP):
            hit = hit + jnp.where(ids[k:k + 1, :] == iota((J, TOK), 0) + me * J, 1.0, 0.0)
        count = jnp.dot(hit.astype(BF), before, preferred_element_type=F32)
        value = jnp.where(hit > 0.5, count, -1.0)
        hot = ones(jnp.dot(repeat, value.astype(BF), preferred_element_type=F32) == turn_in)
        hot_early[at(source * EARLY, EARLY), :] = hot[:EARLY]
        hot_late[at(source * LATE, LATE), :] = hot[EARLY:]

    arrive(0, 0, 2, 0)
    arrive(0, 0, 2, 1)
    to_across(0, 2)
    to_sibling(0, 0, 2)
    arrive(1, 1, 3)
    to_right(1, 1, 3, 0)
    to_sibling(1, 1, 3)
    arrive(1, 1, 1)
    to_left(1, 1, 1, 1)
    to_sibling(1, 1, 1)
    send_cots(EARLY, ROWS, got_late, 1)
    arrive(0, 1, 3)
    to_sibling(0, 1, 3)
    arrive(0, 1, 1)
    to_sibling(0, 1, 1)
    arrive(1, 0, 2, 0)
    arrive(1, 0, 2, 1)
    to_sibling(1, 0, 2)
    arrive(1, 1, 2, 0)
    arrive(1, 1, 2, 1)
    to_sibling(1, 1, 2)
    arrive(0, 1, 2)
    to_sibling(0, 1, 2)
    for half in range(2):
        for dy in range(2):
            for dx in range(4):
                ref = block(dy, dx, 1, half, None)
                copy_to(ref, ref, tok_send.at[0], sib_slot(half, dy, dx), device(0, 0, 1)).wait_recv()

    @pl.loop(0, 4)
    def _(part):
        rows = at(part * UNIT, UNIT)
        low[rows, :] = contract(gathered[rows, :], a16[...], 1, 1).astype(BF)

    def own(size, base, chunk, count=1):
        line = iota((size * count, RC), 0) % size + base
        return line // CAP == iota((size * count, RC), 1) % CH + chunk * CH

    def backward(got, back, size, base, chunk):
        mask = own(size, base, chunk, 4)

        @pl.loop(0, 4)
        def _(part):
            rows = at(part * (4 * size), 4 * size)
            value = contract(got[rows, :], b16[chunk * RC:(chunk + 1) * RC, :], 1, 1)
            back[rows, :] = jnp.where(mask, value, 0.0).astype(BF)

    def hidden(hot, lows, size, base, chunk):
        mask = own(size, base, chunk)

        @pl.loop(0, NE)
        def _(source):
            rows = at(source * size, size)
            value = jnp.dot(
                hot[rows, :], low[at(source * TOK, TOK), chunk * RC:(chunk + 1) * RC], preferred_element_type=F32
            )
            lows[rows, :] = jnp.where(mask, value, 0.0).astype(BF)

    grad_sent = []

    def gradients(chunk):
        backward(got_early, back_early, EARLY, 0, chunk)
        hidden(hot_early, low_early, EARLY, 0, chunk)
        if chunk:
            backward(got_late, back_late, LATE, EARLY, chunk)
            hidden(hot_late, low_late, LATE, EARLY, chunk)

        @pl.loop(0, NE)
        def _(source):
            rows = at(source * EARLY, EARLY)
            value = contract(back_early[rows, :], hot_early[rows, :], 0, 0)
            if chunk:
                rows = at(source * LATE, LATE)
                value = value + contract(back_late[rows, :], hot_late[rows, :], 0, 0)
            weights[:, at(source * TOK, TOK)] = value.astype(BF)

        @pl.loop(0, D // 1024)
        def _(part):
            cols = at(part * 1024, 1024)
            grad_a[:, cols] = jnp.dot(weights[...], gathered[:, cols], preferred_element_type=F32)

        @pl.loop(0, B_UNITS)
        def _(part):
            cols = at(part * UNIT, UNIT)
            value = contract(low_early[...], got_early[:, cols], 0, 0)
            if chunk:
                value = value + contract(low_late[...], got_late[:, cols], 0, 0)
            grad_b[:, cols] = value

        def grad_unit(number):
            if number < A_UNITS * R:
                r, column = divmod(number, A_UNITS)
                return grad_a[r * CH:(r + 1) * CH, column * UNIT:(column + 1) * UNIT]
            r, column = divmod(number - A_UNITS * R, B_UNITS)
            return grad_b[r * CH:(r + 1) * CH, column * UNIT:(column + 1) * UNIT]

        for share in range(ND):
            for column in range(UNITS):
                parts = [grad_unit((share * 4 + quarter) * UNITS + column) for quarter in range(4)]
                wire[chunk, share * 16:(share + 1) * 16, column * UNIT:(column + 1) * UNIT] = jnp.concatenate(parts, axis=0).astype(BF)

        for step in (4, 1, 7, 3, 5, 2, 6):
            to = groups[step - 1]
            copy = copy_to(
                wire.at[chunk, at(to[0] * 16, 16)], wire_got.at[chunk, at(dp * 16, 16)],
                grad_send.at[chunk * ND + step], grad_recv.at[chunk * ND + dp], to,
            )
            copy.start()
            grad_sent.append(copy)
        wire_got[chunk, at(dp * 16, 16), :] = wire[chunk, at(dp * 16, 16), :]

    wait_cots(EARLY, got_early, 0)
    gradients(0)

    exact = lax.Precision.HIGHEST
    start = 4 * UNITS * dp
    a_first = jnp.minimum(start // A_UNITS, R - 8)
    b_first = jnp.clip((start - A_UNITS * R) // B_UNITS, 0, R - 16)

    def chooser(count, base):
        index = iota((count * J, RJ), 0)
        return (iota((count * J, RJ), 1) == (index % J) * R + index // J + base).astype(F32)

    @pl.loop(0, A_UNITS)
    def _(part):
        cols = at(part * UNIT, UNIT)
        rows_a[:, cols] = jnp.dot(chooser(8, a_first), a[:, cols], preferred_element_type=F32, precision=exact)

    @pl.loop(0, B_UNITS)
    def _(part):
        cols = at(part * UNIT, UNIT)
        rows_b[:, cols] = jnp.dot(chooser(16, b_first), b[:, cols], preferred_element_type=F32, precision=exact)

    @pl.loop(0, 4 * UNITS)
    def _(column):
        number = start + column
        in_a = jnp.clip(number // A_UNITS - a_first, 0, 7)
        number_b = jnp.maximum(number - A_UNITS * R, 0)
        in_b = jnp.clip(number_b // B_UNITS - b_first, 0, 15)
        value_a = rows_a[at(in_a * J, J), at(number % A_UNITS * UNIT, UNIT)]
        value_b = rows_b[at(in_b * J, J), at(number_b % B_UNITS * UNIT, UNIT)]
        param[:, at(column * UNIT, UNIT)] = jnp.where(number < A_UNITS * R, value_a, value_b)

    homes_now = homes_row[...].astype(F32).astype(BF)
    lane = iota((128, 128), 1)
    line = iota((128, 128), 0)
    dest = jnp.dot(homes_now, ones(line == me * J + lane % J), preferred_element_type=F32).astype(I32)
    named = ones(homes_row[...] == me * J + line % J)
    owner = contract(ones(iota((1, 128), 1) >= 0) * iota((1, 128), 1).astype(F32).astype(BF), named, 1, 1).astype(I32)
    stay = ones((line // J == lane // J) & (line % J == owner % J) & (owner // J == me))
    lane = iota((256, 128), 1)
    line = iota((256, 128), 0)
    same = (line % 16 == lane // J) & (line // 16 != me)
    leave = ones(same & (line // 16 == dest // J))
    enter = ones(same & (line // 16 == owner // J))

    wait_cots(LATE, got_late, 1)
    gradients(1)

    for chunk in range(2):
        for step in range(1, ND):
            source = (dp + step) % ND
            ref = wire_got.at[chunk, at(source * 16, 16)]
            copy_to(ref, ref, grad_send.at[0], grad_recv.at[chunk * ND + source], groups[step - 1]).wait_recv()
    loads[4].wait()
    loads[5].wait()

    fix_one = 1.0 - beta_one**adam_step
    fix_two = 1.0 - beta_two**adam_step
    for part in range(4):
        inside = pl.ds(part * PIECE, PIECE)
        totals = []
        for chunk in range(2):
            grad = wire_got[chunk, 0:16, inside].astype(F32)
            for source in range(1, ND):
                grad = grad + wire_got[chunk, source * 16:(source + 1) * 16, inside].astype(F32)
            totals.append(adapter_scale_factor * grad)
        for quarter in range(4):
            piece = quarter * 4 + part
            cols = pl.ds(piece * PIECE, PIECE)
            grad = jnp.concatenate([total[quarter * CH:(quarter + 1) * CH] for total in totals], axis=0)
            one = beta_one * first[:, cols] + (1.0 - beta_one) * grad
            two = beta_two * second[:, cols] + (1.0 - beta_two) * grad * grad
            old = param[:, cols]
            new = old - learn_rate * (one / fix_one / (jnp.sqrt(two / fix_two) + adam_eps) + decay_rate * old)
            for kind, value in enumerate((new, one, two)):
                moving[kind, piece * J:(piece + 1) * J, :] = value.astype(BF)

    move_sent = []

    def move(kind):
        packed[kind] = jnp.dot(leave, moving[kind], preferred_element_type=F32).astype(BF)
        landed[kind, at(me * 16, 16), :] = jnp.zeros((16, PIECE), BF)
        for step in (8, 9, 10, 11, 7, 6, 5, 4, 12, 13, 14, 15, 3, 2, 1):
            to = homes[step - 1]
            copy = copy_to(
                packed.at[kind, at(to[1] * 16, 16)], landed.at[kind, at(me * 16, 16)],
                move_send.at[kind * NE + step], move_recv.at[kind * NE + me], to,
            )
            copy.start()
            move_sent.append(copy)

    def arrived(kind):
        for step in range(1, NE):
            source = (me + step) % NE
            ref = landed.at[kind, at(source * 16, 16)]
            copy_to(ref, ref, move_send.at[0], move_recv.at[kind * NE + source], homes[step - 1]).wait_recv()
        return (contract(enter, landed[kind], 0, 0) + contract(stay, moving[kind], 0, 0)).astype(BF)

    move(0)
    whole[at(dp * 128, 128), :] = arrived(0)

    all_sent = []

    def group(dy, dz):
        return ((yl + dy) % 2) * 4 + (z + dz) % 4

    def part_of(dy, dz, late):
        size = 128 - Y_FIRST if late else Y_FIRST
        return whole.at[at(group(dy, dz) * 128 + (Y_FIRST if late else 0), size, 16)]

    def share_slot(dy, dz, late):
        return all_recv.at[(late * 2 + dy) * 4 + dz]

    def pass_on(dy, dz, late, to_y, to_z):
        ref = part_of(dy, dz, late)
        copy = copy_to(
            ref, ref, all_send.at[len(all_sent)], share_slot((dy + to_y) % 2, (dz - to_z) % 4, late), (group(to_y, to_z), me)
        )
        copy.start()
        all_sent.append(copy)

    def came(dy, dz, late):
        ref = part_of(dy, dz, late)
        copy_to(ref, ref, all_send.at[0], share_slot(dy, dz, late), groups[0]).wait_recv()

    pass_on(0, 0, 0, 1, 0)
    for step in (1, 3, 2):
        pass_on(0, 0, 1, 0, step)
    pass_on(0, 0, 1, 1, 0)
    for step in (1, 3, 2):
        pass_on(0, 0, 0, 0, step)
    move(1)
    move(2)
    came(1, 0, 0)
    for step in (1, 3, 2):
        pass_on(1, 0, 0, 0, step)
    for step in (1, 3, 2):
        came(0, step, 1)
        pass_on(0, step, 1, 1, 0)
    first_out[...] = arrived(1)
    second_out[...] = arrived(2)
    for step in (1, 3, 2):
        came(0, step, 0)
        came(1, step, 0)
    for step in range(4):
        came(1, step, 1)
    for copy in sent + small + cot_sent + grad_sent + move_sent + all_sent:
        copy.wait_send()


def finish_kernel(whole, first, second, new_a, new_b, new_first, new_second):
    index = iota((RJ, RJ), 0)
    turn = ones(iota((RJ, RJ), 1) == index % R * J + index // R)

    def unit(number):
        share, inside = divmod(number * UNIT, SHARE)
        parts = []
        left = UNIT
        while left:
            piece, offset = divmod(inside, PIECE)
            size = min(left, PIECE - offset)
            line = share * 128 + piece * J
            pair = whole[line // 16 * 16:line // 16 * 16 + 16, offset:offset + size].astype(F32)
            parts.append(pair[line % 16:line % 16 + J])
            left -= size
            inside += size
        return parts[0] if len(parts) == 1 else jnp.concatenate(parts, axis=1)

    for out, columns, base in ((new_a, A_UNITS, 0), (new_b, B_UNITS, A_UNITS * R)):
        for column in range(columns):
            stack = jnp.concatenate([unit(base + r * columns + column) for r in range(R)], axis=0).astype(BF)
            out[:, column * UNIT:(column + 1) * UNIT] = jnp.dot(turn, stack, preferred_element_type=F32)
    for out, value in ((new_first, first), (new_second, second)):
        for pair in range(8):
            both = value[pair * 16:(pair + 1) * 16, :].astype(F32)
            out[:, 2 * pair * PIECE:(2 * pair + 1) * PIECE] = both[:J]
            out[:, (2 * pair + 1) * PIECE:(2 * pair + 2) * PIECE] = both[J:]


def vmem(count):
    return [pl.BlockSpec(memory_space=pltpu.VMEM)] * count


def anywhere(count):
    return [pl.BlockSpec(memory_space=pl.ANY)] * count


def shards(tokens, up_grad, gate_weights, expert_ids, new_home, adapter_a, adapter_b, first_moment, second_moment):
    dma = pltpu.SemaphoreType.DMA
    whole, first, second = pl.pallas_call(
        main_kernel,
        out_shape=[
            jax.ShapeDtypeStruct((ND * 128, PIECE), BF),
            jax.ShapeDtypeStruct((128, PIECE), BF),
            jax.ShapeDtypeStruct((128, PIECE), BF),
        ],
        in_specs=anywhere(2) + vmem(3) + anywhere(4),
        out_specs=vmem(3),
        scratch_shapes=[
            pltpu.VMEM((NE * TOK, D), BF),
            pltpu.VMEM((COPIES, FF), BF),
            pltpu.VMEM((NE * ROWS, FF), BF),
            pltpu.VMEM((NE * EARLY, FF), BF),
            pltpu.VMEM((NE * LATE, FF), BF),
            pltpu.VMEM((NE * TOP, TOK), I32),
            pltpu.VMEM((RJ, D), F32),
            pltpu.VMEM((RJ, FF), F32),
            pltpu.VMEM((RJ, D), BF),
            pltpu.VMEM((RJ, FF), BF),
            pltpu.VMEM((4 * ROWS, COPIES), BF),
            pltpu.VMEM((NE * EARLY, TOK), BF),
            pltpu.VMEM((NE * LATE, TOK), BF),
            pltpu.VMEM((NE * TOK, RJ), BF),
            pltpu.VMEM((RC, NE * TOK), BF),
            pltpu.VMEM((NE * EARLY, RC), BF),
            pltpu.VMEM((NE * LATE, RC), BF),
            pltpu.VMEM((NE * EARLY, RC), BF),
            pltpu.VMEM((NE * LATE, RC), BF),
            pltpu.VMEM((RC, D), F32),
            pltpu.VMEM((RC, FF), F32),
            pltpu.VMEM((1, COPIES), I32),
            pltpu.VMEM((2, ND * 16, QUARTER), BF),
            pltpu.VMEM((2, ND * 16, QUARTER), BF),
            pltpu.VMEM((J, SHARE), F32),
            pltpu.VMEM((J, SHARE), F32),
            pltpu.VMEM((8 * J, D), F32),
            pltpu.VMEM((16 * J, FF), F32),
            pltpu.VMEM((J, SHARE), F32),
            pltpu.VMEM((3, 128, PIECE), BF),
            pltpu.VMEM((3, 256, PIECE), BF),
            pltpu.VMEM((3, 256, PIECE), BF),
            dma((6,)),
            dma((NE,)),
            dma((NE,)),
            dma((NE * 5,)),
            dma((2 * NE,)),
            dma((64,)),
            dma((32,)),
            dma((16,)),
            dma((2 * ND,)),
            dma((2 * ND,)),
            dma((3 * NE,)),
            dma((3 * NE,)),
            dma((16,)),
            dma((16,)),
        ],
        compiler_params=pltpu.CompilerParams(collective_id=0, has_side_effects=True, vmem_limit_bytes=63 * 2**20),
        name="dispatch_update",
    )(
        tokens, up_grad.reshape(COPIES, FF), gate_weights.T, expert_ids.T, new_home.reshape(1, NE * J),
        adapter_a.reshape(RJ, D), adapter_b.reshape(RJ, FF), first_moment, second_moment,
    )
    new_a, new_b, new_first, new_second = pl.pallas_call(
        finish_kernel,
        out_shape=[
            jax.ShapeDtypeStruct((RJ, D), F32),
            jax.ShapeDtypeStruct((RJ, FF), F32),
            jax.ShapeDtypeStruct((J, SHARE), F32),
            jax.ShapeDtypeStruct((J, SHARE), F32),
        ],
        in_specs=vmem(3),
        out_specs=vmem(4),
        compiler_params=pltpu.CompilerParams(vmem_limit_bytes=60 * 2**20),
        name="finish",
    )(whole, first, second)
    return new_a.reshape(J, R, D), new_b.reshape(J, R, FF), new_first, new_second


def solution(mesh):
    placed = (
        P(("dp", "expert"), None),
        P(("dp", "expert"), None, None),
        P(("dp", "expert"), None),
        P(("dp", "expert"), None),
        P(),
        P("expert", None, None),
        P("expert", None, None),
        P("expert", "dp"),
        P("expert", "dp"),
    )
    return jax.shard_map(
        shards,
        mesh=mesh,
        in_specs=placed,
        out_specs=(P("expert", None, None), P("expert", None, None), P("expert", "dp"), P("expert", "dp")),
        check_vma=False,
    )
```

```python
import jax
import jax.numpy as jnp
from jax import lax
from jax.experimental import pallas as pl
from jax.experimental.pallas import tpu as pltpu
from jax.sharding import PartitionSpec as P

beta_one = 0.9
beta_two = 0.999
learn_rate = 0.001
decay_rate = 0.01
adam_eps = 1e-08
adapter_scale_factor = 2.0
adam_step = 10.0

D = 4096
FF = 1536
TOP = 8
R = 32
J = 8
TOK = 128
COPIES = TOK * TOP
CAP = 10
NE = 16
ND = 8
ROWS = J * CAP
EARLY = 48
LATE = ROWS - EARLY
RJ = R * J
CH = 4
RC = R * CH
UNIT = 512
SHARE = 22528
PIECE = SHARE // 16
QUARTER = SHARE // 4
UNITS = QUARTER // UNIT
A_UNITS = D // UNIT
B_UNITS = FF // UNIT
SPLIT = 1792
SUBS = ((0, 768), (768, 640))

MESH = pl.DeviceIdType.MESH
BF = jnp.bfloat16
F32 = jnp.float32
I32 = jnp.int32


def iota(shape, dim):
    return lax.broadcasted_iota(I32, shape, dim)


def ones(mask):
    return mask.astype(F32).astype(BF)


def contract(lhs, rhs, i, k, precision=None):
    return lax.dot_general(lhs, rhs, (((i,), (k,)), ((), ())), preferred_element_type=F32, precision=precision)


def at(start, size, unit=None):
    return pl.ds(pl.multiple_of(start, unit or size), size)


def main_kernel(
    tok, up_hbm, gate_t, ids_t, homes_row, a_hbm, b_hbm, first_hbm, second_hbm, whole, first_out, second_out,
    gathered, cots, send, got_early, got_late, ids_all, a, b, a16, b16, pick, hot_early, hot_late, low, weights,
    low_early, low_late, back_early, back_late, grad_a, grad_b, row, wire, wire_got,
    first, second, rows_a, rows_b, param, moving, packed, landed,
    local, ids_send, ids_recv, cot_send, cot_recv, tok_send, tok_recv, sib_recv,
    grad_send, grad_recv, move_send, move_recv, all_send, all_recv,
):
    dp = lax.axis_index("dp")
    me = lax.axis_index("expert")
    x = me // 4
    yh = (me // 2) % 2
    core = me % 2
    dp_across = (dp + 4) % 8
    yl = dp // 4
    z = dp % 4

    def place(dy, dx, dc):
        return ((x + dx) % 4) * 4 + ((yh + dy) % 2) * 2 + (core + dc) % 2

    def device(dy, dx, dc):
        return (dp_across if dy else dp, place(dy, dx, dc))

    def copy_to(src, dst, send_sem, recv_sem, to):
        return pltpu.make_async_remote_copy(
            src_ref=src, dst_ref=dst, send_sem=send_sem, recv_sem=recv_sem, device_id=to, device_id_type=MESH
        )

    peers = [
        (1, 0, 0), (0, 2, 0), (0, 1, 0), (0, 3, 0), (1, 2, 0), (1, 0, 1), (0, 2, 1), (1, 1, 0),
        (0, 3, 1), (1, 2, 1), (1, 3, 0), (0, 1, 1), (1, 1, 1), (1, 3, 1), (0, 0, 1),
    ]
    groups = [((dp + step) % ND, me) for step in range(1, ND)]
    homes = [(dp, (me + step) % NE) for step in range(1, NE)]

    loads = [
        pltpu.make_async_copy(src, dst, local.at[number])
        for number, (src, dst) in enumerate([
            (tok, gathered.at[at(me * TOK, TOK)]), (up_hbm, cots), (a_hbm, a), (b_hbm, b), (first_hbm, first), (second_hbm, second),
        ])
    ]
    for load in loads:
        load.start()
    barrier = pltpu.get_barrier_semaphore()
    met = groups + homes + [device(*peer) for peer in peers if peer[0]]
    for peer in met:
        pl.semaphore_signal(barrier, inc=1, device_id=peer, device_id_type=MESH)
    pl.semaphore_wait(barrier, len(met))
    loads[0].wait()

    sent = []

    def block(dy, dx, dc, half, part):
        rows = place(dy, dx, dc) * TOK
        size = TOK
        if part is not None:
            rows = rows + part * (TOK // 2)
            size = TOK // 2
        cols = pl.ds(SPLIT, D - SPLIT) if half else pl.ds(0, SPLIT)
        return gathered.at[at(rows, size), cols]

    def push(src, half, part, to, sem):
        ref = block(*src, half, part)
        copy = copy_to(ref, ref, tok_send.at[len(sent)], sem, device(*to))
        copy.start()
        sent.append(copy)

    def slot(half, dy, dx, part):
        return tok_recv.at[((half * 2 + dy) * 4 + dx) * 2 + part]

    def sib_slot(half, dy, dx):
        return sib_recv.at[(half * 2 + dy) * 4 + dx]

    def arrive(half, dy, dx, part=None):
        ref = block(dy, dx, 0, half, part)
        copy_to(ref, ref, tok_send.at[0], slot(half, dy, dx, part or 0), device(0, 1, 0)).wait_recv()

    def to_sibling(half, dy, dx):
        push((dy, dx, 0), half, None, (0, 0, 1), sib_slot(half, dy, dx))

    def to_across(half, dx):
        push((0, dx, 0), half, None, (1, 0, 0), slot(half, 1, dx, 0))

    def to_right(half, dy, dx, part=None):
        push((dy, dx, 0), half, part, (0, 1, 0), slot(half, dy, (dx + 3) % 4, part or 0))

    def to_left(half, dy, dx, part=None):
        push((dy, dx, 0), half, part, (0, 3, 0), slot(half, dy, (dx + 1) % 4, part or 0))

    to_across(1, 0)
    to_right(0, 0, 0)
    to_left(0, 0, 0)
    to_across(0, 0)
    to_right(1, 0, 0)
    to_left(1, 0, 0)
    to_sibling(0, 0, 0)
    to_sibling(1, 0, 0)

    small = []
    mine = at(me * TOP, TOP)
    ids_all[mine, :] = ids_t[...]
    for number, peer in enumerate(peers):
        copy = copy_to(ids_all.at[mine], ids_all.at[mine], ids_send.at[number], ids_recv.at[me], device(*peer))
        copy.start()
        small.append(copy)

    owner_of = iota((TOK, COPIES), 1) // TOP == iota((TOK, COPIES), 0)
    which = iota((TOP, COPIES), 1) % TOP == iota((TOP, COPIES), 0)
    spread = jnp.dot(ids_t[...].astype(F32).astype(BF), ones(owner_of), preferred_element_type=F32)
    ids_flat = jnp.sum(jnp.where(which, spread, 0.0), axis=0, keepdims=True).astype(I32)
    before = ones(iota((TOK, TOK), 0) < iota((TOK, TOK), 1))
    experts = iota((TOK, TOK), 0)
    total = jnp.zeros((TOK, 1), F32)
    for part in range(TOP):
        hit = ids_flat[:, part * TOK:(part + 1) * TOK] == experts
        value = hit.astype(F32)
        count = jnp.dot(value.astype(BF), before, preferred_element_type=F32) + total
        total = total + jnp.sum(value, axis=1, keepdims=True)
        row[:, part * TOK:(part + 1) * TOK] = jnp.sum(
            jnp.where(hit, count + (CAP * experts).astype(F32), 0.0), axis=0, keepdims=True
        ).astype(I32)

    loads[1].wait()

    @pl.loop(0, TOP)
    def _(part):
        rows = at(part * TOK, TOK)
        mine_of = (iota((TOK, TOK), 0) + part * TOK) // TOP == iota((TOK, TOK), 1)
        scale = contract(mine_of.astype(F32), gate_t[...], 1, 1, lax.Precision.HIGHEST)
        scale = jnp.sum(jnp.where(iota((TOK, TOP), 0) % TOP == iota((TOK, TOP), 1), scale, 0.0), axis=1, keepdims=True)
        cots[rows, :] = (scale * cots[rows, :].astype(F32)).astype(BF)

    for dx in (2, 1, 3, 0):
        base = ((x + dx) % 4) * (4 * ROWS)
        pick[...] = ones(iota((4 * ROWS, COPIES), 0) + base == row[...])

        @pl.loop(0, FF // UNIT)
        def _(part):
            cols = at(part * UNIT, UNIT)
            send[at(base, 4 * ROWS), cols] = jnp.dot(pick[...], cots[:, cols], preferred_element_type=F32).astype(BF)

    cot_sent = []

    def send_cots(low_row, high_row, got, index):
        size = high_row - low_row
        for part in range(size // 16):
            for peer in peers:
                copy = copy_to(
                    send.at[at(place(*peer) * ROWS + low_row + part * 16, 16)], got.at[at(me * size + part * 16, 16)],
                    cot_send.at[len(cot_sent)], cot_recv.at[index * NE + me], device(*peer),
                )
                copy.start()
                cot_sent.append(copy)
        got[at(me * size, size, 16), :] = send[at(me * ROWS + low_row, size, 16), :]

    def wait_cots(size, got, index):
        for peer in peers:
            ref = got.at[at(place(*peer) * size, size, 16)]
            copy_to(ref, ref, cot_send.at[0], cot_recv.at[index * NE + place(*peer)], device(*peer)).wait_recv()

    send_cots(0, EARLY, got_early, 0)

    arrive(1, 1, 0)
    to_right(1, 1, 0)
    to_left(1, 1, 0)
    to_sibling(1, 1, 0)
    arrive(0, 0, 3)
    to_right(0, 0, 3, 0)
    to_across(0, 3)
    to_sibling(0, 0, 3)
    arrive(0, 0, 1)
    to_left(0, 0, 1, 1)
    to_across(0, 1)
    to_sibling(0, 0, 1)

    index = iota((RJ, RJ), 0)
    turn = ones(iota((RJ, RJ), 1) == (index // RC * CH + index % CH) * R + (index % RC) // CH)
    loads[2].wait()
    loads[3].wait()

    @pl.loop(0, A_UNITS)
    def _(part):
        cols = at(part * UNIT, UNIT)
        a16[:, cols] = jnp.dot(turn, a[:, cols].astype(BF), preferred_element_type=F32).astype(BF)

    @pl.loop(0, B_UNITS)
    def _(part):
        cols = at(part * UNIT, UNIT)
        b16[:, cols] = jnp.dot(turn, b[:, cols].astype(BF), preferred_element_type=F32).astype(BF)

    arrive(0, 1, 0)
    to_sibling(0, 1, 0)
    arrive(1, 0, 3)
    to_right(1, 0, 3, 0)
    to_sibling(1, 0, 3)
    arrive(1, 0, 1)
    to_left(1, 0, 1, 1)
    to_sibling(1, 0, 1)

    for peer in peers:
        ref = ids_all.at[at(place(*peer) * TOP, TOP)]
        copy_to(ref, ref, ids_send.at[0], ids_recv.at[place(*peer)], device(*peer)).wait_recv()
    repeat = ones(iota((ROWS, J), 0) // CAP == iota((ROWS, J), 1))
    turn_in = (iota((ROWS, TOK), 0) % CAP).astype(F32)

    @pl.loop(0, NE, unroll=4)
    def _(source):
        ids = ids_all[at(source * TOP, TOP), :]
        hit = jnp.zeros((J, TOK), F32)
        for k in range(TOP):
            hit = hit + jnp.where(ids[k:k + 1, :] == iota((J, TOK), 0) + me * J, 1.0, 0.0)
        count = jnp.dot(hit.astype(BF), before, preferred_element_type=F32)
        value = jnp.where(hit > 0.5, count, -1.0)
        hot = ones(jnp.dot(repeat, value.astype(BF), preferred_element_type=F32) == turn_in)
        hot_early[at(source * EARLY, EARLY), :] = hot[:EARLY]
        hot_late[at(source * LATE, LATE), :] = hot[EARLY:]

    def own(size, base, columns, first_column):
        line = iota((size, columns), 0) + base
        column = iota((size, columns), 1) + first_column
        return line // CAP == column // RC * CH + column % CH

    def from_sibling(dx):
        for half in range(2):
            for dy in range(2):
                ref = block(dy, dx, 1, half, None)
                copy_to(ref, ref, tok_send.at[0], sib_slot(half, dy, dx), device(0, 0, 1)).wait_recv()

    def hidden(dx):
        from_sibling(dx)
        base = (x + dx) % 4
        rows = at(base * 4 * TOK, 4 * TOK)
        low[...] = contract(gathered[rows, :], a16[...], 1, 1).astype(BF)
        for hots, lows, size, first_row in ((hot_early, low_early, EARLY, 0), (hot_late, low_late, LATE, EARLY)):
            mask = own(size, first_row, RJ, 0)
            for inside in range(4):
                rows = at((base * 4 + inside) * size, size, 16)
                value = jnp.dot(hots[rows, :], low[inside * TOK:(inside + 1) * TOK, :], preferred_element_type=F32)
                lows[rows, :] = jnp.where(mask, value, 0.0).astype(BF)

    arrive(0, 0, 2, 0)
    arrive(0, 0, 2, 1)
    to_across(0, 2)
    to_sibling(0, 0, 2)
    arrive(1, 1, 3)
    to_right(1, 1, 3, 0)
    to_sibling(1, 1, 3)
    arrive(1, 1, 1)
    to_left(1, 1, 1, 1)
    to_sibling(1, 1, 1)
    hidden(0)
    arrive(0, 1, 3)
    to_sibling(0, 1, 3)
    arrive(0, 1, 1)
    to_sibling(0, 1, 1)
    arrive(1, 0, 2, 0)
    arrive(1, 0, 2, 1)
    to_sibling(1, 0, 2)
    send_cots(EARLY, ROWS, got_late, 1)
    hidden(3)
    hidden(1)
    arrive(1, 1, 2, 0)
    arrive(1, 1, 2, 1)
    to_sibling(1, 1, 2)
    arrive(0, 1, 2)
    to_sibling(0, 1, 2)
    hidden(2)

    def backward(got, back, size, base, first_column):
        columns = RJ - first_column
        mask = jnp.concatenate([own(size, base, columns, first_column)] * 4, axis=0)

        @pl.loop(0, 4)
        def _(part):
            rows = at(part * (4 * size), 4 * size)
            value = contract(got[rows, :], b16[first_column:, :], 1, 1)
            back[rows, first_column:] = jnp.where(mask, value, 0.0).astype(BF)

    def grad_flat(number, size):
        parts = []
        while size:
            if number < R * D:
                ref, (r, column), width = grad_a, divmod(number, D), D
            else:
                ref, (r, column), width = grad_b, divmod(number - R * D, FF), FF
            step = min(size, width - column)
            parts.append(ref[r * CH:(r + 1) * CH, column:column + step])
            number += step
            size -= step
        return parts[0] if len(parts) == 1 else jnp.concatenate(parts, axis=1)

    grad_sent = []

    def send_grads(chunk, cols, index):
        for step in (4, 1, 7, 3, 5, 2, 6):
            to = groups[step - 1]
            copy = copy_to(
                wire.at[chunk, at(to[0] * 16, 16), cols], wire_got.at[chunk, at(dp * 16, 16), cols],
                grad_send.at[index * ND + step], grad_recv.at[index * ND + dp], to,
            )
            copy.start()
            grad_sent.append(copy)
        wire_got[chunk, at(dp * 16, 16), cols] = wire[chunk, at(dp * 16, 16), cols]

    def wait_grads(chunk, cols, index):
        for step in range(1, ND):
            source = (dp + step) % ND
            ref = wire_got.at[chunk, at(source * 16, 16), cols]
            copy_to(ref, ref, grad_send.at[0], grad_recv.at[index * ND + source], groups[step - 1]).wait_recv()

    def wire_cols(sub):
        return pl.ds(4 * SUBS[sub][0], 4 * SUBS[sub][1])

    def gradients(chunk):
        chunk_cols = slice(chunk * RC, (chunk + 1) * RC)
        if chunk:
            backward(got_late, back_late, LATE, EARLY, RC)
        else:
            backward(got_early, back_early, EARLY, 0, 0)

        @pl.loop(0, NE, unroll=8)
        def _(source):
            rows = at(source * EARLY, EARLY)
            value = contract(back_early[rows, chunk_cols], hot_early[rows, :], 0, 0)
            if chunk:
                rows = at(source * LATE, LATE)
                value = value + contract(back_late[rows, chunk_cols], hot_late[rows, :], 0, 0)
            weights[:, at(source * TOK, TOK)] = value.astype(BF)

        @pl.loop(0, D // 1024)
        def _(part):
            cols = at(part * 1024, 1024)
            grad_a[:, cols] = jnp.dot(weights[...], gathered[:, cols], preferred_element_type=F32)

        @pl.loop(0, B_UNITS)
        def _(part):
            cols = at(part * UNIT, UNIT)
            value = contract(low_early[:, chunk_cols], got_early[:, cols], 0, 0)
            if chunk:
                value = value + contract(low_late[:, chunk_cols], got_late[:, cols], 0, 0)
            grad_b[:, cols] = value

        for sub, (offset, size) in enumerate(SUBS):
            for share in range(ND):
                for part in range(4):
                    base = share * SHARE + part * PIECE + offset
                    value = jnp.concatenate([grad_flat(base + quarter * QUARTER, size) for quarter in range(4)], axis=0)
                    col = 4 * offset + part * size
                    wire[chunk, share * 16:(share + 1) * 16, col:col + size] = value.astype(BF)
            if chunk:
                send_grads(1, wire_cols(sub), 1 + sub)
        if not chunk:
            send_grads(0, pl.ds(0, QUARTER), 0)

    wait_cots(EARLY, got_early, 0)
    gradients(0)

    exact = lax.Precision.HIGHEST
    start = 4 * UNITS * dp
    a_first = jnp.minimum(start // A_UNITS, R - 8)
    b_first = jnp.clip((start - A_UNITS * R) // B_UNITS, 0, R - 16)

    def chooser(count, base):
        index = iota((count * J, RJ), 0)
        return (iota((count * J, RJ), 1) == (index % J) * R + index // J + base).astype(F32)

    @pl.loop(0, A_UNITS)
    def _(part):
        cols = at(part * UNIT, UNIT)
        rows_a[:, cols] = jnp.dot(chooser(8, a_first), a[:, cols], preferred_element_type=F32, precision=exact)

    @pl.loop(0, B_UNITS)
    def _(part):
        cols = at(part * UNIT, UNIT)
        rows_b[:, cols] = jnp.dot(chooser(16, b_first), b[:, cols], preferred_element_type=F32, precision=exact)

    @pl.loop(0, 4 * UNITS)
    def _(column):
        number = start + column
        in_a = jnp.clip(number // A_UNITS - a_first, 0, 7)
        number_b = jnp.maximum(number - A_UNITS * R, 0)
        in_b = jnp.clip(number_b // B_UNITS - b_first, 0, 15)
        value_a = rows_a[at(in_a * J, J), at(number % A_UNITS * UNIT, UNIT)]
        value_b = rows_b[at(in_b * J, J), at(number_b % B_UNITS * UNIT, UNIT)]
        param[:, at(column * UNIT, UNIT)] = jnp.where(number < A_UNITS * R, value_a, value_b)

    homes_now = homes_row[...].astype(F32).astype(BF)
    lane = iota((128, 128), 1)
    line = iota((128, 128), 0)
    dest = jnp.dot(homes_now, ones(line == me * J + lane % J), preferred_element_type=F32).astype(I32)
    named = ones(homes_row[...] == me * J + line % J)
    owner = contract(ones(iota((1, 128), 1) >= 0) * iota((1, 128), 1).astype(F32).astype(BF), named, 1, 1).astype(I32)
    stay = ones((line // J == lane // J) & (line % J == owner % J) & (owner // J == me))
    lane = iota((256, 128), 1)
    line = iota((256, 128), 0)
    same = (line % 16 == lane // J) & (line // 16 != me)
    leave = ones(same & (line // 16 == dest // J))
    enter = ones(same & (line // 16 == owner // J))

    wait_cots(LATE, got_late, 1)
    gradients(1)

    loads[4].wait()
    loads[5].wait()
    fix_one = 1.0 - beta_one**adam_step
    fix_two = 1.0 - beta_two**adam_step

    def update(sub):
        offset, size = SUBS[sub]
        for part in range(4):
            inside = pl.ds(4 * offset + part * size, size)
            totals = []
            for chunk in range(2):
                grad = wire_got[chunk, 0:16, inside].astype(F32)
                for source in range(1, ND):
                    grad = grad + wire_got[chunk, source * 16:(source + 1) * 16, inside].astype(F32)
                totals.append(adapter_scale_factor * grad)
            for quarter in range(4):
                piece = quarter * 4 + part
                cols = pl.ds(piece * PIECE + offset, size)
                grad = jnp.concatenate([total[quarter * CH:(quarter + 1) * CH] for total in totals], axis=0)
                one = beta_one * first[:, cols] + (1.0 - beta_one) * grad
                two = beta_two * second[:, cols] + (1.0 - beta_two) * grad * grad
                old = param[:, cols]
                new = old - learn_rate * (one / fix_one / (jnp.sqrt(two / fix_two) + adam_eps) + decay_rate * old)
                for kind, value in enumerate((new, one, two)):
                    moving[kind, piece * J:(piece + 1) * J, pl.ds(offset, size)] = value.astype(BF)

    move_sent = []

    def move(kind, cols, index):
        packed[kind, :, cols] = jnp.dot(leave, moving[kind, :, cols], preferred_element_type=F32).astype(BF)
        landed[kind, at(me * 16, 16), cols] = jnp.zeros((16, cols.size), BF)
        for step in (8, 9, 10, 11, 7, 6, 5, 4, 12, 13, 14, 15, 3, 2, 1):
            to = homes[step - 1]
            copy = copy_to(
                packed.at[kind, at(to[1] * 16, 16), cols], landed.at[kind, at(me * 16, 16), cols],
                move_send.at[index * NE + step], move_recv.at[index * NE + me], to,
            )
            copy.start()
            move_sent.append(copy)

    def arrived(kind, cols, index):
        for step in range(1, NE):
            source = (me + step) % NE
            ref = landed.at[kind, at(source * 16, 16), cols]
            copy_to(ref, ref, move_send.at[0], move_recv.at[index * NE + source], homes[step - 1]).wait_recv()
        return (contract(enter, landed[kind, :, cols], 0, 0) + contract(stay, moving[kind, :, cols], 0, 0)).astype(BF)

    all_sent = []

    def group(dy, dz):
        return ((yl + dy) % 2) * 4 + (z + dz) % 4

    def part_of(dy, dz, sub, half):
        rows = at(group(dy, dz) * 128, 128) if half is None else at(group(dy, dz) * 128 + half * 64, 64)
        return whole.at[rows, pl.ds(*SUBS[sub])]

    def share_slot(dy, dz, sub, half):
        return all_recv.at[((sub * 2 + dy) * 4 + dz) * 2 + (half or 0)]

    def pass_on(dy, dz, sub, to_y, to_z, half=None):
        ref = part_of(dy, dz, sub, half)
        copy = copy_to(
            ref, ref, all_send.at[len(all_sent)], share_slot((dy + to_y) % 2, (dz - to_z) % 4, sub, half), (group(to_y, to_z), me)
        )
        copy.start()
        all_sent.append(copy)

    def came(dy, dz, sub, half=None):
        ref = part_of(dy, dz, sub, half)
        copy_to(ref, ref, all_send.at[0], share_slot(dy, dz, sub, half), groups[0]).wait_recv()

    wait_grads(0, pl.ds(0, QUARTER), 0)
    for sub in range(2):
        wait_grads(1, wire_cols(sub), 1 + sub)
        update(sub)
        move(0, pl.ds(*SUBS[sub]), sub)
    for sub in range(2):
        cols = pl.ds(*SUBS[sub])
        whole[at(dp * 128, 128), cols] = arrived(0, cols, sub)
        pass_on(0, 0, sub, 1, 0)
        pass_on(0, 0, sub, 0, 1)
        pass_on(0, 0, sub, 0, 3)
    full = pl.ds(0, PIECE)
    move(1, full, 2)
    move(2, full, 3)
    for sub in range(2):
        came(1, 0, sub)
        pass_on(1, 0, sub, 0, 1)
        pass_on(1, 0, sub, 0, 3)
        came(0, 3, sub)
        pass_on(0, 3, sub, 0, 1, 0)
        came(0, 1, sub)
        pass_on(0, 1, sub, 0, 3, 1)
    for sub in range(2):
        came(1, 3, sub)
        pass_on(1, 3, sub, 0, 1, 0)
        came(1, 1, sub)
        pass_on(1, 1, sub, 0, 3, 1)
    first_out[...] = arrived(1, full, 2)
    second_out[...] = arrived(2, full, 3)
    for sub in range(2):
        for half in range(2):
            came(0, 2, sub, half)
            came(1, 2, sub, half)
    for copy in sent + small + cot_sent + grad_sent + move_sent + all_sent:
        copy.wait_send()


def finish_kernel(whole, first, second, new_a, new_b, new_first, new_second):
    index = iota((RJ, RJ), 0)
    turn = ones(iota((RJ, RJ), 1) == index % R * J + index // R)

    def unit(number):
        share, inside = divmod(number * UNIT, SHARE)
        parts = []
        left = UNIT
        while left:
            piece, offset = divmod(inside, PIECE)
            size = min(left, PIECE - offset)
            line = share * 128 + piece * J
            pair = whole[line // 16 * 16:line // 16 * 16 + 16, offset:offset + size].astype(F32)
            parts.append(pair[line % 16:line % 16 + J])
            left -= size
            inside += size
        return parts[0] if len(parts) == 1 else jnp.concatenate(parts, axis=1)

    for out, columns, base in ((new_a, A_UNITS, 0), (new_b, B_UNITS, A_UNITS * R)):
        for column in range(columns):
            stack = jnp.concatenate([unit(base + r * columns + column) for r in range(R)], axis=0).astype(BF)
            out[:, column * UNIT:(column + 1) * UNIT] = jnp.dot(turn, stack, preferred_element_type=F32)
    for out, value in ((new_first, first), (new_second, second)):
        for pair in range(8):
            both = value[pair * 16:(pair + 1) * 16, :].astype(F32)
            out[:, 2 * pair * PIECE:(2 * pair + 1) * PIECE] = both[:J]
            out[:, (2 * pair + 1) * PIECE:(2 * pair + 2) * PIECE] = both[J:]


def vmem(count):
    return [pl.BlockSpec(memory_space=pltpu.VMEM)] * count


def anywhere(count):
    return [pl.BlockSpec(memory_space=pl.ANY)] * count


def shards(tokens, up_grad, gate_weights, expert_ids, new_home, adapter_a, adapter_b, first_moment, second_moment):
    dma = pltpu.SemaphoreType.DMA
    whole, first, second = pl.pallas_call(
        main_kernel,
        out_shape=[
            jax.ShapeDtypeStruct((ND * 128, PIECE), BF),
            jax.ShapeDtypeStruct((128, PIECE), BF),
            jax.ShapeDtypeStruct((128, PIECE), BF),
        ],
        in_specs=anywhere(2) + vmem(3) + anywhere(4),
        out_specs=vmem(3),
        scratch_shapes=[
            pltpu.VMEM((NE * TOK, D), BF),
            pltpu.VMEM((COPIES, FF), BF),
            pltpu.VMEM((NE * ROWS, FF), BF),
            pltpu.VMEM((NE * EARLY, FF), BF),
            pltpu.VMEM((NE * LATE, FF), BF),
            pltpu.VMEM((NE * TOP, TOK), I32),
            pltpu.VMEM((RJ, D), F32),
            pltpu.VMEM((RJ, FF), F32),
            pltpu.VMEM((RJ, D), BF),
            pltpu.VMEM((RJ, FF), BF),
            pltpu.VMEM((4 * ROWS, COPIES), BF),
            pltpu.VMEM((NE * EARLY, TOK), BF),
            pltpu.VMEM((NE * LATE, TOK), BF),
            pltpu.VMEM((4 * TOK, RJ), BF),
            pltpu.VMEM((RC, NE * TOK), BF),
            pltpu.VMEM((NE * EARLY, RJ), BF),
            pltpu.VMEM((NE * LATE, RJ), BF),
            pltpu.VMEM((NE * EARLY, RJ), BF),
            pltpu.VMEM((NE * LATE, RJ), BF),
            pltpu.VMEM((RC, D), F32),
            pltpu.VMEM((RC, FF), F32),
            pltpu.VMEM((1, COPIES), I32),
            pltpu.VMEM((2, ND * 16, QUARTER), BF),
            pltpu.VMEM((2, ND * 16, QUARTER), BF),
            pltpu.VMEM((J, SHARE), F32),
            pltpu.VMEM((J, SHARE), F32),
            pltpu.VMEM((8 * J, D), F32),
            pltpu.VMEM((16 * J, FF), F32),
            pltpu.VMEM((J, SHARE), F32),
            pltpu.VMEM((3, 128, PIECE), BF),
            pltpu.VMEM((3, 256, PIECE), BF),
            pltpu.VMEM((3, 256, PIECE), BF),
            dma((6,)),
            dma((NE,)),
            dma((NE,)),
            dma((NE * 5,)),
            dma((2 * NE,)),
            dma((64,)),
            dma((32,)),
            dma((16,)),
            dma((3 * ND,)),
            dma((3 * ND,)),
            dma((4 * NE,)),
            dma((4 * NE,)),
            dma((32,)),
            dma((32,)),
        ],
        compiler_params=pltpu.CompilerParams(collective_id=0, has_side_effects=True, vmem_limit_bytes=63 * 2**20),
        name="dispatch_update",
    )(
        tokens, up_grad.reshape(COPIES, FF), gate_weights.T, expert_ids.T, new_home.reshape(1, NE * J),
        adapter_a.reshape(RJ, D), adapter_b.reshape(RJ, FF), first_moment, second_moment,
    )
    new_a, new_b, new_first, new_second = pl.pallas_call(
        finish_kernel,
        out_shape=[
            jax.ShapeDtypeStruct((RJ, D), F32),
            jax.ShapeDtypeStruct((RJ, FF), F32),
            jax.ShapeDtypeStruct((J, SHARE), F32),
            jax.ShapeDtypeStruct((J, SHARE), F32),
        ],
        in_specs=vmem(3),
        out_specs=vmem(4),
        compiler_params=pltpu.CompilerParams(vmem_limit_bytes=60 * 2**20),
        name="finish",
    )(whole, first, second)
    return new_a.reshape(J, R, D), new_b.reshape(J, R, FF), new_first, new_second


def solution(mesh):
    placed = (
        P(("dp", "expert"), None),
        P(("dp", "expert"), None, None),
        P(("dp", "expert"), None),
        P(("dp", "expert"), None),
        P(),
        P("expert", None, None),
        P("expert", None, None),
        P("expert", "dp"),
        P("expert", "dp"),
    )
    return jax.shard_map(
        shards,
        mesh=mesh,
        in_specs=placed,
        out_specs=(P("expert", None, None), P("expert", None, None), P("expert", "dp"), P("expert", "dp")),
        check_vma=False,
    )
```

```python
import jax
import jax.numpy as jnp
from jax import lax
from jax.experimental import pallas as pl
from jax.experimental.pallas import tpu as pltpu
from jax.sharding import PartitionSpec as P

beta_one = 0.9
beta_two = 0.999
learn_rate = 0.001
decay_rate = 0.01
adam_eps = 1e-08
adapter_scale_factor = 2.0
adam_step = 10.0

D = 4096
FF = 1536
TOP = 8
R = 32
J = 8
TOK = 128
COPIES = TOK * TOP
CAP = 10
NE = 16
ND = 8
ROWS = J * CAP
EARLY = 48
LATE = ROWS - EARLY
RJ = R * J
CH = 4
RC = R * CH
UNIT = 512
SHARE = 22528
PIECE = SHARE // 16
QUARTER = SHARE // 4
UNITS = QUARTER // UNIT
A_UNITS = D // UNIT
B_UNITS = FF // UNIT
SPLIT = 1792
SUBS = ((0, 768), (768, 640))

MESH = pl.DeviceIdType.MESH
BF = jnp.bfloat16
F32 = jnp.float32
I32 = jnp.int32


def iota(shape, dim):
    return lax.broadcasted_iota(I32, shape, dim)


def ones(mask):
    return mask.astype(F32).astype(BF)


def contract(lhs, rhs, i, k, precision=None):
    return lax.dot_general(lhs, rhs, (((i,), (k,)), ((), ())), preferred_element_type=F32, precision=precision)


def at(start, size, unit=None):
    return pl.ds(pl.multiple_of(start, unit or size), size)


def main_kernel(
    tok, up_hbm, gate_t, ids_t, homes_row, a_hbm, b_hbm, first_hbm, second_hbm, whole, first_out, second_out,
    gathered, cots, send, got_early, got_late, ids_all, a, b, a16, b16, pick, hot_early, hot_late, low, weights,
    low_early, low_late, back_early, back_late, grad_a, grad_b, row, wire, wire_got,
    first, second, rows_a, rows_b, param, moving, packed, landed,
    local, ids_send, ids_recv, cot_send, cot_recv, tok_send, tok_recv, sib_recv,
    grad_send, grad_recv, move_send, move_recv, all_send, all_recv,
):
    dp = lax.axis_index("dp")
    me = lax.axis_index("expert")
    x = me // 4
    yh = (me // 2) % 2
    core = me % 2
    dp_across = (dp + 4) % 8
    yl = dp // 4
    z = dp % 4

    def place(dy, dx, dc):
        return ((x + dx) % 4) * 4 + ((yh + dy) % 2) * 2 + (core + dc) % 2

    def device(dy, dx, dc):
        return (dp_across if dy else dp, place(dy, dx, dc))

    def copy_to(src, dst, send_sem, recv_sem, to):
        return pltpu.make_async_remote_copy(
            src_ref=src, dst_ref=dst, send_sem=send_sem, recv_sem=recv_sem, device_id=to, device_id_type=MESH
        )

    peers = [
        (1, 0, 0), (0, 2, 0), (0, 1, 0), (0, 3, 0), (1, 2, 0), (1, 0, 1), (0, 2, 1), (1, 1, 0),
        (0, 3, 1), (1, 2, 1), (1, 3, 0), (0, 1, 1), (1, 1, 1), (1, 3, 1), (0, 0, 1),
    ]
    groups = [((dp + step) % ND, me) for step in range(1, ND)]
    homes = [(dp, (me + step) % NE) for step in range(1, NE)]

    loads = [
        pltpu.make_async_copy(src, dst, local.at[number])
        for number, (src, dst) in enumerate([
            (tok, gathered.at[at(me * TOK, TOK)]), (up_hbm, cots), (a_hbm, a), (b_hbm, b), (first_hbm, first), (second_hbm, second),
        ])
    ]
    for load in loads:
        load.start()
    barrier = pltpu.get_barrier_semaphore()
    met = groups + homes + [device(*peer) for peer in peers if peer[0]]
    for peer in met:
        pl.semaphore_signal(barrier, inc=1, device_id=peer, device_id_type=MESH)
    pl.semaphore_wait(barrier, len(met))
    loads[0].wait()

    sent = []

    def block(dy, dx, dc, half, part):
        rows = place(dy, dx, dc) * TOK
        size = TOK
        if part is not None:
            rows = rows + part * (TOK // 2)
            size = TOK // 2
        cols = pl.ds(SPLIT, D - SPLIT) if half else pl.ds(0, SPLIT)
        return gathered.at[at(rows, size), cols]

    def push(src, half, part, to, sem):
        ref = block(*src, half, part)
        copy = copy_to(ref, ref, tok_send.at[len(sent)], sem, device(*to))
        copy.start()
        sent.append(copy)

    def slot(half, dy, dx, part):
        return tok_recv.at[((half * 2 + dy) * 4 + dx) * 2 + part]

    def sib_slot(half, dy, dx):
        return sib_recv.at[(half * 2 + dy) * 4 + dx]

    def arrive(half, dy, dx, part=None):
        ref = block(dy, dx, 0, half, part)
        copy_to(ref, ref, tok_send.at[0], slot(half, dy, dx, part or 0), device(0, 1, 0)).wait_recv()

    def to_sibling(half, dy, dx):
        push((dy, dx, 0), half, None, (0, 0, 1), sib_slot(half, dy, dx))

    def to_across(half, dx):
        push((0, dx, 0), half, None, (1, 0, 0), slot(half, 1, dx, 0))

    def to_right(half, dy, dx, part=None):
        push((dy, dx, 0), half, part, (0, 1, 0), slot(half, dy, (dx + 3) % 4, part or 0))

    def to_left(half, dy, dx, part=None):
        push((dy, dx, 0), half, part, (0, 3, 0), slot(half, dy, (dx + 1) % 4, part or 0))

    to_across(1, 0)
    to_right(0, 0, 0)
    to_left(0, 0, 0)
    to_across(0, 0)
    to_right(1, 0, 0)
    to_left(1, 0, 0)
    to_sibling(0, 0, 0)
    to_sibling(1, 0, 0)

    small = []
    mine = at(me * TOP, TOP)
    ids_all[mine, :] = ids_t[...]
    for number, peer in enumerate(peers):
        copy = copy_to(ids_all.at[mine], ids_all.at[mine], ids_send.at[number], ids_recv.at[me], device(*peer))
        copy.start()
        small.append(copy)

    owner_of = iota((TOK, COPIES), 1) // TOP == iota((TOK, COPIES), 0)
    which = iota((TOP, COPIES), 1) % TOP == iota((TOP, COPIES), 0)
    spread = jnp.dot(ids_t[...].astype(F32).astype(BF), ones(owner_of), preferred_element_type=F32)
    ids_flat = jnp.sum(jnp.where(which, spread, 0.0), axis=0, keepdims=True).astype(I32)
    before = ones(iota((TOK, TOK), 0) < iota((TOK, TOK), 1))
    experts = iota((TOK, TOK), 0)
    total = jnp.zeros((TOK, 1), F32)
    for part in range(TOP):
        hit = ids_flat[:, part * TOK:(part + 1) * TOK] == experts
        value = hit.astype(F32)
        count = jnp.dot(value.astype(BF), before, preferred_element_type=F32) + total
        total = total + jnp.sum(value, axis=1, keepdims=True)
        row[:, part * TOK:(part + 1) * TOK] = jnp.sum(
            jnp.where(hit, count + (CAP * experts).astype(F32), 0.0), axis=0, keepdims=True
        ).astype(I32)

    loads[1].wait()

    @pl.loop(0, TOP)
    def _(part):
        rows = at(part * TOK, TOK)
        mine_of = (iota((TOK, TOK), 0) + part * TOK) // TOP == iota((TOK, TOK), 1)
        scale = contract(mine_of.astype(F32), gate_t[...], 1, 1, lax.Precision.HIGHEST)
        scale = jnp.sum(jnp.where(iota((TOK, TOP), 0) % TOP == iota((TOK, TOP), 1), scale, 0.0), axis=1, keepdims=True)
        cots[rows, :] = (scale * cots[rows, :].astype(F32)).astype(BF)

    for dx in (2, 1, 3, 0):
        base = ((x + dx) % 4) * (4 * ROWS)
        pick[...] = ones(iota((4 * ROWS, COPIES), 0) + base == row[...])

        @pl.loop(0, FF // UNIT)
        def _(part):
            cols = at(part * UNIT, UNIT)
            send[at(base, 4 * ROWS), cols] = jnp.dot(pick[...], cots[:, cols], preferred_element_type=F32).astype(BF)

    cot_sent = []

    def send_cots(low_row, high_row, got, index):
        size = high_row - low_row
        for part in range(size // 16):
            for peer in peers:
                copy = copy_to(
                    send.at[at(place(*peer) * ROWS + low_row + part * 16, 16)], got.at[at(me * size + part * 16, 16)],
                    cot_send.at[len(cot_sent)], cot_recv.at[index * NE + me], device(*peer),
                )
                copy.start()
                cot_sent.append(copy)
        got[at(me * size, size, 16), :] = send[at(me * ROWS + low_row, size, 16), :]

    def wait_cots(size, got, index):
        for peer in peers:
            ref = got.at[at(place(*peer) * size, size, 16)]
            copy_to(ref, ref, cot_send.at[0], cot_recv.at[index * NE + place(*peer)], device(*peer)).wait_recv()

    arrive(1, 1, 0)
    to_right(1, 1, 0)
    to_left(1, 1, 0)
    to_sibling(1, 1, 0)
    arrive(0, 0, 3)
    to_right(0, 0, 3, 0)
    to_across(0, 3)
    to_sibling(0, 0, 3)
    arrive(0, 0, 1)
    to_left(0, 0, 1, 1)
    to_across(0, 1)
    to_sibling(0, 0, 1)
    send_cots(0, EARLY, got_early, 0)

    index = iota((RJ, RJ), 0)
    turn = ones(iota((RJ, RJ), 1) == (index // RC * CH + index % CH) * R + (index % RC) // CH)
    loads[2].wait()
    loads[3].wait()

    @pl.loop(0, A_UNITS)
    def _(part):
        cols = at(part * UNIT, UNIT)
        a16[:, cols] = jnp.dot(turn, a[:, cols].astype(BF), preferred_element_type=F32).astype(BF)

    @pl.loop(0, B_UNITS)
    def _(part):
        cols = at(part * UNIT, UNIT)
        b16[:, cols] = jnp.dot(turn, b[:, cols].astype(BF), preferred_element_type=F32).astype(BF)

    arrive(0, 1, 0)
    to_sibling(0, 1, 0)
    arrive(1, 0, 3)
    to_right(1, 0, 3, 0)
    to_sibling(1, 0, 3)
    arrive(1, 0, 1)
    to_left(1, 0, 1, 1)
    to_sibling(1, 0, 1)

    def own(size, base, columns, first_column):
        line = iota((size, columns), 0) + base
        column = iota((size, columns), 1) + first_column
        return line // CAP == column // RC * CH + column % CH

    def from_sibling(dx):
        for half in range(2):
            for dy in range(2):
                ref = block(dy, dx, 1, half, None)
                copy_to(ref, ref, tok_send.at[0], sib_slot(half, dy, dx), device(0, 0, 1)).wait_recv()

    def hidden(dx):
        from_sibling(dx)
        base = (x + dx) % 4
        rows = at(base * 4 * TOK, 4 * TOK)
        low[...] = contract(gathered[rows, :], a16[...], 1, 1).astype(BF)
        for hots, lows, size, first_row in ((hot_early, low_early, EARLY, 0), (hot_late, low_late, LATE, EARLY)):
            mask = own(size, first_row, RJ, 0)
            for inside in range(4):
                rows = at((base * 4 + inside) * size, size, 16)
                value = jnp.dot(hots[rows, :], low[inside * TOK:(inside + 1) * TOK, :], preferred_element_type=F32)
                lows[rows, :] = jnp.where(mask, value, 0.0).astype(BF)

    arrive(0, 0, 2, 0)
    arrive(0, 0, 2, 1)
    to_across(0, 2)
    to_sibling(0, 0, 2)
    arrive(1, 1, 3)
    to_right(1, 1, 3, 0)
    to_sibling(1, 1, 3)
    arrive(1, 1, 1)
    to_left(1, 1, 1, 1)
    to_sibling(1, 1, 1)

    for peer in peers:
        ref = ids_all.at[at(place(*peer) * TOP, TOP)]
        copy_to(ref, ref, ids_send.at[0], ids_recv.at[place(*peer)], device(*peer)).wait_recv()
    repeat = ones(iota((ROWS, J), 0) // CAP == iota((ROWS, J), 1))
    turn_in = (iota((ROWS, TOK), 0) % CAP).astype(F32)

    @pl.loop(0, NE, unroll=4)
    def _(source):
        ids = ids_all[at(source * TOP, TOP), :]
        hit = jnp.zeros((J, TOK), F32)
        for k in range(TOP):
            hit = hit + jnp.where(ids[k:k + 1, :] == iota((J, TOK), 0) + me * J, 1.0, 0.0)
        count = jnp.dot(hit.astype(BF), before, preferred_element_type=F32)
        value = jnp.where(hit > 0.5, count, -1.0)
        hot = ones(jnp.dot(repeat, value.astype(BF), preferred_element_type=F32) == turn_in)
        hot_early[at(source * EARLY, EARLY), :] = hot[:EARLY]
        hot_late[at(source * LATE, LATE), :] = hot[EARLY:]

    hidden(0)
    arrive(0, 1, 3)
    to_sibling(0, 1, 3)
    arrive(0, 1, 1)
    to_sibling(0, 1, 1)
    arrive(1, 0, 2, 0)
    arrive(1, 0, 2, 1)
    to_sibling(1, 0, 2)
    send_cots(EARLY, ROWS, got_late, 1)
    hidden(3)
    hidden(1)
    arrive(1, 1, 2, 0)
    arrive(1, 1, 2, 1)
    to_sibling(1, 1, 2)
    arrive(0, 1, 2)
    to_sibling(0, 1, 2)

    def backward(got, back, size, base, first_column):
        columns = RJ - first_column
        mask = jnp.concatenate([own(size, base, columns, first_column)] * 4, axis=0)

        @pl.loop(0, 4)
        def _(part):
            rows = at(part * (4 * size), 4 * size)
            value = contract(got[rows, :], b16[first_column:, :], 1, 1)
            back[rows, first_column:] = jnp.where(mask, value, 0.0).astype(BF)

    def grad_flat(number, size):
        parts = []
        while size:
            if number < R * D:
                ref, (r, column), width = grad_a, divmod(number, D), D
            else:
                ref, (r, column), width = grad_b, divmod(number - R * D, FF), FF
            step = min(size, width - column)
            parts.append(ref[r * CH:(r + 1) * CH, column:column + step])
            number += step
            size -= step
        return parts[0] if len(parts) == 1 else jnp.concatenate(parts, axis=1)

    grad_sent = []

    def send_grads(chunk, cols, index):
        for step in (4, 1, 7, 3, 5, 2, 6):
            to = groups[step - 1]
            copy = copy_to(
                wire.at[chunk, at(to[0] * 16, 16), cols], wire_got.at[chunk, at(dp * 16, 16), cols],
                grad_send.at[index * ND + step], grad_recv.at[index * ND + dp], to,
            )
            copy.start()
            grad_sent.append(copy)
        wire_got[chunk, at(dp * 16, 16), cols] = wire[chunk, at(dp * 16, 16), cols]

    def wait_grads(chunk, cols, index):
        for step in range(1, ND):
            source = (dp + step) % ND
            ref = wire_got.at[chunk, at(source * 16, 16), cols]
            copy_to(ref, ref, grad_send.at[0], grad_recv.at[index * ND + source], groups[step - 1]).wait_recv()

    def wire_cols(sub):
        return pl.ds(4 * SUBS[sub][0], 4 * SUBS[sub][1])

    def gradients(chunk):
        chunk_cols = slice(chunk * RC, (chunk + 1) * RC)
        if chunk:
            wait_cots(LATE, got_late, 1)
            backward(got_late, back_late, LATE, EARLY, RC)
        else:
            wait_cots(EARLY, got_early, 0)
            backward(got_early, back_early, EARLY, 0, 0)

        @pl.loop(0, NE, unroll=8)
        def _(source):
            rows = at(source * EARLY, EARLY)
            value = contract(back_early[rows, chunk_cols], hot_early[rows, :], 0, 0)
            if chunk:
                rows = at(source * LATE, LATE)
                value = value + contract(back_late[rows, chunk_cols], hot_late[rows, :], 0, 0)
            weights[:, at(source * TOK, TOK)] = value.astype(BF)

        if not chunk:
            hidden(2)

        @pl.loop(0, D // 1024)
        def _(part):
            cols = at(part * 1024, 1024)
            grad_a[:, cols] = jnp.dot(weights[...], gathered[:, cols], preferred_element_type=F32)

        @pl.loop(0, B_UNITS)
        def _(part):
            cols = at(part * UNIT, UNIT)
            value = contract(low_early[:, chunk_cols], got_early[:, cols], 0, 0)
            if chunk:
                value = value + contract(low_late[:, chunk_cols], got_late[:, cols], 0, 0)
            grad_b[:, cols] = value

        for sub, (offset, size) in enumerate(SUBS):
            for share in range(ND):
                for part in range(4):
                    base = share * SHARE + part * PIECE + offset
                    value = jnp.concatenate([grad_flat(base + quarter * QUARTER, size) for quarter in range(4)], axis=0)
                    col = 4 * offset + part * size
                    wire[chunk, share * 16:(share + 1) * 16, col:col + size] = value.astype(BF)
            send_grads(chunk, wire_cols(sub), 2 * chunk + sub)

    gradients(0)
    gradients(1)

    exact = lax.Precision.HIGHEST
    start = 4 * UNITS * dp
    a_first = jnp.minimum(start // A_UNITS, R - 8)
    b_first = jnp.clip((start - A_UNITS * R) // B_UNITS, 0, R - 16)

    def chooser(count, base):
        index = iota((count * J, RJ), 0)
        return (iota((count * J, RJ), 1) == (index % J) * R + index // J + base).astype(F32)

    @pl.loop(0, A_UNITS)
    def _(part):
        cols = at(part * UNIT, UNIT)
        rows_a[:, cols] = jnp.dot(chooser(8, a_first), a[:, cols], preferred_element_type=F32, precision=exact)

    @pl.loop(0, B_UNITS)
    def _(part):
        cols = at(part * UNIT, UNIT)
        rows_b[:, cols] = jnp.dot(chooser(16, b_first), b[:, cols], preferred_element_type=F32, precision=exact)

    @pl.loop(0, 4 * UNITS)
    def _(column):
        number = start + column
        in_a = jnp.clip(number // A_UNITS - a_first, 0, 7)
        number_b = jnp.maximum(number - A_UNITS * R, 0)
        in_b = jnp.clip(number_b // B_UNITS - b_first, 0, 15)
        value_a = rows_a[at(in_a * J, J), at(number % A_UNITS * UNIT, UNIT)]
        value_b = rows_b[at(in_b * J, J), at(number_b % B_UNITS * UNIT, UNIT)]
        param[:, at(column * UNIT, UNIT)] = jnp.where(number < A_UNITS * R, value_a, value_b)

    homes_now = homes_row[...].astype(F32).astype(BF)
    lane = iota((128, 128), 1)
    line = iota((128, 128), 0)
    dest = jnp.dot(homes_now, ones(line == me * J + lane % J), preferred_element_type=F32).astype(I32)
    named = ones(homes_row[...] == me * J + line % J)
    owner = contract(ones(iota((1, 128), 1) >= 0) * iota((1, 128), 1).astype(F32).astype(BF), named, 1, 1).astype(I32)
    stay = ones((line // J == lane // J) & (line % J == owner % J) & (owner // J == me))
    lane = iota((256, 128), 1)
    line = iota((256, 128), 0)
    same = (line % 16 == lane // J) & (line // 16 != me)
    leave = ones(same & (line // 16 == dest // J))
    enter = ones(same & (line // 16 == owner // J))

    loads[4].wait()
    loads[5].wait()
    fix_one = 1.0 - beta_one**adam_step
    fix_two = 1.0 - beta_two**adam_step

    def update(sub):
        offset, size = SUBS[sub]
        for part in range(4):
            inside = pl.ds(4 * offset + part * size, size)
            totals = []
            for chunk in range(2):
                grad = wire_got[chunk, 0:16, inside].astype(F32)
                for source in range(1, ND):
                    grad = grad + wire_got[chunk, source * 16:(source + 1) * 16, inside].astype(F32)
                totals.append(adapter_scale_factor * grad)
            for quarter in range(4):
                piece = quarter * 4 + part
                cols = pl.ds(piece * PIECE + offset, size)
                grad = jnp.concatenate([total[quarter * CH:(quarter + 1) * CH] for total in totals], axis=0)
                one = beta_one * first[:, cols] + (1.0 - beta_one) * grad
                two = beta_two * second[:, cols] + (1.0 - beta_two) * grad * grad
                old = param[:, cols]
                new = old - learn_rate * (one / fix_one / (jnp.sqrt(two / fix_two) + adam_eps) + decay_rate * old)
                for kind, value in enumerate((new, one, two)):
                    moving[kind, piece * J:(piece + 1) * J, pl.ds(offset, size)] = value.astype(BF)

    move_sent = []

    def move(kind, cols, index):
        packed[kind, :, cols] = jnp.dot(leave, moving[kind, :, cols], preferred_element_type=F32).astype(BF)
        landed[kind, at(me * 16, 16), cols] = jnp.zeros((16, cols.size), BF)
        for step in (8, 9, 10, 11, 7, 6, 5, 4, 12, 13, 14, 15, 3, 2, 1):
            to = homes[step - 1]
            copy = copy_to(
                packed.at[kind, at(to[1] * 16, 16), cols], landed.at[kind, at(me * 16, 16), cols],
                move_send.at[index * NE + step], move_recv.at[index * NE + me], to,
            )
            copy.start()
            move_sent.append(copy)

    def arrived(kind, cols, index):
        for step in range(1, NE):
            source = (me + step) % NE
            ref = landed.at[kind, at(source * 16, 16), cols]
            copy_to(ref, ref, move_send.at[0], move_recv.at[index * NE + source], homes[step - 1]).wait_recv()
        return (contract(enter, landed[kind, :, cols], 0, 0) + contract(stay, moving[kind, :, cols], 0, 0)).astype(BF)

    all_sent = []

    def group(dy, dz):
        return ((yl + dy) % 2) * 4 + (z + dz) % 4

    def part_of(dy, dz, sub, half):
        rows = at(group(dy, dz) * 128, 128) if half is None else at(group(dy, dz) * 128 + half * 64, 64)
        return whole.at[rows, pl.ds(*SUBS[sub])]

    def share_slot(dy, dz, sub, half):
        return all_recv.at[((sub * 2 + dy) * 4 + dz) * 2 + (half or 0)]

    def pass_on(dy, dz, sub, to_y, to_z, half=None):
        ref = part_of(dy, dz, sub, half)
        copy = copy_to(
            ref, ref, all_send.at[len(all_sent)], share_slot((dy + to_y) % 2, (dz - to_z) % 4, sub, half), (group(to_y, to_z), me)
        )
        copy.start()
        all_sent.append(copy)

    def came(dy, dz, sub, half=None):
        ref = part_of(dy, dz, sub, half)
        copy_to(ref, ref, all_send.at[0], share_slot(dy, dz, sub, half), groups[0]).wait_recv()

    for sub in range(2):
        for chunk in range(2):
            wait_grads(chunk, wire_cols(sub), 2 * chunk + sub)
        update(sub)
        move(0, pl.ds(*SUBS[sub]), sub)
    for sub in range(2):
        cols = pl.ds(*SUBS[sub])
        whole[at(dp * 128, 128), cols] = arrived(0, cols, sub)
        pass_on(0, 0, sub, 1, 0)
        pass_on(0, 0, sub, 0, 1)
        pass_on(0, 0, sub, 0, 3)
    full = pl.ds(0, PIECE)
    move(1, full, 2)
    move(2, full, 3)
    for sub in range(2):
        came(1, 0, sub)
        pass_on(1, 0, sub, 0, 1)
        pass_on(1, 0, sub, 0, 3)
        came(0, 3, sub)
        pass_on(0, 3, sub, 0, 1, 0)
        came(0, 1, sub)
        pass_on(0, 1, sub, 0, 3, 1)
    for sub in range(2):
        came(1, 3, sub)
        pass_on(1, 3, sub, 0, 1, 0)
        came(1, 1, sub)
        pass_on(1, 1, sub, 0, 3, 1)
    first_out[...] = arrived(1, full, 2)
    second_out[...] = arrived(2, full, 3)
    for sub in range(2):
        for half in range(2):
            came(0, 2, sub, half)
            came(1, 2, sub, half)
    for copy in sent + small + cot_sent + grad_sent + move_sent + all_sent:
        copy.wait_send()


def finish_kernel(whole, first, second, out_a, out_b, out_first, out_second, new_a, new_b, new_first, new_second, sems):
    index = iota((RJ, RJ), 0)
    turn = ones(iota((RJ, RJ), 1) == index % R * J + index // R)

    def unit(number):
        share, inside = divmod(number * UNIT, SHARE)
        parts = []
        left = UNIT
        while left:
            piece, offset = divmod(inside, PIECE)
            size = min(left, PIECE - offset)
            line = share * 128 + piece * J
            pair = whole[line // 16 * 16:line // 16 * 16 + 16, offset:offset + size].astype(F32)
            parts.append(pair[line % 16:line % 16 + J])
            left -= size
            inside += size
        return parts[0] if len(parts) == 1 else jnp.concatenate(parts, axis=1)

    copies = []

    def write(src, dst):
        copy = pltpu.make_async_copy(src, dst, sems.at[len(copies)])
        copy.start()
        copies.append(copy)

    for kept, out, value in ((new_first, out_first, first), (new_second, out_second, second)):
        for pair in range(8):
            both = value[pair * 16:(pair + 1) * 16, :].astype(F32)
            kept[:, 2 * pair * PIECE:(2 * pair + 1) * PIECE] = both[:J]
            kept[:, (2 * pair + 1) * PIECE:(2 * pair + 2) * PIECE] = both[J:]
        write(kept, out)
    for kept, out, columns, base in ((new_a, out_a, A_UNITS, 0), (new_b, out_b, B_UNITS, A_UNITS * R)):
        for column in range(columns):
            cols = pl.ds(column * UNIT, UNIT)
            stack = jnp.concatenate([unit(base + r * columns + column) for r in range(R)], axis=0).astype(BF)
            kept[:, cols] = jnp.dot(turn, stack, preferred_element_type=F32)
            write(kept.at[:, cols], out.at[:, cols])
    for copy in copies:
        copy.wait()


def vmem(count):
    return [pl.BlockSpec(memory_space=pltpu.VMEM)] * count


def anywhere(count):
    return [pl.BlockSpec(memory_space=pl.ANY)] * count


def shards(tokens, up_grad, gate_weights, expert_ids, new_home, adapter_a, adapter_b, first_moment, second_moment):
    dma = pltpu.SemaphoreType.DMA
    whole, first, second = pl.pallas_call(
        main_kernel,
        out_shape=[
            jax.ShapeDtypeStruct((ND * 128, PIECE), BF),
            jax.ShapeDtypeStruct((128, PIECE), BF),
            jax.ShapeDtypeStruct((128, PIECE), BF),
        ],
        in_specs=anywhere(2) + vmem(3) + anywhere(4),
        out_specs=vmem(3),
        scratch_shapes=[
            pltpu.VMEM((NE * TOK, D), BF),
            pltpu.VMEM((COPIES, FF), BF),
            pltpu.VMEM((NE * ROWS, FF), BF),
            pltpu.VMEM((NE * EARLY, FF), BF),
            pltpu.VMEM((NE * LATE, FF), BF),
            pltpu.VMEM((NE * TOP, TOK), I32),
            pltpu.VMEM((RJ, D), F32),
            pltpu.VMEM((RJ, FF), F32),
            pltpu.VMEM((RJ, D), BF),
            pltpu.VMEM((RJ, FF), BF),
            pltpu.VMEM((4 * ROWS, COPIES), BF),
            pltpu.VMEM((NE * EARLY, TOK), BF),
            pltpu.VMEM((NE * LATE, TOK), BF),
            pltpu.VMEM((4 * TOK, RJ), BF),
            pltpu.VMEM((RC, NE * TOK), BF),
            pltpu.VMEM((NE * EARLY, RJ), BF),
            pltpu.VMEM((NE * LATE, RJ), BF),
            pltpu.VMEM((NE * EARLY, RJ), BF),
            pltpu.VMEM((NE * LATE, RJ), BF),
            pltpu.VMEM((RC, D), F32),
            pltpu.VMEM((RC, FF), F32),
            pltpu.VMEM((1, COPIES), I32),
            pltpu.VMEM((2, ND * 16, QUARTER), BF),
            pltpu.VMEM((2, ND * 16, QUARTER), BF),
            pltpu.VMEM((J, SHARE), F32),
            pltpu.VMEM((J, SHARE), F32),
            pltpu.VMEM((8 * J, D), F32),
            pltpu.VMEM((16 * J, FF), F32),
            pltpu.VMEM((J, SHARE), F32),
            pltpu.VMEM((3, 128, PIECE), BF),
            pltpu.VMEM((3, 256, PIECE), BF),
            pltpu.VMEM((3, 256, PIECE), BF),
            dma((6,)),
            dma((NE,)),
            dma((NE,)),
            dma((NE * 5,)),
            dma((2 * NE,)),
            dma((64,)),
            dma((32,)),
            dma((16,)),
            dma((4 * ND,)),
            dma((4 * ND,)),
            dma((4 * NE,)),
            dma((4 * NE,)),
            dma((32,)),
            dma((32,)),
        ],
        compiler_params=pltpu.CompilerParams(collective_id=0, has_side_effects=True, vmem_limit_bytes=63 * 2**20),
        name="dispatch_update",
    )(
        tokens, up_grad.reshape(COPIES, FF), gate_weights.T, expert_ids.T, new_home.reshape(1, NE * J),
        adapter_a.reshape(RJ, D), adapter_b.reshape(RJ, FF), first_moment, second_moment,
    )
    new_a, new_b, new_first, new_second = pl.pallas_call(
        finish_kernel,
        out_shape=[
            jax.ShapeDtypeStruct((RJ, D), F32),
            jax.ShapeDtypeStruct((RJ, FF), F32),
            jax.ShapeDtypeStruct((J, SHARE), F32),
            jax.ShapeDtypeStruct((J, SHARE), F32),
        ],
        in_specs=vmem(3),
        out_specs=anywhere(4),
        scratch_shapes=[
            pltpu.VMEM((RJ, D), F32),
            pltpu.VMEM((RJ, FF), F32),
            pltpu.VMEM((J, SHARE), F32),
            pltpu.VMEM((J, SHARE), F32),
            dma((2 + A_UNITS + B_UNITS,)),
        ],
        compiler_params=pltpu.CompilerParams(vmem_limit_bytes=60 * 2**20),
        name="finish",
    )(whole, first, second)
    return new_a.reshape(J, R, D), new_b.reshape(J, R, FF), new_first, new_second


def solution(mesh):
    placed = (
        P(("dp", "expert"), None),
        P(("dp", "expert"), None, None),
        P(("dp", "expert"), None),
        P(("dp", "expert"), None),
        P(),
        P("expert", None, None),
        P("expert", None, None),
        P("expert", "dp"),
        P("expert", "dp"),
    )
    return jax.shard_map(
        shards,
        mesh=mesh,
        in_specs=placed,
        out_specs=(P("expert", None, None), P("expert", None, None), P("expert", "dp"), P("expert", "dp")),
        check_vma=False,
    )
```

```python
import jax
import jax.numpy as jnp
from jax import lax
from jax.experimental import pallas as pl
from jax.experimental.pallas import tpu as pltpu
from jax.sharding import PartitionSpec as P

beta_one = 0.9
beta_two = 0.999
learn_rate = 0.001
decay_rate = 0.01
adam_eps = 1e-08
adapter_scale_factor = 2.0
adam_step = 10.0

D = 4096
FF = 1536
TOP = 8
R = 32
J = 8
TOK = 128
COPIES = TOK * TOP
CAP = 10
NE = 16
ND = 8
ROWS = J * CAP
MSG = 16
MESSAGES = ROWS // MSG
BLOCK = NE * MSG
RJ = R * J
CH = 2
CHUNKS = J // CH
RC = R * CH
UNIT = 512
SHARE = 22528
PIECE = SHARE // 16
EIGHTH = SHARE // 8
UNITS = SHARE // UNIT
A_UNITS = D // UNIT
B_UNITS = FF // UNIT
SPLIT = 1792
SUBS = ((0, 768), (768, 640))

MESH = pl.DeviceIdType.MESH
BF = jnp.bfloat16
F32 = jnp.float32
I32 = jnp.int32


def iota(shape, dim):
    return lax.broadcasted_iota(I32, shape, dim)


def ones(mask):
    return mask.astype(F32).astype(BF)


def contract(lhs, rhs, i, k, precision=None):
    return lax.dot_general(lhs, rhs, (((i,), (k,)), ((), ())), preferred_element_type=F32, precision=precision)


def at(start, size, unit=None):
    return pl.ds(pl.multiple_of(start, unit or size), size)


def main_kernel(
    tok, up_hbm, gate_t, ids_t, homes_row, a_hbm, b_hbm, first_hbm, second_hbm, whole, first_out, second_out,
    gathered, cots, send, got, ids_all, a, b, a16, b16, pick, hot, low, weights,
    lows, back, grad_a, grad_b, row, wire, wire_got,
    first, second, rows_a, rows_b, param, moving, packed, landed,
    local, ids_send, ids_recv, cot_send, cot_recv, tok_send, tok_recv, sib_recv,
    grad_send, grad_recv, move_send, move_recv, all_send, all_recv,
):
    dp = lax.axis_index("dp")
    me = lax.axis_index("expert")
    x = me // 4
    yh = (me // 2) % 2
    core = me % 2
    dp_across = (dp + 4) % 8
    yl = dp // 4
    z = dp % 4

    def place(dy, dx, dc):
        return ((x + dx) % 4) * 4 + ((yh + dy) % 2) * 2 + (core + dc) % 2

    def device(dy, dx, dc):
        return (dp_across if dy else dp, place(dy, dx, dc))

    def copy_to(src, dst, send_sem, recv_sem, to):
        return pltpu.make_async_remote_copy(
            src_ref=src, dst_ref=dst, send_sem=send_sem, recv_sem=recv_sem, device_id=to, device_id_type=MESH
        )

    peers = [
        (1, 0, 0), (0, 2, 0), (0, 1, 0), (0, 3, 0), (1, 2, 0), (1, 0, 1), (0, 2, 1), (1, 1, 0),
        (0, 3, 1), (1, 2, 1), (1, 3, 0), (0, 1, 1), (1, 1, 1), (1, 3, 1), (0, 0, 1),
    ]
    groups = [((dp + step) % ND, me) for step in range(1, ND)]
    homes = [(dp, (me + step) % NE) for step in range(1, NE)]

    loads = [
        pltpu.make_async_copy(src, dst, local.at[number])
        for number, (src, dst) in enumerate([
            (tok, gathered.at[at(me * TOK, TOK)]), (up_hbm, cots), (a_hbm, a), (b_hbm, b), (first_hbm, first), (second_hbm, second),
        ])
    ]
    for load in loads:
        load.start()
    barrier = pltpu.get_barrier_semaphore()
    met = groups + homes + [device(*peer) for peer in peers if peer[0]]
    for peer in met:
        pl.semaphore_signal(barrier, inc=1, device_id=peer, device_id_type=MESH)
    pl.semaphore_wait(barrier, len(met))
    loads[0].wait()

    sent = []

    def block(dy, dx, dc, half, part):
        rows = place(dy, dx, dc) * TOK
        size = TOK
        if part is not None:
            rows = rows + part * (TOK // 2)
            size = TOK // 2
        cols = pl.ds(SPLIT, D - SPLIT) if half else pl.ds(0, SPLIT)
        return gathered.at[at(rows, size), cols]

    def push(src, half, part, to, sem):
        ref = block(*src, half, part)
        copy = copy_to(ref, ref, tok_send.at[len(sent)], sem, device(*to))
        copy.start()
        sent.append(copy)

    def slot(half, dy, dx, part):
        return tok_recv.at[((half * 2 + dy) * 4 + dx) * 2 + part]

    def sib_slot(half, dy, dx):
        return sib_recv.at[(half * 2 + dy) * 4 + dx]

    def arrive(half, dy, dx, part=None):
        ref = block(dy, dx, 0, half, part)
        copy_to(ref, ref, tok_send.at[0], slot(half, dy, dx, part or 0), device(0, 1, 0)).wait_recv()

    def to_sibling(half, dy, dx):
        push((dy, dx, 0), half, None, (0, 0, 1), sib_slot(half, dy, dx))

    def to_across(half, dx):
        push((0, dx, 0), half, None, (1, 0, 0), slot(half, 1, dx, 0))

    def to_right(half, dy, dx, part=None):
        push((dy, dx, 0), half, part, (0, 1, 0), slot(half, dy, (dx + 3) % 4, part or 0))

    def to_left(half, dy, dx, part=None):
        push((dy, dx, 0), half, part, (0, 3, 0), slot(half, dy, (dx + 1) % 4, part or 0))

    to_across(1, 0)
    to_right(0, 0, 0)
    to_left(0, 0, 0)
    to_across(0, 0)
    to_right(1, 0, 0)
    to_left(1, 0, 0)
    to_sibling(0, 0, 0)
    to_sibling(1, 0, 0)

    small = []
    mine = at(me * TOP, TOP)
    ids_all[mine, :] = ids_t[...]
    for number, peer in enumerate(peers):
        copy = copy_to(ids_all.at[mine], ids_all.at[mine], ids_send.at[number], ids_recv.at[me], device(*peer))
        copy.start()
        small.append(copy)

    owner_of = iota((TOK, COPIES), 1) // TOP == iota((TOK, COPIES), 0)
    which = iota((TOP, COPIES), 1) % TOP == iota((TOP, COPIES), 0)
    spread = jnp.dot(ids_t[...].astype(F32).astype(BF), ones(owner_of), preferred_element_type=F32)
    ids_flat = jnp.sum(jnp.where(which, spread, 0.0), axis=0, keepdims=True).astype(I32)
    before = ones(iota((TOK, TOK), 0) < iota((TOK, TOK), 1))
    experts = iota((TOK, TOK), 0)
    total = jnp.zeros((TOK, 1), F32)
    for part in range(TOP):
        hit = ids_flat[:, part * TOK:(part + 1) * TOK] == experts
        value = hit.astype(F32)
        count = jnp.dot(value.astype(BF), before, preferred_element_type=F32) + total
        total = total + jnp.sum(value, axis=1, keepdims=True)
        row[:, part * TOK:(part + 1) * TOK] = jnp.sum(
            jnp.where(hit, count + (CAP * experts).astype(F32), 0.0), axis=0, keepdims=True
        ).astype(I32)

    loads[1].wait()

    @pl.loop(0, TOP)
    def _(part):
        rows = at(part * TOK, TOK)
        mine_of = (iota((TOK, TOK), 0) + part * TOK) // TOP == iota((TOK, TOK), 1)
        scale = contract(mine_of.astype(F32), gate_t[...], 1, 1, lax.Precision.HIGHEST)
        scale = jnp.sum(jnp.where(iota((TOK, TOP), 0) % TOP == iota((TOK, TOP), 1), scale, 0.0), axis=1, keepdims=True)
        cots[rows, :] = (scale * cots[rows, :].astype(F32)).astype(BF)

    for dx in (2, 1, 3, 0):
        base = ((x + dx) % 4) * (4 * ROWS)
        pick[...] = ones(iota((4 * ROWS, COPIES), 0) + base == row[...])

        @pl.loop(0, FF // UNIT)
        def _(part):
            cols = at(part * UNIT, UNIT)
            send[at(base, 4 * ROWS), cols] = jnp.dot(pick[...], cots[:, cols], preferred_element_type=F32).astype(BF)

    cot_sent = []

    def send_cots(message):
        for peer in peers:
            copy = copy_to(
                send.at[at(place(*peer) * ROWS + message * MSG, MSG)], got.at[at(message * BLOCK + me * MSG, MSG)],
                cot_send.at[len(cot_sent)], cot_recv.at[message * NE + me], device(*peer),
            )
            copy.start()
            cot_sent.append(copy)
        got[at(message * BLOCK + me * MSG, MSG), :] = send[at(me * ROWS + message * MSG, MSG), :]

    def wait_cots(message):
        for peer in peers:
            ref = got.at[at(message * BLOCK + place(*peer) * MSG, MSG)]
            copy_to(ref, ref, cot_send.at[0], cot_recv.at[message * NE + place(*peer)], device(*peer)).wait_recv()

    arrive(1, 1, 0)
    to_right(1, 1, 0)
    to_left(1, 1, 0)
    to_sibling(1, 1, 0)
    arrive(0, 0, 3)
    to_right(0, 0, 3, 0)
    to_across(0, 3)
    to_sibling(0, 0, 3)
    arrive(0, 0, 1)
    to_left(0, 0, 1, 1)
    to_across(0, 1)
    to_sibling(0, 0, 1)
    send_cots(0)

    index = iota((RJ, RJ), 0)
    turn = ones(iota((RJ, RJ), 1) == (index // RC * CH + index % CH) * R + (index % RC) // CH)
    loads[2].wait()
    loads[3].wait()

    @pl.loop(0, A_UNITS)
    def _(part):
        cols = at(part * UNIT, UNIT)
        a16[:, cols] = jnp.dot(turn, a[:, cols].astype(BF), preferred_element_type=F32).astype(BF)

    @pl.loop(0, B_UNITS)
    def _(part):
        cols = at(part * UNIT, UNIT)
        b16[:, cols] = jnp.dot(turn, b[:, cols].astype(BF), preferred_element_type=F32).astype(BF)

    arrive(0, 1, 0)
    to_sibling(0, 1, 0)
    arrive(1, 0, 3)
    to_right(1, 0, 3, 0)
    to_sibling(1, 0, 3)
    arrive(1, 0, 1)
    to_left(1, 0, 1, 1)
    to_sibling(1, 0, 1)

    def own(size, first_row, chunk):
        line = iota((size, RC), 0) + first_row
        return line // CAP == chunk * CH + iota((size, RC), 1) % CH

    def from_sibling(dx):
        for half in range(2):
            for dy in range(2):
                ref = block(dy, dx, 1, half, None)
                copy_to(ref, ref, tok_send.at[0], sib_slot(half, dy, dx), device(0, 0, 1)).wait_recv()

    def hidden(dx):
        from_sibling(dx)
        base = (x + dx) % 4
        rows = at(base * 4 * TOK, 4 * TOK)
        low[...] = contract(gathered[rows, :], a16[...], 1, 1).astype(BF)
        for inside in range(4):
            source = base * 4 + inside
            value = jnp.dot(
                hot[at(source * ROWS, ROWS, MSG), :], low[inside * TOK:(inside + 1) * TOK, :], preferred_element_type=F32
            )
            for chunk in range(CHUNKS):
                first_row = chunk * MSG
                part = jnp.where(
                    own(2 * MSG, first_row, chunk),
                    value[first_row:first_row + 2 * MSG, chunk * RC:(chunk + 1) * RC], 0.0,
                ).astype(BF)
                lows[chunk, at(source * MSG, MSG), :] = part[:MSG]
                lows[chunk, at(BLOCK + source * MSG, MSG), :] = part[MSG:]

    arrive(0, 0, 2, 0)
    arrive(0, 0, 2, 1)
    to_across(0, 2)
    to_sibling(0, 0, 2)
    arrive(1, 1, 3)
    to_right(1, 1, 3, 0)
    to_sibling(1, 1, 3)
    arrive(1, 1, 1)
    to_left(1, 1, 1, 1)
    to_sibling(1, 1, 1)

    for peer in peers:
        ref = ids_all.at[at(place(*peer) * TOP, TOP)]
        copy_to(ref, ref, ids_send.at[0], ids_recv.at[place(*peer)], device(*peer)).wait_recv()
    repeat = ones(iota((ROWS, J), 0) // CAP == iota((ROWS, J), 1))
    turn_in = (iota((ROWS, TOK), 0) % CAP).astype(F32)

    @pl.loop(0, NE, unroll=4)
    def _(source):
        ids = ids_all[at(source * TOP, TOP), :]
        hit = jnp.zeros((J, TOK), F32)
        for k in range(TOP):
            hit = hit + jnp.where(ids[k:k + 1, :] == iota((J, TOK), 0) + me * J, 1.0, 0.0)
        count = jnp.dot(hit.astype(BF), before, preferred_element_type=F32)
        value = jnp.where(hit > 0.5, count, -1.0)
        found = ones(jnp.dot(repeat, value.astype(BF), preferred_element_type=F32) == turn_in)
        hot[at(source * ROWS, ROWS, MSG), :] = found

    exact = lax.Precision.HIGHEST
    start = UNITS * dp
    a_first = jnp.minimum(start // A_UNITS, R - 8)
    b_first = jnp.clip((start - A_UNITS * R) // B_UNITS, 0, R - 16)

    def chooser(count, base):
        index = iota((count * J, RJ), 0)
        return (iota((count * J, RJ), 1) == (index % J) * R + index // J + base).astype(F32)

    @pl.loop(0, A_UNITS)
    def _(part):
        cols = at(part * UNIT, UNIT)
        rows_a[:, cols] = jnp.dot(chooser(8, a_first), a[:, cols], preferred_element_type=F32, precision=exact)

    @pl.loop(0, B_UNITS)
    def _(part):
        cols = at(part * UNIT, UNIT)
        rows_b[:, cols] = jnp.dot(chooser(16, b_first), b[:, cols], preferred_element_type=F32, precision=exact)

    @pl.loop(0, UNITS)
    def _(column):
        number = start + column
        in_a = jnp.clip(number // A_UNITS - a_first, 0, 7)
        number_b = jnp.maximum(number - A_UNITS * R, 0)
        in_b = jnp.clip(number_b // B_UNITS - b_first, 0, 15)
        value_a = rows_a[at(in_a * J, J), at(number % A_UNITS * UNIT, UNIT)]
        value_b = rows_b[at(in_b * J, J), at(number_b % B_UNITS * UNIT, UNIT)]
        param[:, at(column * UNIT, UNIT)] = jnp.where(number < A_UNITS * R, value_a, value_b)

    homes_now = homes_row[...].astype(F32).astype(BF)
    lane = iota((128, 128), 1)
    line = iota((128, 128), 0)
    dest = jnp.dot(homes_now, ones(line == me * J + lane % J), preferred_element_type=F32).astype(I32)
    named = ones(homes_row[...] == me * J + line % J)
    owner = contract(ones(iota((1, 128), 1) >= 0) * iota((1, 128), 1).astype(F32).astype(BF), named, 1, 1).astype(I32)
    stay = ones((line // J == lane // J) & (line % J == owner % J) & (owner // J == me))
    lane = iota((256, 128), 1)
    line = iota((256, 128), 0)
    same = (line % 16 == lane // J) & (line // 16 != me)
    leave = ones(same & (line // 16 == dest // J))
    enter = ones(same & (line // 16 == owner // J))

    hidden(0)
    arrive(0, 1, 3)
    to_sibling(0, 1, 3)
    arrive(0, 1, 1)
    to_sibling(0, 1, 1)
    send_cots(1)
    arrive(1, 0, 2, 0)
    arrive(1, 0, 2, 1)
    to_sibling(1, 0, 2)
    hidden(3)
    hidden(1)
    arrive(1, 1, 2, 0)
    arrive(1, 1, 2, 1)
    to_sibling(1, 1, 2)
    arrive(0, 1, 2)
    to_sibling(0, 1, 2)
    send_cots(2)
    hidden(2)

    def grad_flat(number, size):
        parts = []
        while size:
            if number < R * D:
                ref, (r, column), width = grad_a, divmod(number, D), D
            else:
                ref, (r, column), width = grad_b, divmod(number - R * D, FF), FF
            step = min(size, width - column)
            parts.append(ref[r * CH:(r + 1) * CH, column:column + step])
            number += step
            size -= step
        return parts[0] if len(parts) == 1 else jnp.concatenate(parts, axis=1)

    grad_sent = []

    def send_grads(chunk, cols, index):
        for step in (4, 1, 7, 3, 5, 2, 6):
            to = groups[step - 1]
            copy = copy_to(
                wire.at[chunk, at(to[0] * 16, 16), cols], wire_got.at[chunk, at(dp * 16, 16), cols],
                grad_send.at[index * ND + step], grad_recv.at[index * ND + dp], to,
            )
            copy.start()
            grad_sent.append(copy)
        wire_got[chunk, at(dp * 16, 16), cols] = wire[chunk, at(dp * 16, 16), cols]

    def wait_grads(chunk, cols, index):
        for step in range(1, ND):
            source = (dp + step) % ND
            ref = wire_got.at[chunk, at(source * 16, 16), cols]
            copy_to(ref, ref, grad_send.at[0], grad_recv.at[index * ND + source], groups[step - 1]).wait_recv()

    def wire_cols(sub):
        return pl.ds(0, EIGHTH) if sub is None else pl.ds(2 * SUBS[sub][0], 2 * SUBS[sub][1])

    def gradients(chunk):
        used = pl.ds(chunk * BLOCK, 2 * BLOCK)
        mask = [
            jnp.concatenate([own(MSG, (chunk + message) * MSG, chunk)] * 4, axis=0) for message in range(2)
        ]
        for message in range(2):
            for part in range(4):
                rows = pl.ds((chunk + message) * BLOCK + part * 4 * MSG, 4 * MSG)
                value = contract(got[rows, :], b16[chunk * RC:(chunk + 1) * RC, :], 1, 1)
                value = jnp.where(mask[message], value, 0.0).astype(BF)
                for inside in range(4):
                    row0 = (part * 4 + inside) * 2 * MSG + message * MSG
                    back[row0:row0 + MSG, :] = value[inside * MSG:(inside + 1) * MSG, :]

        @pl.loop(0, NE, unroll=8)
        def _(source):
            value = contract(
                back[at(source * 2 * MSG, 2 * MSG), :], hot[at(source * ROWS + chunk * MSG, 2 * MSG, MSG), :], 0, 0
            )
            weights[:, at(source * TOK, TOK)] = value.astype(BF)

        @pl.loop(0, D // 1024)
        def _(part):
            cols = at(part * 1024, 1024)
            grad_a[:, cols] = jnp.dot(weights[...], gathered[:, cols], preferred_element_type=F32)

        @pl.loop(0, B_UNITS)
        def _(part):
            cols = at(part * UNIT, UNIT)
            grad_b[:, cols] = contract(lows[chunk], got[used, cols], 0, 0)

        last = chunk == CHUNKS - 1
        for sub, (offset, size) in enumerate(SUBS):
            for share in range(ND):
                for part in range(2):
                    base = share * SHARE + part * PIECE + offset
                    value = jnp.concatenate([grad_flat(base + eighth * EIGHTH, size) for eighth in range(8)], axis=0)
                    col = 2 * offset + part * size
                    wire[chunk, share * 16:(share + 1) * 16, col:col + size] = value.astype(BF)
            if last:
                send_grads(chunk, wire_cols(sub), chunk + sub)
        if not last:
            send_grads(chunk, wire_cols(None), chunk)

    wait_cots(0)
    send_cots(3)
    wait_cots(1)
    gradients(0)
    wait_cots(2)
    send_cots(4)
    gradients(1)
    wait_cots(3)
    gradients(2)
    wait_cots(4)
    gradients(3)

    loads[4].wait()
    loads[5].wait()
    fix_one = 1.0 - beta_one**adam_step
    fix_two = 1.0 - beta_two**adam_step

    def update(sub):
        offset, size = SUBS[sub]
        for part in range(2):
            inside = pl.ds(2 * offset + part * size, size)
            totals = []
            for chunk in range(CHUNKS):
                grad = wire_got[chunk, 0:16, inside].astype(F32)
                for source in range(1, ND):
                    grad = grad + wire_got[chunk, source * 16:(source + 1) * 16, inside].astype(F32)
                totals.append(adapter_scale_factor * grad)
            for eighth in range(8):
                piece = eighth * 2 + part
                cols = pl.ds(piece * PIECE + offset, size)
                grad = jnp.concatenate([total[eighth * CH:(eighth + 1) * CH] for total in totals], axis=0)
                one = beta_one * first[:, cols] + (1.0 - beta_one) * grad
                two = beta_two * second[:, cols] + (1.0 - beta_two) * grad * grad
                old = param[:, cols]
                new = old - learn_rate * (one / fix_one / (jnp.sqrt(two / fix_two) + adam_eps) + decay_rate * old)
                for kind, value in enumerate((new, one, two)):
                    moving[kind, piece * J:(piece + 1) * J, pl.ds(offset, size)] = value.astype(BF)

    move_sent = []

    def move(kind, cols, index):
        packed[kind, :, cols] = jnp.dot(leave, moving[kind, :, cols], preferred_element_type=F32).astype(BF)
        landed[kind, at(me * 16, 16), cols] = jnp.zeros((16, cols.size), BF)
        for step in (8, 9, 10, 11, 7, 6, 5, 4, 12, 13, 14, 15, 3, 2, 1):
            to = homes[step - 1]
            copy = copy_to(
                packed.at[kind, at(to[1] * 16, 16), cols], landed.at[kind, at(me * 16, 16), cols],
                move_send.at[index * NE + step], move_recv.at[index * NE + me], to,
            )
            copy.start()
            move_sent.append(copy)

    def arrived(kind, cols, index):
        for step in range(1, NE):
            source = (me + step) % NE
            ref = landed.at[kind, at(source * 16, 16), cols]
            copy_to(ref, ref, move_send.at[0], move_recv.at[index * NE + source], homes[step - 1]).wait_recv()
        return (contract(enter, landed[kind, :, cols], 0, 0) + contract(stay, moving[kind, :, cols], 0, 0)).astype(BF)

    all_sent = []

    def group(dy, dz):
        return ((yl + dy) % 2) * 4 + (z + dz) % 4

    def part_of(dy, dz, sub, half):
        rows = at(group(dy, dz) * 128, 128) if half is None else at(group(dy, dz) * 128 + half * 64, 64)
        return whole.at[rows, pl.ds(*SUBS[sub])]

    def share_slot(dy, dz, sub, half):
        return all_recv.at[((sub * 2 + dy) * 4 + dz) * 2 + (half or 0)]

    def pass_on(dy, dz, sub, to_y, to_z, half=None):
        ref = part_of(dy, dz, sub, half)
        copy = copy_to(
            ref, ref, all_send.at[len(all_sent)], share_slot((dy + to_y) % 2, (dz - to_z) % 4, sub, half), (group(to_y, to_z), me)
        )
        copy.start()
        all_sent.append(copy)

    def came(dy, dz, sub, half=None):
        ref = part_of(dy, dz, sub, half)
        copy_to(ref, ref, all_send.at[0], share_slot(dy, dz, sub, half), groups[0]).wait_recv()

    for chunk in range(CHUNKS - 1):
        wait_grads(chunk, wire_cols(None), chunk)
    for sub in range(2):
        wait_grads(CHUNKS - 1, wire_cols(sub), CHUNKS - 1 + sub)
        update(sub)
        move(0, pl.ds(*SUBS[sub]), sub)
    for sub in range(2):
        cols = pl.ds(*SUBS[sub])
        whole[at(dp * 128, 128), cols] = arrived(0, cols, sub)
        pass_on(0, 0, sub, 1, 0)
        pass_on(0, 0, sub, 0, 1)
        pass_on(0, 0, sub, 0, 3)
    full = pl.ds(0, PIECE)
    move(1, full, 2)
    move(2, full, 3)
    for sub in range(2):
        came(1, 0, sub)
        pass_on(1, 0, sub, 0, 1)
        pass_on(1, 0, sub, 0, 3)
        came(0, 3, sub)
        pass_on(0, 3, sub, 0, 1, 0)
        came(0, 1, sub)
        pass_on(0, 1, sub, 0, 3, 1)
    for sub in range(2):
        came(1, 3, sub)
        pass_on(1, 3, sub, 0, 1, 0)
        came(1, 1, sub)
        pass_on(1, 1, sub, 0, 3, 1)
    first_out[...] = arrived(1, full, 2)
    second_out[...] = arrived(2, full, 3)
    for sub in range(2):
        for half in range(2):
            came(0, 2, sub, half)
            came(1, 2, sub, half)
    for copy in sent + small + cot_sent + grad_sent + move_sent + all_sent:
        copy.wait_send()


def finish_kernel(whole, first, second, out_a, out_b, out_first, out_second, new_a, new_b, new_first, new_second, sems):
    index = iota((RJ, RJ), 0)
    turn = ones(iota((RJ, RJ), 1) == index % R * J + index // R)

    def unit(number):
        share, inside = divmod(number * UNIT, SHARE)
        parts = []
        left = UNIT
        while left:
            piece, offset = divmod(inside, PIECE)
            size = min(left, PIECE - offset)
            line = share * 128 + piece * J
            pair = whole[line // 16 * 16:line // 16 * 16 + 16, offset:offset + size].astype(F32)
            parts.append(pair[line % 16:line % 16 + J])
            left -= size
            inside += size
        return parts[0] if len(parts) == 1 else jnp.concatenate(parts, axis=1)

    copies = []

    def write(src, dst):
        copy = pltpu.make_async_copy(src, dst, sems.at[len(copies)])
        copy.start()
        copies.append(copy)

    for kept, out, value in ((new_first, out_first, first), (new_second, out_second, second)):
        for pair in range(8):
            both = value[pair * 16:(pair + 1) * 16, :].astype(F32)
            kept[:, 2 * pair * PIECE:(2 * pair + 1) * PIECE] = both[:J]
            kept[:, (2 * pair + 1) * PIECE:(2 * pair + 2) * PIECE] = both[J:]
        write(kept, out)
    for kept, out, columns, base in ((new_a, out_a, A_UNITS, 0), (new_b, out_b, B_UNITS, A_UNITS * R)):
        for column in range(columns):
            cols = pl.ds(column * UNIT, UNIT)
            stack = jnp.concatenate([unit(base + r * columns + column) for r in range(R)], axis=0).astype(BF)
            kept[:, cols] = jnp.dot(turn, stack, preferred_element_type=F32)
            write(kept.at[:, cols], out.at[:, cols])
    for copy in copies:
        copy.wait()


def vmem(count):
    return [pl.BlockSpec(memory_space=pltpu.VMEM)] * count


def anywhere(count):
    return [pl.BlockSpec(memory_space=pl.ANY)] * count


def shards(tokens, up_grad, gate_weights, expert_ids, new_home, adapter_a, adapter_b, first_moment, second_moment):
    dma = pltpu.SemaphoreType.DMA
    whole, first, second = pl.pallas_call(
        main_kernel,
        out_shape=[
            jax.ShapeDtypeStruct((ND * 128, PIECE), BF),
            jax.ShapeDtypeStruct((128, PIECE), BF),
            jax.ShapeDtypeStruct((128, PIECE), BF),
        ],
        in_specs=anywhere(2) + vmem(3) + anywhere(4),
        out_specs=vmem(3),
        scratch_shapes=[
            pltpu.VMEM((NE * TOK, D), BF),
            pltpu.VMEM((COPIES, FF), BF),
            pltpu.VMEM((NE * ROWS, FF), BF),
            pltpu.VMEM((NE * ROWS, FF), BF),
            pltpu.VMEM((NE * TOP, TOK), I32),
            pltpu.VMEM((RJ, D), F32),
            pltpu.VMEM((RJ, FF), F32),
            pltpu.VMEM((RJ, D), BF),
            pltpu.VMEM((RJ, FF), BF),
            pltpu.VMEM((4 * ROWS, COPIES), BF),
            pltpu.VMEM((NE * ROWS, TOK), BF),
            pltpu.VMEM((4 * TOK, RJ), BF),
            pltpu.VMEM((RC, NE * TOK), BF),
            pltpu.VMEM((CHUNKS, 2 * BLOCK, RC), BF),
            pltpu.VMEM((2 * BLOCK, RC), BF),
            pltpu.VMEM((RC, D), F32),
            pltpu.VMEM((RC, FF), F32),
            pltpu.VMEM((1, COPIES), I32),
            pltpu.VMEM((CHUNKS, ND * 16, EIGHTH), BF),
            pltpu.VMEM((CHUNKS, ND * 16, EIGHTH), BF),
            pltpu.VMEM((J, SHARE), F32),
            pltpu.VMEM((J, SHARE), F32),
            pltpu.VMEM((8 * J, D), F32),
            pltpu.VMEM((16 * J, FF), F32),
            pltpu.VMEM((J, SHARE), F32),
            pltpu.VMEM((3, 128, PIECE), BF),
            pltpu.VMEM((3, 256, PIECE), BF),
            pltpu.VMEM((3, 256, PIECE), BF),
            dma((6,)),
            dma((NE,)),
            dma((NE,)),
            dma((NE * 5,)),
            dma((MESSAGES * NE,)),
            dma((64,)),
            dma((32,)),
            dma((16,)),
            dma(((CHUNKS + 1) * ND,)),
            dma(((CHUNKS + 1) * ND,)),
            dma((4 * NE,)),
            dma((4 * NE,)),
            dma((32,)),
            dma((32,)),
        ],
        compiler_params=pltpu.CompilerParams(collective_id=0, has_side_effects=True, vmem_limit_bytes=63 * 2**20),
        name="dispatch_update",
    )(
        tokens, up_grad.reshape(COPIES, FF), gate_weights.T, expert_ids.T, new_home.reshape(1, NE * J),
        adapter_a.reshape(RJ, D), adapter_b.reshape(RJ, FF), first_moment, second_moment,
    )
    new_a, new_b, new_first, new_second = pl.pallas_call(
        finish_kernel,
        out_shape=[
            jax.ShapeDtypeStruct((RJ, D), F32),
            jax.ShapeDtypeStruct((RJ, FF), F32),
            jax.ShapeDtypeStruct((J, SHARE), F32),
            jax.ShapeDtypeStruct((J, SHARE), F32),
        ],
        in_specs=vmem(3),
        out_specs=anywhere(4),
        scratch_shapes=[
            pltpu.VMEM((RJ, D), F32),
            pltpu.VMEM((RJ, FF), F32),
            pltpu.VMEM((J, SHARE), F32),
            pltpu.VMEM((J, SHARE), F32),
            dma((2 + A_UNITS + B_UNITS,)),
        ],
        compiler_params=pltpu.CompilerParams(vmem_limit_bytes=60 * 2**20),
        name="finish",
    )(whole, first, second)
    return new_a.reshape(J, R, D), new_b.reshape(J, R, FF), new_first, new_second


def solution(mesh):
    placed = (
        P(("dp", "expert"), None),
        P(("dp", "expert"), None, None),
        P(("dp", "expert"), None),
        P(("dp", "expert"), None),
        P(),
        P("expert", None, None),
        P("expert", None, None),
        P("expert", "dp"),
        P("expert", "dp"),
    )
    return jax.shard_map(
        shards,
        mesh=mesh,
        in_specs=placed,
        out_specs=(P("expert", None, None), P("expert", None, None), P("expert", "dp"), P("expert", "dp")),
        check_vma=False,
    )
```

```python
import jax
import jax.numpy as jnp
from jax import lax
from jax.experimental import pallas as pl
from jax.experimental.pallas import tpu as pltpu
from jax.sharding import PartitionSpec as P

beta_one = 0.9
beta_two = 0.999
learn_rate = 0.001
decay_rate = 0.01
adam_eps = 1e-08
adapter_scale_factor = 2.0
adam_step = 10.0

D = 4096
FF = 1536
TOP = 8
R = 32
J = 8
TOK = 128
COPIES = TOK * TOP
CAP = 10
NE = 16
ND = 8
ROWS = J * CAP
MSG = 16
MESSAGES = ROWS // MSG
BLOCK = NE * MSG
RJ = R * J
CH = 2
CHUNKS = J // CH
RC = R * CH
UNIT = 512
SHARE = 22528
PIECE = SHARE // 16
EIGHTH = SHARE // 8
UNITS = SHARE // UNIT
A_UNITS = D // UNIT
B_UNITS = FF // UNIT
SPLIT = 1792
SUBS = ((0, 640), (640, 768))

MESH = pl.DeviceIdType.MESH
BF = jnp.bfloat16
F32 = jnp.float32
I32 = jnp.int32


def iota(shape, dim):
    return lax.broadcasted_iota(I32, shape, dim)


def ones(mask):
    return mask.astype(F32).astype(BF)


def contract(lhs, rhs, i, k, precision=None):
    return lax.dot_general(lhs, rhs, (((i,), (k,)), ((), ())), preferred_element_type=F32, precision=precision)


def at(start, size, unit=None):
    return pl.ds(pl.multiple_of(start, unit or size), size)


def main_kernel(
    tok, up_hbm, gate_t, ids_t, homes_row, a_hbm, b_hbm, first_hbm, second_hbm, whole, first_out, second_out,
    gathered, cots, send, got, ids_all, a, b, a16, b16, pick, hot, low, weights, picked,
    lows, back, grad_a, grad_b, row, wire, wire_got,
    first, second, rows_a, rows_b, param, moving, packed, landed,
    local, ids_send, ids_recv, cot_send, cot_recv, tok_send, tok_recv, sib_recv,
    grad_send, grad_recv, move_send, move_recv, all_send, all_recv,
):
    dp = lax.axis_index("dp")
    me = lax.axis_index("expert")
    x = me // 4
    yh = (me // 2) % 2
    core = me % 2
    dp_across = (dp + 4) % 8
    yl = dp // 4
    z = dp % 4

    def place(dy, dx, dc):
        return ((x + dx) % 4) * 4 + ((yh + dy) % 2) * 2 + (core + dc) % 2

    def device(dy, dx, dc):
        return (dp_across if dy else dp, place(dy, dx, dc))

    def copy_to(src, dst, send_sem, recv_sem, to):
        return pltpu.make_async_remote_copy(
            src_ref=src, dst_ref=dst, send_sem=send_sem, recv_sem=recv_sem, device_id=to, device_id_type=MESH
        )

    peers = [
        (1, 0, 0), (0, 2, 0), (0, 1, 0), (0, 3, 0), (1, 2, 0), (1, 0, 1), (0, 2, 1), (1, 1, 0),
        (0, 3, 1), (1, 2, 1), (1, 3, 0), (0, 1, 1), (1, 1, 1), (1, 3, 1), (0, 0, 1),
    ]
    groups = [((dp + step) % ND, me) for step in range(1, ND)]
    homes = [(dp, (me + step) % NE) for step in range(1, NE)]

    loads = [
        pltpu.make_async_copy(src, dst, local.at[number])
        for number, (src, dst) in enumerate([
            (tok, gathered.at[at(me * TOK, TOK)]), (up_hbm, cots), (a_hbm, a), (b_hbm, b), (first_hbm, first), (second_hbm, second),
        ])
    ]
    for load in loads:
        load.start()
    barrier = pltpu.get_barrier_semaphore()
    met = groups + homes + [device(*peer) for peer in peers if peer[0]]
    for peer in met:
        pl.semaphore_signal(barrier, inc=1, device_id=peer, device_id_type=MESH)
    pl.semaphore_wait(barrier, len(met))
    loads[0].wait()

    sent = []

    def block(dy, dx, dc, half, part):
        rows = place(dy, dx, dc) * TOK
        size = TOK
        if part is not None:
            rows = rows + part * (TOK // 2)
            size = TOK // 2
        cols = pl.ds(SPLIT, D - SPLIT) if half else pl.ds(0, SPLIT)
        return gathered.at[at(rows, size), cols]

    def push(src, half, part, to, sem):
        ref = block(*src, half, part)
        copy = copy_to(ref, ref, tok_send.at[len(sent)], sem, device(*to))
        copy.start()
        sent.append(copy)

    def slot(half, dy, dx, part):
        return tok_recv.at[((half * 2 + dy) * 4 + dx) * 2 + part]

    def sib_slot(half, dy, dx):
        return sib_recv.at[(half * 2 + dy) * 4 + dx]

    def arrive(half, dy, dx, part=None):
        ref = block(dy, dx, 0, half, part)
        copy_to(ref, ref, tok_send.at[0], slot(half, dy, dx, part or 0), device(0, 1, 0)).wait_recv()

    def to_sibling(half, dy, dx):
        push((dy, dx, 0), half, None, (0, 0, 1), sib_slot(half, dy, dx))

    def to_across(half, dx):
        push((0, dx, 0), half, None, (1, 0, 0), slot(half, 1, dx, 0))

    def to_right(half, dy, dx, part=None):
        push((dy, dx, 0), half, part, (0, 1, 0), slot(half, dy, (dx + 3) % 4, part or 0))

    def to_left(half, dy, dx, part=None):
        push((dy, dx, 0), half, part, (0, 3, 0), slot(half, dy, (dx + 1) % 4, part or 0))

    to_across(1, 0)
    to_right(0, 0, 0)
    to_left(0, 0, 0)
    to_across(0, 0)
    to_right(1, 0, 0)
    to_left(1, 0, 0)
    to_sibling(0, 0, 0)
    to_sibling(1, 0, 0)

    small = []
    mine = at(me * TOP, TOP)
    ids_all[mine, :] = ids_t[...]
    for number, peer in enumerate(peers):
        copy = copy_to(ids_all.at[mine], ids_all.at[mine], ids_send.at[number], ids_recv.at[me], device(*peer))
        copy.start()
        small.append(copy)

    owner_of = iota((TOK, COPIES), 1) // TOP == iota((TOK, COPIES), 0)
    which = iota((TOP, COPIES), 1) % TOP == iota((TOP, COPIES), 0)
    spread = jnp.dot(ids_t[...].astype(F32).astype(BF), ones(owner_of), preferred_element_type=F32)
    ids_flat = jnp.sum(jnp.where(which, spread, 0.0), axis=0, keepdims=True).astype(I32)
    before = ones(iota((TOK, TOK), 0) < iota((TOK, TOK), 1))
    experts = iota((TOK, TOK), 0)
    total = jnp.zeros((TOK, 1), F32)
    for part in range(TOP):
        hit = ids_flat[:, part * TOK:(part + 1) * TOK] == experts
        value = hit.astype(F32)
        count = jnp.dot(value.astype(BF), before, preferred_element_type=F32) + total
        total = total + jnp.sum(value, axis=1, keepdims=True)
        row[:, part * TOK:(part + 1) * TOK] = jnp.sum(
            jnp.where(hit, count + (CAP * experts).astype(F32), 0.0), axis=0, keepdims=True
        ).astype(I32)

    loads[1].wait()

    @pl.loop(0, TOP)
    def _(part):
        rows = at(part * TOK, TOK)
        mine_of = (iota((TOK, TOK), 0) + part * TOK) // TOP == iota((TOK, TOK), 1)
        scale = contract(mine_of.astype(F32), gate_t[...], 1, 1, lax.Precision.HIGHEST)
        scale = jnp.sum(jnp.where(iota((TOK, TOP), 0) % TOP == iota((TOK, TOP), 1), scale, 0.0), axis=1, keepdims=True)
        cots[rows, :] = (scale * cots[rows, :].astype(F32)).astype(BF)

    for dx in (2, 1, 3, 0):
        base = ((x + dx) % 4) * (4 * ROWS)
        pick[...] = ones(iota((4 * ROWS, COPIES), 0) + base == row[...])

        @pl.loop(0, FF // UNIT)
        def _(part):
            cols = at(part * UNIT, UNIT)
            send[at(base, 4 * ROWS), cols] = jnp.dot(pick[...], cots[:, cols], preferred_element_type=F32).astype(BF)

    cot_sent = []

    def send_cots(message):
        for peer in peers:
            copy = copy_to(
                send.at[at(place(*peer) * ROWS + message * MSG, MSG)], got.at[at(message * BLOCK + me * MSG, MSG)],
                cot_send.at[len(cot_sent)], cot_recv.at[message * NE + me], device(*peer),
            )
            copy.start()
            cot_sent.append(copy)
        got[at(message * BLOCK + me * MSG, MSG), :] = send[at(me * ROWS + message * MSG, MSG), :]

    def wait_cots(message):
        for peer in peers:
            ref = got.at[at(message * BLOCK + place(*peer) * MSG, MSG)]
            copy_to(ref, ref, cot_send.at[0], cot_recv.at[message * NE + place(*peer)], device(*peer)).wait_recv()

    arrive(1, 1, 0)
    to_right(1, 1, 0)
    to_left(1, 1, 0)
    to_sibling(1, 1, 0)
    arrive(0, 0, 3)
    to_right(0, 0, 3, 0)
    to_across(0, 3)
    to_sibling(0, 0, 3)
    arrive(0, 0, 1)
    to_left(0, 0, 1, 1)
    to_across(0, 1)
    to_sibling(0, 0, 1)
    send_cots(0)

    index = iota((RJ, RJ), 0)
    turn = ones(iota((RJ, RJ), 1) == (index // RC * CH + index % CH) * R + (index % RC) // CH)
    loads[2].wait()
    loads[3].wait()

    @pl.loop(0, A_UNITS)
    def _(part):
        cols = at(part * UNIT, UNIT)
        a16[:, cols] = jnp.dot(turn, a[:, cols].astype(BF), preferred_element_type=F32).astype(BF)

    @pl.loop(0, B_UNITS)
    def _(part):
        cols = at(part * UNIT, UNIT)
        b16[:, cols] = jnp.dot(turn, b[:, cols].astype(BF), preferred_element_type=F32).astype(BF)

    arrive(0, 1, 0)
    to_sibling(0, 1, 0)
    arrive(1, 0, 3)
    to_right(1, 0, 3, 0)
    to_sibling(1, 0, 3)
    arrive(1, 0, 1)
    to_left(1, 0, 1, 1)
    to_sibling(1, 0, 1)

    def own(size, first_row, chunk):
        line = iota((size, RC), 0) + first_row
        return line // CAP == chunk * CH + iota((size, RC), 1) % CH

    def from_sibling(dx):
        for half in range(2):
            for dy in range(2):
                ref = block(dy, dx, 1, half, None)
                copy_to(ref, ref, tok_send.at[0], sib_slot(half, dy, dx), device(0, 0, 1)).wait_recv()

    def hidden(dx):
        from_sibling(dx)
        base = (x + dx) % 4
        rows = at(base * 4 * TOK, 4 * TOK)
        low[...] = contract(gathered[rows, :], a16[...], 1, 1).astype(BF)
        for inside in range(4):
            source = base * 4 + inside
            value = jnp.dot(
                hot[at(source * ROWS, ROWS, MSG), :], low[inside * TOK:(inside + 1) * TOK, :], preferred_element_type=F32
            )
            for chunk in range(CHUNKS):
                first_row = chunk * MSG
                part = jnp.where(
                    own(2 * MSG, first_row, chunk),
                    value[first_row:first_row + 2 * MSG, chunk * RC:(chunk + 1) * RC], 0.0,
                ).astype(BF)
                lows[chunk, at(source * MSG, MSG), :] = part[:MSG]
                lows[chunk, at(BLOCK + source * MSG, MSG), :] = part[MSG:]

    arrive(0, 0, 2, 0)
    arrive(0, 0, 2, 1)
    to_across(0, 2)
    to_sibling(0, 0, 2)
    arrive(1, 1, 3)
    to_right(1, 1, 3, 0)
    to_sibling(1, 1, 3)
    arrive(1, 1, 1)
    to_left(1, 1, 1, 1)
    to_sibling(1, 1, 1)

    for peer in peers:
        ref = ids_all.at[at(place(*peer) * TOP, TOP)]
        copy_to(ref, ref, ids_send.at[0], ids_recv.at[place(*peer)], device(*peer)).wait_recv()
    repeat = ones(iota((ROWS, J), 0) // CAP == iota((ROWS, J), 1))
    turn_in = (iota((ROWS, TOK), 0) % CAP).astype(F32)

    @pl.loop(0, NE, unroll=4)
    def _(source):
        ids = ids_all[at(source * TOP, TOP), :]
        hit = jnp.zeros((J, TOK), F32)
        for k in range(TOP):
            hit = hit + jnp.where(ids[k:k + 1, :] == iota((J, TOK), 0) + me * J, 1.0, 0.0)
        count = jnp.dot(hit.astype(BF), before, preferred_element_type=F32)
        value = jnp.where(hit > 0.5, count, -1.0)
        found = ones(jnp.dot(repeat, value.astype(BF), preferred_element_type=F32) == turn_in)
        hot[at(source * ROWS, ROWS, MSG), :] = found

    exact = lax.Precision.HIGHEST
    start = UNITS * dp
    a_first = jnp.minimum(start // A_UNITS, R - 8)
    b_first = jnp.clip((start - A_UNITS * R) // B_UNITS, 0, R - 16)

    def chooser(count, base):
        index = iota((count * J, RJ), 0)
        return (iota((count * J, RJ), 1) == (index % J) * R + index // J + base).astype(F32)

    @pl.loop(0, A_UNITS)
    def _(part):
        cols = at(part * UNIT, UNIT)
        rows_a[:, cols] = jnp.dot(chooser(8, a_first), a[:, cols], preferred_element_type=F32, precision=exact)

    @pl.loop(0, B_UNITS)
    def _(part):
        cols = at(part * UNIT, UNIT)
        rows_b[:, cols] = jnp.dot(chooser(16, b_first), b[:, cols], preferred_element_type=F32, precision=exact)

    @pl.loop(0, UNITS)
    def _(column):
        number = start + column
        in_a = jnp.clip(number // A_UNITS - a_first, 0, 7)
        number_b = jnp.maximum(number - A_UNITS * R, 0)
        in_b = jnp.clip(number_b // B_UNITS - b_first, 0, 15)
        value_a = rows_a[at(in_a * J, J), at(number % A_UNITS * UNIT, UNIT)]
        value_b = rows_b[at(in_b * J, J), at(number_b % B_UNITS * UNIT, UNIT)]
        param[:, at(column * UNIT, UNIT)] = jnp.where(number < A_UNITS * R, value_a, value_b)

    homes_now = homes_row[...].astype(F32).astype(BF)
    lane = iota((128, 128), 1)
    line = iota((128, 128), 0)
    dest = jnp.dot(homes_now, ones(line == me * J + lane % J), preferred_element_type=F32).astype(I32)
    named = ones(homes_row[...] == me * J + line % J)
    owner = contract(ones(iota((1, 128), 1) >= 0) * iota((1, 128), 1).astype(F32).astype(BF), named, 1, 1).astype(I32)
    stay = ones((line // J == lane // J) & (line % J == owner % J) & (owner // J == me))
    lane = iota((256, 128), 1)
    line = iota((256, 128), 0)
    same = (line % 16 == lane // J) & (line // 16 != me)
    leave = ones(same & (line // 16 == dest // J))
    enter = ones(same & (line // 16 == owner // J))

    hidden(0)
    arrive(0, 1, 3)
    to_sibling(0, 1, 3)
    arrive(0, 1, 1)
    to_sibling(0, 1, 1)
    send_cots(1)
    arrive(1, 0, 2, 0)
    arrive(1, 0, 2, 1)
    to_sibling(1, 0, 2)
    hidden(3)
    hidden(1)
    arrive(1, 1, 2, 0)
    arrive(1, 1, 2, 1)
    to_sibling(1, 1, 2)
    arrive(0, 1, 2)
    to_sibling(0, 1, 2)
    send_cots(2)
    hidden(2)

    def grad_flat(number, size):
        parts = []
        while size:
            if number < R * D:
                ref, (r, column), width = grad_a, divmod(number, D), D
            else:
                ref, (r, column), width = grad_b, divmod(number - R * D, FF), FF
            step = min(size, width - column)
            parts.append(ref[r * CH:(r + 1) * CH, column:column + step])
            number += step
            size -= step
        return parts[0] if len(parts) == 1 else jnp.concatenate(parts, axis=1)

    grad_sent = []

    def send_grads(chunk, cols, index):
        for step in (4, 1, 7, 3, 5, 2, 6):
            to = groups[step - 1]
            copy = copy_to(
                wire.at[chunk, at(to[0] * 16, 16), cols], wire_got.at[chunk, at(dp * 16, 16), cols],
                grad_send.at[index * ND + step], grad_recv.at[index * ND + dp], to,
            )
            copy.start()
            grad_sent.append(copy)
        wire_got[chunk, at(dp * 16, 16), cols] = wire[chunk, at(dp * 16, 16), cols]

    def wait_grads(chunk, cols, index):
        for step in range(1, ND):
            source = (dp + step) % ND
            ref = wire_got.at[chunk, at(source * 16, 16), cols]
            copy_to(ref, ref, grad_send.at[0], grad_recv.at[index * ND + source], groups[step - 1]).wait_recv()

    def wire_cols(sub):
        return pl.ds(0, EIGHTH) if sub is None else pl.ds(2 * SUBS[sub][0], 2 * SUBS[sub][1])

    def gradients(chunk):
        used = pl.ds(chunk * BLOCK, 2 * BLOCK)
        mask = [
            jnp.concatenate([own(MSG, (chunk + message) * MSG, chunk)] * 4, axis=0) for message in range(2)
        ]
        for message in range(2):
            if message:
                wait_cots(chunk + 1)
            for part in range(4):
                rows = pl.ds((chunk + message) * BLOCK + part * 4 * MSG, 4 * MSG)
                value = contract(got[rows, :], b16[chunk * RC:(chunk + 1) * RC, :], 1, 1)
                value = jnp.where(mask[message], value, 0.0).astype(BF)
                for inside in range(4):
                    row0 = (part * 4 + inside) * 2 * MSG + message * MSG
                    back[row0:row0 + MSG, :] = value[inside * MSG:(inside + 1) * MSG, :]

        last = chunk == CHUNKS - 1
        if last:
            @pl.loop(0, D // 1024)
            def _(part):
                cols = at(part * 1024, 1024)
                grad_a[:, cols] = contract(back[...], picked[:, cols], 0, 0)
        else:
            @pl.loop(0, NE, unroll=8)
            def _(source):
                value = contract(
                    back[at(source * 2 * MSG, 2 * MSG), :], hot[at(source * ROWS + chunk * MSG, 2 * MSG, MSG), :], 0, 0
                )
                weights[:, at(source * TOK, TOK)] = value.astype(BF)

            @pl.loop(0, D // 1024)
            def _(part):
                cols = at(part * 1024, 1024)
                grad_a[:, cols] = jnp.dot(weights[...], gathered[:, cols], preferred_element_type=F32)

        @pl.loop(0, B_UNITS)
        def _(part):
            cols = at(part * UNIT, UNIT)
            grad_b[:, cols] = contract(lows[chunk], got[used, cols], 0, 0)

        for sub, (offset, size) in enumerate(SUBS):
            for share in range(ND):
                for part in range(2):
                    base = share * SHARE + part * PIECE + offset
                    value = jnp.concatenate([grad_flat(base + eighth * EIGHTH, size) for eighth in range(8)], axis=0)
                    col = 2 * offset + part * size
                    wire[chunk, share * 16:(share + 1) * 16, col:col + size] = value.astype(BF)
            if last:
                send_grads(chunk, wire_cols(sub), chunk + sub)
        if not last:
            send_grads(chunk, wire_cols(None), chunk)

    wait_cots(0)
    send_cots(3)

    @pl.loop(0, NE)
    def _(source):
        rows = at(source * TOK, TOK)
        mark = hot[at(source * ROWS + (CHUNKS - 1) * MSG, 2 * MSG, MSG), :]
        for part in range(D // 1024):
            cols = pl.ds(part * 1024, 1024)
            picked[at(source * 2 * MSG, 2 * MSG), cols] = jnp.dot(mark, gathered[rows, cols], preferred_element_type=F32).astype(BF)


    gradients(0)
    send_cots(4)
    gradients(1)
    gradients(2)
    gradients(3)

    loads[4].wait()
    loads[5].wait()
    fix_one = 1.0 - beta_one**adam_step
    fix_two = 1.0 - beta_two**adam_step

    def update(sub):
        offset, size = SUBS[sub]
        for part in range(2):
            inside = pl.ds(2 * offset + part * size, size)
            totals = []
            for chunk in range(CHUNKS):
                grad = wire_got[chunk, 0:16, inside].astype(F32)
                for source in range(1, ND):
                    grad = grad + wire_got[chunk, source * 16:(source + 1) * 16, inside].astype(F32)
                totals.append(adapter_scale_factor * grad)
            for eighth in range(8):
                piece = eighth * 2 + part
                cols = pl.ds(piece * PIECE + offset, size)
                grad = jnp.concatenate([total[eighth * CH:(eighth + 1) * CH] for total in totals], axis=0)
                one = beta_one * first[:, cols] + (1.0 - beta_one) * grad
                two = beta_two * second[:, cols] + (1.0 - beta_two) * grad * grad
                old = param[:, cols]
                new = old - learn_rate * (one / fix_one / (jnp.sqrt(two / fix_two) + adam_eps) + decay_rate * old)
                for kind, value in enumerate((new, one, two)):
                    moving[kind, piece * J:(piece + 1) * J, pl.ds(offset, size)] = value.astype(BF)

    move_sent = []

    def pack_moves(kind, cols):
        packed[kind, :, cols] = jnp.dot(leave, moving[kind, :, cols], preferred_element_type=F32).astype(BF)
        landed[kind, at(me * 16, 16), cols] = jnp.zeros((16, cols.size), BF)

    def move(kind, cols, index):
        for step in (8, 9, 10, 11, 7, 6, 5, 4, 12, 13, 14, 15, 3, 2, 1):
            to = homes[step - 1]
            copy = copy_to(
                packed.at[kind, at(to[1] * 16, 16), cols], landed.at[kind, at(me * 16, 16), cols],
                move_send.at[index * NE + step], move_recv.at[index * NE + me], to,
            )
            copy.start()
            move_sent.append(copy)

    def arrived(kind, cols, index):
        for step in range(1, NE):
            source = (me + step) % NE
            ref = landed.at[kind, at(source * 16, 16), cols]
            copy_to(ref, ref, move_send.at[0], move_recv.at[index * NE + source], homes[step - 1]).wait_recv()
        return (contract(enter, landed[kind, :, cols], 0, 0) + contract(stay, moving[kind, :, cols], 0, 0)).astype(BF)

    all_sent = []

    def group(dy, dz):
        return ((yl + dy) % 2) * 4 + (z + dz) % 4

    def part_of(dy, dz, sub, half):
        rows = at(group(dy, dz) * 128, 128) if half is None else at(group(dy, dz) * 128 + half * 64, 64)
        return whole.at[rows, pl.ds(*SUBS[sub])]

    def share_slot(dy, dz, sub, half):
        return all_recv.at[((sub * 2 + dy) * 4 + dz) * 2 + (half or 0)]

    def pass_on(dy, dz, sub, to_y, to_z, half=None):
        ref = part_of(dy, dz, sub, half)
        copy = copy_to(
            ref, ref, all_send.at[len(all_sent)], share_slot((dy + to_y) % 2, (dz - to_z) % 4, sub, half), (group(to_y, to_z), me)
        )
        copy.start()
        all_sent.append(copy)

    def came(dy, dz, sub, half=None):
        ref = part_of(dy, dz, sub, half)
        copy_to(ref, ref, all_send.at[0], share_slot(dy, dz, sub, half), groups[0]).wait_recv()

    for chunk in range(CHUNKS - 1):
        wait_grads(chunk, wire_cols(None), chunk)
    for sub in range(2):
        wait_grads(CHUNKS - 1, wire_cols(sub), CHUNKS - 1 + sub)
        update(sub)
        pack_moves(0, pl.ds(*SUBS[sub]))
        move(0, pl.ds(*SUBS[sub]), sub)
    full = pl.ds(0, PIECE)
    pack_moves(1, full)
    pack_moves(2, full)

    def begin(sub):
        cols = pl.ds(*SUBS[sub])
        whole[at(dp * 128, 128), cols] = arrived(0, cols, sub)
        pass_on(0, 0, sub, 1, 0)
        pass_on(0, 0, sub, 0, 1)
        pass_on(0, 0, sub, 0, 3)

    def across(sub):
        came(1, 0, sub)
        pass_on(1, 0, sub, 0, 1)
        pass_on(1, 0, sub, 0, 3)

    def around(dy, sub):
        came(dy, 3, sub)
        pass_on(dy, 3, sub, 0, 1, 0)
        came(dy, 1, sub)
        pass_on(dy, 1, sub, 0, 3, 1)

    begin(0)
    across(0)
    begin(1)
    around(0, 0)
    move(1, full, 2)
    across(1)
    around(1, 0)
    move(2, full, 3)
    around(0, 1)
    around(1, 1)
    first_out[...] = arrived(1, full, 2)
    second_out[...] = arrived(2, full, 3)
    for sub in range(2):
        for half in range(2):
            came(0, 2, sub, half)
            came(1, 2, sub, half)
    for copy in sent + small + cot_sent + grad_sent + move_sent + all_sent:
        copy.wait_send()


def finish_kernel(whole, first, second, out_a, out_b, out_first, out_second, new_a, new_b, new_first, new_second, sems):
    index = iota((RJ, RJ), 0)
    turn = ones(iota((RJ, RJ), 1) == index % R * J + index // R)

    def unit(number):
        share, inside = divmod(number * UNIT, SHARE)
        parts = []
        left = UNIT
        while left:
            piece, offset = divmod(inside, PIECE)
            size = min(left, PIECE - offset)
            line = share * 128 + piece * J
            pair = whole[line // 16 * 16:line // 16 * 16 + 16, offset:offset + size].astype(F32)
            parts.append(pair[line % 16:line % 16 + J])
            left -= size
            inside += size
        return parts[0] if len(parts) == 1 else jnp.concatenate(parts, axis=1)

    copies = []

    def write(src, dst):
        copy = pltpu.make_async_copy(src, dst, sems.at[len(copies)])
        copy.start()
        copies.append(copy)

    for kept, out, value in ((new_first, out_first, first), (new_second, out_second, second)):
        for pair in range(8):
            both = value[pair * 16:(pair + 1) * 16, :].astype(F32)
            kept[:, 2 * pair * PIECE:(2 * pair + 1) * PIECE] = both[:J]
            kept[:, (2 * pair + 1) * PIECE:(2 * pair + 2) * PIECE] = both[J:]
        write(kept, out)
    for kept, out, columns, base in ((new_a, out_a, A_UNITS, 0), (new_b, out_b, B_UNITS, A_UNITS * R)):
        for column in range(columns):
            cols = pl.ds(column * UNIT, UNIT)
            stack = jnp.concatenate([unit(base + r * columns + column) for r in range(R)], axis=0).astype(BF)
            kept[:, cols] = jnp.dot(turn, stack, preferred_element_type=F32)
            write(kept.at[:, cols], out.at[:, cols])
    for copy in copies:
        copy.wait()


def vmem(count):
    return [pl.BlockSpec(memory_space=pltpu.VMEM)] * count


def anywhere(count):
    return [pl.BlockSpec(memory_space=pl.ANY)] * count


def shards(tokens, up_grad, gate_weights, expert_ids, new_home, adapter_a, adapter_b, first_moment, second_moment):
    dma = pltpu.SemaphoreType.DMA
    whole, first, second = pl.pallas_call(
        main_kernel,
        out_shape=[
            jax.ShapeDtypeStruct((ND * 128, PIECE), BF),
            jax.ShapeDtypeStruct((128, PIECE), BF),
            jax.ShapeDtypeStruct((128, PIECE), BF),
        ],
        in_specs=anywhere(2) + vmem(3) + anywhere(4),
        out_specs=vmem(3),
        scratch_shapes=[
            pltpu.VMEM((NE * TOK, D), BF),
            pltpu.VMEM((COPIES, FF), BF),
            pltpu.VMEM((NE * ROWS, FF), BF),
            pltpu.VMEM((NE * ROWS, FF), BF),
            pltpu.VMEM((NE * TOP, TOK), I32),
            pltpu.VMEM((RJ, D), F32),
            pltpu.VMEM((RJ, FF), F32),
            pltpu.VMEM((RJ, D), BF),
            pltpu.VMEM((RJ, FF), BF),
            pltpu.VMEM((4 * ROWS, COPIES), BF),
            pltpu.VMEM((NE * ROWS, TOK), BF),
            pltpu.VMEM((4 * TOK, RJ), BF),
            pltpu.VMEM((RC, NE * TOK), BF),
            pltpu.VMEM((2 * BLOCK, D), BF),
            pltpu.VMEM((CHUNKS, 2 * BLOCK, RC), BF),
            pltpu.VMEM((2 * BLOCK, RC), BF),
            pltpu.VMEM((RC, D), F32),
            pltpu.VMEM((RC, FF), F32),
            pltpu.VMEM((1, COPIES), I32),
            pltpu.VMEM((CHUNKS, ND * 16, EIGHTH), BF),
            pltpu.VMEM((CHUNKS, ND * 16, EIGHTH), BF),
            pltpu.VMEM((J, SHARE), F32),
            pltpu.VMEM((J, SHARE), F32),
            pltpu.VMEM((8 * J, D), F32),
            pltpu.VMEM((16 * J, FF), F32),
            pltpu.VMEM((J, SHARE), F32),
            pltpu.VMEM((3, 128, PIECE), BF),
            pltpu.VMEM((3, 256, PIECE), BF),
            pltpu.VMEM((3, 256, PIECE), BF),
            dma((6,)),
            dma((NE,)),
            dma((NE,)),
            dma((NE * 5,)),
            dma((MESSAGES * NE,)),
            dma((64,)),
            dma((32,)),
            dma((16,)),
            dma(((CHUNKS + 1) * ND,)),
            dma(((CHUNKS + 1) * ND,)),
            dma((4 * NE,)),
            dma((4 * NE,)),
            dma((32,)),
            dma((32,)),
        ],
        compiler_params=pltpu.CompilerParams(collective_id=0, has_side_effects=True, vmem_limit_bytes=63 * 2**20),
        name="dispatch_update",
    )(
        tokens, up_grad.reshape(COPIES, FF), gate_weights.T, expert_ids.T, new_home.reshape(1, NE * J),
        adapter_a.reshape(RJ, D), adapter_b.reshape(RJ, FF), first_moment, second_moment,
    )
    new_a, new_b, new_first, new_second = pl.pallas_call(
        finish_kernel,
        out_shape=[
            jax.ShapeDtypeStruct((RJ, D), F32),
            jax.ShapeDtypeStruct((RJ, FF), F32),
            jax.ShapeDtypeStruct((J, SHARE), F32),
            jax.ShapeDtypeStruct((J, SHARE), F32),
        ],
        in_specs=vmem(3),
        out_specs=anywhere(4),
        scratch_shapes=[
            pltpu.VMEM((RJ, D), F32),
            pltpu.VMEM((RJ, FF), F32),
            pltpu.VMEM((J, SHARE), F32),
            pltpu.VMEM((J, SHARE), F32),
            dma((2 + A_UNITS + B_UNITS,)),
        ],
        compiler_params=pltpu.CompilerParams(vmem_limit_bytes=60 * 2**20),
        name="finish",
    )(whole, first, second)
    return new_a.reshape(J, R, D), new_b.reshape(J, R, FF), new_first, new_second


def solution(mesh):
    placed = (
        P(("dp", "expert"), None),
        P(("dp", "expert"), None, None),
        P(("dp", "expert"), None),
        P(("dp", "expert"), None),
        P(),
        P("expert", None, None),
        P("expert", None, None),
        P("expert", "dp"),
        P("expert", "dp"),
    )
    return jax.shard_map(
        shards,
        mesh=mesh,
        in_specs=placed,
        out_specs=(P("expert", None, None), P("expert", None, None), P("expert", "dp"), P("expert", "dp")),
        check_vma=False,
    )
```

```python
import jax
import jax.numpy as jnp
from jax import lax
from jax.experimental import pallas as pl
from jax.experimental.pallas import tpu as pltpu
from jax.sharding import PartitionSpec as P

beta_one = 0.9
beta_two = 0.999
learn_rate = 0.001
decay_rate = 0.01
adam_eps = 1e-08
adapter_scale_factor = 2.0
adam_step = 10.0

D = 4096
FF = 1536
TOP = 8
R = 32
J = 8
TOK = 128
COPIES = TOK * TOP
CAP = 10
NE = 16
ND = 8
ROWS = J * CAP
MSG = 16
MESSAGES = ROWS // MSG
BLOCK = NE * MSG
RJ = R * J
CH = 2
CHUNKS = J // CH
RC = R * CH
UNIT = 512
SHARE = 22528
PIECE = SHARE // 16
EIGHTH = SHARE // 8
UNITS = SHARE // UNIT
A_UNITS = D // UNIT
B_UNITS = FF // UNIT
SPLIT = 1792
SUBS = ((0, 768), (768, 640))

MESH = pl.DeviceIdType.MESH
BF = jnp.bfloat16
F32 = jnp.float32
I32 = jnp.int32


def iota(shape, dim):
    return lax.broadcasted_iota(I32, shape, dim)


def ones(mask):
    return mask.astype(F32).astype(BF)


def contract(lhs, rhs, i, k, precision=None):
    return lax.dot_general(lhs, rhs, (((i,), (k,)), ((), ())), preferred_element_type=F32, precision=precision)


def at(start, size, unit=None):
    return pl.ds(pl.multiple_of(start, unit or size), size)


def main_kernel(
    tok, up_hbm, gate_t, ids_t, homes_row, a_hbm, b_hbm, first_hbm, second_hbm, whole, first_out, second_out,
    gathered, cots, send, got, ids_all, a, b, a16, b16, pick, hot, low, weights, picked,
    lows, back, grad_a, grad_b, row, wire, wire_got,
    first, second, rows_a, rows_b, param, moving, packed, landed,
    local, ids_send, ids_recv, cot_send, cot_recv, tok_send, tok_recv, sib_recv,
    grad_send, grad_recv, move_send, move_recv, all_send, all_recv,
):
    dp = lax.axis_index("dp")
    me = lax.axis_index("expert")
    x = me // 4
    yh = (me // 2) % 2
    core = me % 2
    dp_across = (dp + 4) % 8
    yl = dp // 4
    z = dp % 4

    def place(dy, dx, dc):
        return ((x + dx) % 4) * 4 + ((yh + dy) % 2) * 2 + (core + dc) % 2

    def device(dy, dx, dc):
        return (dp_across if dy else dp, place(dy, dx, dc))

    def copy_to(src, dst, send_sem, recv_sem, to):
        return pltpu.make_async_remote_copy(
            src_ref=src, dst_ref=dst, send_sem=send_sem, recv_sem=recv_sem, device_id=to, device_id_type=MESH
        )

    peers = [
        (1, 0, 0), (0, 2, 0), (0, 1, 0), (0, 3, 0), (1, 2, 0), (1, 0, 1), (0, 2, 1), (1, 1, 0),
        (0, 3, 1), (1, 2, 1), (1, 3, 0), (0, 1, 1), (1, 1, 1), (1, 3, 1), (0, 0, 1),
    ]
    groups = [((dp + step) % ND, me) for step in range(1, ND)]
    homes = [(dp, (me + step) % NE) for step in range(1, NE)]

    loads = [
        pltpu.make_async_copy(src, dst, local.at[number])
        for number, (src, dst) in enumerate([
            (tok, gathered.at[at(me * TOK, TOK)]), (up_hbm, cots), (a_hbm, a), (b_hbm, b), (first_hbm, first), (second_hbm, second),
        ])
    ]
    for load in loads:
        load.start()
    barrier = pltpu.get_barrier_semaphore()
    met = groups + homes + [device(*peer) for peer in peers if peer[0]]
    for peer in met:
        pl.semaphore_signal(barrier, inc=1, device_id=peer, device_id_type=MESH)
    pl.semaphore_wait(barrier, len(met))
    loads[0].wait()

    sent = []

    def block(dy, dx, dc, half, part):
        rows = place(dy, dx, dc) * TOK
        size = TOK
        if part is not None:
            rows = rows + part * (TOK // 2)
            size = TOK // 2
        cols = pl.ds(SPLIT, D - SPLIT) if half else pl.ds(0, SPLIT)
        return gathered.at[at(rows, size), cols]

    def push(src, half, part, to, sem):
        ref = block(*src, half, part)
        copy = copy_to(ref, ref, tok_send.at[len(sent)], sem, device(*to))
        copy.start()
        sent.append(copy)

    def slot(half, dy, dx, part):
        return tok_recv.at[((half * 2 + dy) * 4 + dx) * 2 + part]

    def sib_slot(half, dy, dx):
        return sib_recv.at[(half * 2 + dy) * 4 + dx]

    def arrive(half, dy, dx, part=None):
        ref = block(dy, dx, 0, half, part)
        copy_to(ref, ref, tok_send.at[0], slot(half, dy, dx, part or 0), device(0, 1, 0)).wait_recv()

    def to_sibling(half, dy, dx):
        push((dy, dx, 0), half, None, (0, 0, 1), sib_slot(half, dy, dx))

    def to_across(half, dx):
        push((0, dx, 0), half, None, (1, 0, 0), slot(half, 1, dx, 0))

    def to_right(half, dy, dx, part=None):
        push((dy, dx, 0), half, part, (0, 1, 0), slot(half, dy, (dx + 3) % 4, part or 0))

    def to_left(half, dy, dx, part=None):
        push((dy, dx, 0), half, part, (0, 3, 0), slot(half, dy, (dx + 1) % 4, part or 0))

    to_across(1, 0)
    to_right(0, 0, 0)
    to_left(0, 0, 0)
    to_across(0, 0)
    to_right(1, 0, 0)
    to_left(1, 0, 0)
    to_sibling(0, 0, 0)
    to_sibling(1, 0, 0)

    small = []
    mine = at(me * TOP, TOP)
    ids_all[mine, :] = ids_t[...]
    for number, peer in enumerate(peers):
        copy = copy_to(ids_all.at[mine], ids_all.at[mine], ids_send.at[number], ids_recv.at[me], device(*peer))
        copy.start()
        small.append(copy)

    owner_of = iota((TOK, COPIES), 1) // TOP == iota((TOK, COPIES), 0)
    which = iota((TOP, COPIES), 1) % TOP == iota((TOP, COPIES), 0)
    spread = jnp.dot(ids_t[...].astype(F32).astype(BF), ones(owner_of), preferred_element_type=F32)
    ids_flat = jnp.sum(jnp.where(which, spread, 0.0), axis=0, keepdims=True).astype(I32)
    before = ones(iota((TOK, TOK), 0) < iota((TOK, TOK), 1))
    experts = iota((TOK, TOK), 0)
    total = jnp.zeros((TOK, 1), F32)
    for part in range(TOP):
        hit = ids_flat[:, part * TOK:(part + 1) * TOK] == experts
        value = hit.astype(F32)
        count = jnp.dot(value.astype(BF), before, preferred_element_type=F32) + total
        total = total + jnp.sum(value, axis=1, keepdims=True)
        row[:, part * TOK:(part + 1) * TOK] = jnp.sum(
            jnp.where(hit, count + (CAP * experts).astype(F32), 0.0), axis=0, keepdims=True
        ).astype(I32)

    loads[1].wait()

    @pl.loop(0, TOP)
    def _(part):
        rows = at(part * TOK, TOK)
        mine_of = (iota((TOK, TOK), 0) + part * TOK) // TOP == iota((TOK, TOK), 1)
        scale = contract(mine_of.astype(F32), gate_t[...], 1, 1, lax.Precision.HIGHEST)
        scale = jnp.sum(jnp.where(iota((TOK, TOP), 0) % TOP == iota((TOK, TOP), 1), scale, 0.0), axis=1, keepdims=True)
        cots[rows, :] = (scale * cots[rows, :].astype(F32)).astype(BF)

    for dx in (2, 1, 3, 0):
        base = ((x + dx) % 4) * (4 * ROWS)
        pick[...] = ones(iota((4 * ROWS, COPIES), 0) + base == row[...])

        @pl.loop(0, FF // UNIT)
        def _(part):
            cols = at(part * UNIT, UNIT)
            send[at(base, 4 * ROWS), cols] = jnp.dot(pick[...], cots[:, cols], preferred_element_type=F32).astype(BF)

    cot_sent = []

    def send_cots(message):
        for peer in peers:
            copy = copy_to(
                send.at[at(place(*peer) * ROWS + message * MSG, MSG)], got.at[at(message * BLOCK + me * MSG, MSG)],
                cot_send.at[len(cot_sent)], cot_recv.at[message * NE + me], device(*peer),
            )
            copy.start()
            cot_sent.append(copy)
        got[at(message * BLOCK + me * MSG, MSG), :] = send[at(me * ROWS + message * MSG, MSG), :]

    def wait_cots(message):
        for peer in peers:
            ref = got.at[at(message * BLOCK + place(*peer) * MSG, MSG)]
            copy_to(ref, ref, cot_send.at[0], cot_recv.at[message * NE + place(*peer)], device(*peer)).wait_recv()

    arrive(1, 1, 0)
    to_right(1, 1, 0)
    to_left(1, 1, 0)
    to_sibling(1, 1, 0)
    arrive(0, 0, 3)
    to_right(0, 0, 3, 0)
    to_across(0, 3)
    to_sibling(0, 0, 3)
    arrive(0, 0, 1)
    to_left(0, 0, 1, 1)
    to_across(0, 1)
    to_sibling(0, 0, 1)
    send_cots(0)

    index = iota((RJ, RJ), 0)
    turn = ones(iota((RJ, RJ), 1) == (index // RC * CH + index % CH) * R + (index % RC) // CH)
    loads[2].wait()
    loads[3].wait()

    @pl.loop(0, A_UNITS)
    def _(part):
        cols = at(part * UNIT, UNIT)
        a16[:, cols] = jnp.dot(turn, a[:, cols].astype(BF), preferred_element_type=F32).astype(BF)

    @pl.loop(0, B_UNITS)
    def _(part):
        cols = at(part * UNIT, UNIT)
        b16[:, cols] = jnp.dot(turn, b[:, cols].astype(BF), preferred_element_type=F32).astype(BF)

    arrive(0, 1, 0)
    to_sibling(0, 1, 0)
    arrive(1, 0, 3)
    to_right(1, 0, 3, 0)
    to_sibling(1, 0, 3)
    arrive(1, 0, 1)
    to_left(1, 0, 1, 1)
    to_sibling(1, 0, 1)

    def own(size, first_row, chunk):
        line = iota((size, RC), 0) + first_row
        return line // CAP == chunk * CH + iota((size, RC), 1) % CH

    def from_sibling(dx):
        for half in range(2):
            for dy in range(2):
                ref = block(dy, dx, 1, half, None)
                copy_to(ref, ref, tok_send.at[0], sib_slot(half, dy, dx), device(0, 0, 1)).wait_recv()

    def hidden(dx):
        from_sibling(dx)
        base = (x + dx) % 4
        rows = at(base * 4 * TOK, 4 * TOK)
        low[...] = contract(gathered[rows, :], a16[...], 1, 1).astype(BF)
        for inside in range(4):
            source = base * 4 + inside
            value = jnp.dot(
                hot[at(source * ROWS, ROWS, MSG), :], low[inside * TOK:(inside + 1) * TOK, :], preferred_element_type=F32
            )
            for chunk in range(CHUNKS):
                first_row = chunk * MSG
                part = jnp.where(
                    own(2 * MSG, first_row, chunk),
                    value[first_row:first_row + 2 * MSG, chunk * RC:(chunk + 1) * RC], 0.0,
                ).astype(BF)
                lows[chunk, at(source * MSG, MSG), :] = part[:MSG]
                lows[chunk, at(BLOCK + source * MSG, MSG), :] = part[MSG:]

    arrive(0, 0, 2, 0)
    arrive(0, 0, 2, 1)
    to_across(0, 2)
    to_sibling(0, 0, 2)
    arrive(1, 1, 3)
    to_right(1, 1, 3, 0)
    to_sibling(1, 1, 3)
    arrive(1, 1, 1)
    to_left(1, 1, 1, 1)
    to_sibling(1, 1, 1)

    for peer in peers:
        ref = ids_all.at[at(place(*peer) * TOP, TOP)]
        copy_to(ref, ref, ids_send.at[0], ids_recv.at[place(*peer)], device(*peer)).wait_recv()
    repeat = ones(iota((ROWS, J), 0) // CAP == iota((ROWS, J), 1))
    turn_in = (iota((ROWS, TOK), 0) % CAP).astype(F32)

    @pl.loop(0, NE, unroll=4)
    def _(source):
        ids = ids_all[at(source * TOP, TOP), :]
        hit = jnp.zeros((J, TOK), F32)
        for k in range(TOP):
            hit = hit + jnp.where(ids[k:k + 1, :] == iota((J, TOK), 0) + me * J, 1.0, 0.0)
        count = jnp.dot(hit.astype(BF), before, preferred_element_type=F32)
        value = jnp.where(hit > 0.5, count, -1.0)
        found = ones(jnp.dot(repeat, value.astype(BF), preferred_element_type=F32) == turn_in)
        hot[at(source * ROWS, ROWS, MSG), :] = found

    exact = lax.Precision.HIGHEST
    start = UNITS * dp
    a_first = jnp.minimum(start // A_UNITS, R - 8)
    b_first = jnp.clip((start - A_UNITS * R) // B_UNITS, 0, R - 16)

    def chooser(count, base):
        index = iota((count * J, RJ), 0)
        return (iota((count * J, RJ), 1) == (index % J) * R + index // J + base).astype(F32)

    @pl.loop(0, A_UNITS)
    def _(part):
        cols = at(part * UNIT, UNIT)
        rows_a[:, cols] = jnp.dot(chooser(8, a_first), a[:, cols], preferred_element_type=F32, precision=exact)

    @pl.loop(0, B_UNITS)
    def _(part):
        cols = at(part * UNIT, UNIT)
        rows_b[:, cols] = jnp.dot(chooser(16, b_first), b[:, cols], preferred_element_type=F32, precision=exact)

    @pl.loop(0, UNITS)
    def _(column):
        number = start + column
        in_a = jnp.clip(number // A_UNITS - a_first, 0, 7)
        number_b = jnp.maximum(number - A_UNITS * R, 0)
        in_b = jnp.clip(number_b // B_UNITS - b_first, 0, 15)
        value_a = rows_a[at(in_a * J, J), at(number % A_UNITS * UNIT, UNIT)]
        value_b = rows_b[at(in_b * J, J), at(number_b % B_UNITS * UNIT, UNIT)]
        param[:, at(column * UNIT, UNIT)] = jnp.where(number < A_UNITS * R, value_a, value_b)

    homes_now = homes_row[...].astype(F32).astype(BF)
    lane = iota((128, 128), 1)
    line = iota((128, 128), 0)
    dest = jnp.dot(homes_now, ones(line == me * J + lane % J), preferred_element_type=F32).astype(I32)
    named = ones(homes_row[...] == me * J + line % J)
    owner = contract(ones(iota((1, 128), 1) >= 0) * iota((1, 128), 1).astype(F32).astype(BF), named, 1, 1).astype(I32)
    stay = ones((line // J == lane // J) & (line % J == owner % J) & (owner // J == me))
    lane = iota((256, 128), 1)
    line = iota((256, 128), 0)
    same = (line % 16 == lane // J) & (line // 16 != me)
    leave = ones(same & (line // 16 == dest // J))
    enter = ones(same & (line // 16 == owner // J))

    hidden(0)
    arrive(0, 1, 3)
    to_sibling(0, 1, 3)
    arrive(0, 1, 1)
    to_sibling(0, 1, 1)
    send_cots(1)
    arrive(1, 0, 2, 0)
    arrive(1, 0, 2, 1)
    to_sibling(1, 0, 2)
    hidden(3)
    hidden(1)
    arrive(1, 1, 2, 0)
    arrive(1, 1, 2, 1)
    to_sibling(1, 1, 2)
    arrive(0, 1, 2)
    to_sibling(0, 1, 2)
    send_cots(2)
    hidden(2)

    def grad_flat(number, size):
        parts = []
        while size:
            if number < R * D:
                ref, (r, column), width = grad_a, divmod(number, D), D
            else:
                ref, (r, column), width = grad_b, divmod(number - R * D, FF), FF
            step = min(size, width - column)
            parts.append(ref[r * CH:(r + 1) * CH, column:column + step])
            number += step
            size -= step
        return parts[0] if len(parts) == 1 else jnp.concatenate(parts, axis=1)

    grad_sent = []

    def send_grads(chunk, cols, index):
        for step in (4, 1, 7, 3, 5, 2, 6):
            to = groups[step - 1]
            copy = copy_to(
                wire.at[chunk, at(to[0] * 16, 16), cols], wire_got.at[chunk, at(dp * 16, 16), cols],
                grad_send.at[index * ND + step], grad_recv.at[index * ND + dp], to,
            )
            copy.start()
            grad_sent.append(copy)
        wire_got[chunk, at(dp * 16, 16), cols] = wire[chunk, at(dp * 16, 16), cols]

    def wait_grads(chunk, cols, index):
        for step in range(1, ND):
            source = (dp + step) % ND
            ref = wire_got.at[chunk, at(source * 16, 16), cols]
            copy_to(ref, ref, grad_send.at[0], grad_recv.at[index * ND + source], groups[step - 1]).wait_recv()

    def wire_cols(sub):
        return pl.ds(0, EIGHTH) if sub is None else pl.ds(2 * SUBS[sub][0], 2 * SUBS[sub][1])

    def gradients(chunk):
        used = pl.ds(chunk * BLOCK, 2 * BLOCK)
        mask = [
            jnp.concatenate([own(MSG, (chunk + message) * MSG, chunk)] * 4, axis=0) for message in range(2)
        ]
        for message in range(2):
            if message:
                wait_cots(chunk + 1)
            for part in range(4):
                rows = pl.ds((chunk + message) * BLOCK + part * 4 * MSG, 4 * MSG)
                value = contract(got[rows, :], b16[chunk * RC:(chunk + 1) * RC, :], 1, 1)
                value = jnp.where(mask[message], value, 0.0).astype(BF)
                for inside in range(4):
                    row0 = (part * 4 + inside) * 2 * MSG + message * MSG
                    back[row0:row0 + MSG, :] = value[inside * MSG:(inside + 1) * MSG, :]

        last = chunk == CHUNKS - 1
        if last:
            @pl.loop(0, D // 1024)
            def _(part):
                cols = at(part * 1024, 1024)
                grad_a[:, cols] = contract(back[...], picked[:, cols], 0, 0)
        else:
            @pl.loop(0, NE, unroll=8)
            def _(source):
                value = contract(
                    back[at(source * 2 * MSG, 2 * MSG), :], hot[at(source * ROWS + chunk * MSG, 2 * MSG, MSG), :], 0, 0
                )
                weights[:, at(source * TOK, TOK)] = value.astype(BF)

            @pl.loop(0, D // 1024)
            def _(part):
                cols = at(part * 1024, 1024)
                grad_a[:, cols] = jnp.dot(weights[...], gathered[:, cols], preferred_element_type=F32)

        @pl.loop(0, B_UNITS)
        def _(part):
            cols = at(part * UNIT, UNIT)
            grad_b[:, cols] = contract(lows[chunk], got[used, cols], 0, 0)

        for sub, (offset, size) in enumerate(SUBS):
            for share in range(ND):
                for part in range(2):
                    base = share * SHARE + part * PIECE + offset
                    value = jnp.concatenate([grad_flat(base + eighth * EIGHTH, size) for eighth in range(8)], axis=0)
                    col = 2 * offset + part * size
                    wire[chunk, share * 16:(share + 1) * 16, col:col + size] = value.astype(BF)
            if last:
                send_grads(chunk, wire_cols(sub), chunk + sub)
        if not last:
            send_grads(chunk, wire_cols(None), chunk)

    wait_cots(0)
    send_cots(3)

    @pl.loop(0, NE)
    def _(source):
        rows = at(source * TOK, TOK)
        mark = hot[at(source * ROWS + (CHUNKS - 1) * MSG, 2 * MSG, MSG), :]
        for part in range(D // 1024):
            cols = pl.ds(part * 1024, 1024)
            picked[at(source * 2 * MSG, 2 * MSG), cols] = jnp.dot(mark, gathered[rows, cols], preferred_element_type=F32).astype(BF)


    gradients(0)
    send_cots(4)
    gradients(1)
    gradients(2)
    gradients(3)

    loads[4].wait()
    loads[5].wait()
    fix_one = 1.0 - beta_one**adam_step
    fix_two = 1.0 - beta_two**adam_step

    def update(sub):
        offset, size = SUBS[sub]
        for part in range(2):
            inside = pl.ds(2 * offset + part * size, size)
            totals = []
            for chunk in range(CHUNKS):
                grad = wire_got[chunk, 0:16, inside].astype(F32)
                for source in range(1, ND):
                    grad = grad + wire_got[chunk, source * 16:(source + 1) * 16, inside].astype(F32)
                totals.append(adapter_scale_factor * grad)
            for eighth in range(8):
                piece = eighth * 2 + part
                cols = pl.ds(piece * PIECE + offset, size)
                grad = jnp.concatenate([total[eighth * CH:(eighth + 1) * CH] for total in totals], axis=0)
                one = beta_one * first[:, cols] + (1.0 - beta_one) * grad
                two = beta_two * second[:, cols] + (1.0 - beta_two) * grad * grad
                old = param[:, cols]
                new = old - learn_rate * (one / fix_one / (jnp.sqrt(two / fix_two) + adam_eps) + decay_rate * old)
                for kind, value in enumerate((new, one, two)):
                    moving[kind, piece * J:(piece + 1) * J, pl.ds(offset, size)] = value.astype(BF)

    move_sent = []

    def pack_moves(kind, cols):
        packed[kind, :, cols] = jnp.dot(leave, moving[kind, :, cols], preferred_element_type=F32).astype(BF)
        landed[kind, at(me * 16, 16), cols] = jnp.zeros((16, cols.size), BF)

    def move(kind, cols, index):
        for step in (8, 9, 10, 11, 7, 6, 5, 4, 12, 13, 14, 15, 3, 2, 1):
            to = homes[step - 1]
            copy = copy_to(
                packed.at[kind, at(to[1] * 16, 16), cols], landed.at[kind, at(me * 16, 16), cols],
                move_send.at[index * NE + step], move_recv.at[index * NE + me], to,
            )
            copy.start()
            move_sent.append(copy)

    def arrived(kind, cols, index):
        for step in range(1, NE):
            source = (me + step) % NE
            ref = landed.at[kind, at(source * 16, 16), cols]
            copy_to(ref, ref, move_send.at[0], move_recv.at[index * NE + source], homes[step - 1]).wait_recv()
        return (contract(enter, landed[kind, :, cols], 0, 0) + contract(stay, moving[kind, :, cols], 0, 0)).astype(BF)

    all_sent = []

    def group(dy, dz):
        return ((yl + dy) % 2) * 4 + (z + dz) % 4

    def part_of(dy, dz, sub, half):
        rows = at(group(dy, dz) * 128, 128) if half is None else at(group(dy, dz) * 128 + half * 64, 64)
        return whole.at[rows, pl.ds(*SUBS[sub])]

    def share_slot(dy, dz, sub, half):
        return all_recv.at[((sub * 2 + dy) * 4 + dz) * 2 + (half or 0)]

    def pass_on(dy, dz, sub, to_y, to_z, half=None):
        ref = part_of(dy, dz, sub, half)
        copy = copy_to(
            ref, ref, all_send.at[len(all_sent)], share_slot((dy + to_y) % 2, (dz - to_z) % 4, sub, half), (group(to_y, to_z), me)
        )
        copy.start()
        all_sent.append(copy)

    def came(dy, dz, sub, half=None):
        ref = part_of(dy, dz, sub, half)
        copy_to(ref, ref, all_send.at[0], share_slot(dy, dz, sub, half), groups[0]).wait_recv()

    for chunk in range(CHUNKS - 1):
        wait_grads(chunk, wire_cols(None), chunk)
    for sub in range(2):
        wait_grads(CHUNKS - 1, wire_cols(sub), CHUNKS - 1 + sub)
        update(sub)
        pack_moves(0, pl.ds(*SUBS[sub]))
        move(0, pl.ds(*SUBS[sub]), sub)
    full = pl.ds(0, PIECE)
    pack_moves(1, full)
    pack_moves(2, full)

    def begin(sub):
        cols = pl.ds(*SUBS[sub])
        whole[at(dp * 128, 128), cols] = arrived(0, cols, sub)
        pass_on(0, 0, sub, 1, 0)
        pass_on(0, 0, sub, 0, 1)
        pass_on(0, 0, sub, 0, 3)

    def across(sub):
        came(1, 0, sub)
        pass_on(1, 0, sub, 0, 1)
        pass_on(1, 0, sub, 0, 3)

    def around(dy, sub):
        came(dy, 3, sub)
        pass_on(dy, 3, sub, 0, 1, 0)
        came(dy, 1, sub)
        pass_on(dy, 1, sub, 0, 3, 1)

    begin(0)
    across(0)
    begin(1)
    around(0, 0)
    across(1)
    move(1, full, 2)
    around(1, 0)
    around(0, 1)
    move(2, full, 3)
    around(1, 1)
    first_out[...] = arrived(1, full, 2)
    second_out[...] = arrived(2, full, 3)
    for sub in range(2):
        for half in range(2):
            came(0, 2, sub, half)
            came(1, 2, sub, half)
    for copy in sent + small + cot_sent + grad_sent + move_sent + all_sent:
        copy.wait_send()


def finish_kernel(whole, first, second, out_a, out_b, out_first, out_second, new_a, new_b, new_first, new_second, sems):
    index = iota((RJ, RJ), 0)
    turn = ones(iota((RJ, RJ), 1) == index % R * J + index // R)

    def unit(number):
        share, inside = divmod(number * UNIT, SHARE)
        parts = []
        left = UNIT
        while left:
            piece, offset = divmod(inside, PIECE)
            size = min(left, PIECE - offset)
            line = share * 128 + piece * J
            pair = whole[line // 16 * 16:line // 16 * 16 + 16, offset:offset + size].astype(F32)
            parts.append(pair[line % 16:line % 16 + J])
            left -= size
            inside += size
        return parts[0] if len(parts) == 1 else jnp.concatenate(parts, axis=1)

    copies = []

    def write(src, dst):
        copy = pltpu.make_async_copy(src, dst, sems.at[len(copies)])
        copy.start()
        copies.append(copy)

    for kept, out, value in ((new_first, out_first, first), (new_second, out_second, second)):
        for pair in range(8):
            both = value[pair * 16:(pair + 1) * 16, :].astype(F32)
            kept[:, 2 * pair * PIECE:(2 * pair + 1) * PIECE] = both[:J]
            kept[:, (2 * pair + 1) * PIECE:(2 * pair + 2) * PIECE] = both[J:]
        write(kept, out)
    for kept, out, columns, base in ((new_a, out_a, A_UNITS, 0), (new_b, out_b, B_UNITS, A_UNITS * R)):
        for column in range(columns):
            cols = pl.ds(column * UNIT, UNIT)
            stack = jnp.concatenate([unit(base + r * columns + column) for r in range(R)], axis=0).astype(BF)
            kept[:, cols] = jnp.dot(turn, stack, preferred_element_type=F32)
            write(kept.at[:, cols], out.at[:, cols])
    for copy in copies:
        copy.wait()


def vmem(count):
    return [pl.BlockSpec(memory_space=pltpu.VMEM)] * count


def anywhere(count):
    return [pl.BlockSpec(memory_space=pl.ANY)] * count


def shards(tokens, up_grad, gate_weights, expert_ids, new_home, adapter_a, adapter_b, first_moment, second_moment):
    dma = pltpu.SemaphoreType.DMA
    whole, first, second = pl.pallas_call(
        main_kernel,
        out_shape=[
            jax.ShapeDtypeStruct((ND * 128, PIECE), BF),
            jax.ShapeDtypeStruct((128, PIECE), BF),
            jax.ShapeDtypeStruct((128, PIECE), BF),
        ],
        in_specs=anywhere(2) + vmem(3) + anywhere(4),
        out_specs=vmem(3),
        scratch_shapes=[
            pltpu.VMEM((NE * TOK, D), BF),
            pltpu.VMEM((COPIES, FF), BF),
            pltpu.VMEM((NE * ROWS, FF), BF),
            pltpu.VMEM((NE * ROWS, FF), BF),
            pltpu.VMEM((NE * TOP, TOK), I32),
            pltpu.VMEM((RJ, D), F32),
            pltpu.VMEM((RJ, FF), F32),
            pltpu.VMEM((RJ, D), BF),
            pltpu.VMEM((RJ, FF), BF),
            pltpu.VMEM((4 * ROWS, COPIES), BF),
            pltpu.VMEM((NE * ROWS, TOK), BF),
            pltpu.VMEM((4 * TOK, RJ), BF),
            pltpu.VMEM((RC, NE * TOK), BF),
            pltpu.VMEM((2 * BLOCK, D), BF),
            pltpu.VMEM((CHUNKS, 2 * BLOCK, RC), BF),
            pltpu.VMEM((2 * BLOCK, RC), BF),
            pltpu.VMEM((RC, D), F32),
            pltpu.VMEM((RC, FF), F32),
            pltpu.VMEM((1, COPIES), I32),
            pltpu.VMEM((CHUNKS, ND * 16, EIGHTH), BF),
            pltpu.VMEM((CHUNKS, ND * 16, EIGHTH), BF),
            pltpu.VMEM((J, SHARE), F32),
            pltpu.VMEM((J, SHARE), F32),
            pltpu.VMEM((8 * J, D), F32),
            pltpu.VMEM((16 * J, FF), F32),
            pltpu.VMEM((J, SHARE), F32),
            pltpu.VMEM((3, 128, PIECE), BF),
            pltpu.VMEM((3, 256, PIECE), BF),
            pltpu.VMEM((3, 256, PIECE), BF),
            dma((6,)),
            dma((NE,)),
            dma((NE,)),
            dma((NE * 5,)),
            dma((MESSAGES * NE,)),
            dma((64,)),
            dma((32,)),
            dma((16,)),
            dma(((CHUNKS + 1) * ND,)),
            dma(((CHUNKS + 1) * ND,)),
            dma((4 * NE,)),
            dma((4 * NE,)),
            dma((32,)),
            dma((32,)),
        ],
        compiler_params=pltpu.CompilerParams(collective_id=0, has_side_effects=True, vmem_limit_bytes=63 * 2**20),
        name="dispatch_update",
    )(
        tokens, up_grad.reshape(COPIES, FF), gate_weights.T, expert_ids.T, new_home.reshape(1, NE * J),
        adapter_a.reshape(RJ, D), adapter_b.reshape(RJ, FF), first_moment, second_moment,
    )
    new_a, new_b, new_first, new_second = pl.pallas_call(
        finish_kernel,
        out_shape=[
            jax.ShapeDtypeStruct((RJ, D), F32),
            jax.ShapeDtypeStruct((RJ, FF), F32),
            jax.ShapeDtypeStruct((J, SHARE), F32),
            jax.ShapeDtypeStruct((J, SHARE), F32),
        ],
        in_specs=vmem(3),
        out_specs=anywhere(4),
        scratch_shapes=[
            pltpu.VMEM((RJ, D), F32),
            pltpu.VMEM((RJ, FF), F32),
            pltpu.VMEM((J, SHARE), F32),
            pltpu.VMEM((J, SHARE), F32),
            dma((2 + A_UNITS + B_UNITS,)),
        ],
        compiler_params=pltpu.CompilerParams(vmem_limit_bytes=60 * 2**20),
        name="finish",
    )(whole, first, second)
    return new_a.reshape(J, R, D), new_b.reshape(J, R, FF), new_first, new_second


def solution(mesh):
    placed = (
        P(("dp", "expert"), None),
        P(("dp", "expert"), None, None),
        P(("dp", "expert"), None),
        P(("dp", "expert"), None),
        P(),
        P("expert", None, None),
        P("expert", None, None),
        P("expert", "dp"),
        P("expert", "dp"),
    )
    return jax.shard_map(
        shards,
        mesh=mesh,
        in_specs=placed,
        out_specs=(P("expert", None, None), P("expert", None, None), P("expert", "dp"), P("expert", "dp")),
        check_vma=False,
    )
```
